32 devices in a mesh: pipe: 4 (over y, core), dp: 4 (over z), tensor: 2 (over x).
Axes of the slice: x: 2, y: 2, z: 4, core: 2. Of those that a mesh axis runs over, the one named last changes fastest.
Arguments:
- activations: bfloat16 [4, 2, 512, 16384], P('pipe', None, 'dp', 'tensor'), may hold values from -6 to 6
- cotangent: bfloat16 [4, 2, 512, 1024], P('pipe', None, 'dp', 'tensor'), may hold values from -0.5 to 0.5
- error_tiles: bfloat16 [4, 4, 2, 2, 1, 128, 128], P('pipe', 'dp', 'tensor'), may hold values from -4 to 4
- tile_picks: int32 [4, 4, 2, 2, 1, 2], P('pipe', None, 'tensor'), may hold values from 0 to 63, as said below
- row_owners: int32 [4, 2, 64], P('pipe', 'tensor'), may hold values from 0 to 63, as said below
Outputs:
- grad_strips: bfloat16 [4, 2, 8192, 1024], P('pipe', 'tensor', 'dp')
The draws below stay inside these ranges and needn't reach their ends.
Inputs may be any that keep to these rules, and one draw needn't show every extreme that they name: `tile_picks`: for each section, replica and row group, the 2 picked row blocks j have distinct owners row_owners[p, u, j] // 16; c is below 4. Each row_owners[p, u] is a permutation of 0 to 63.
All inputs are finite; a program needn't handle non-finite values.
Results may differ from the reference program's by a relative error of at most 0.001.
Values may be sent and summed in bfloat16 or wider, within the bound.
No kernel may reach another device: no remote copies, remote signals or barrier semaphores. Data moves between devices by JAX's collectives and lax.ppermute only.
A program may use at most 64 MiB of HBM per device.

```python
import jax
import jax.numpy as jnp
from jax import lax

D = 16384
KV = 1024
TILE = 128
MICRO = 2
TOK_DEV = 128
TOKENS = 512
SLOTS = 1
ROWB = 64
CBLK = 4
N_PIPE = 4
N_DP = 4
N_TENSOR = 2


def owner_table(key):
    row_count = D // (TILE * N_TENSOR)
    keys = jax.random.split(jax.random.fold_in(key, 11), N_PIPE * N_TENSOR)
    perms = jax.vmap(lambda single: jax.random.permutation(single, row_count))(keys)
    return perms.reshape(N_PIPE, N_TENSOR, row_count).astype(jnp.int32)


def draw_row_owners(key, part):
    return owner_table(key)


def draw_tile_picks(key, part):
    row_count = D // (TILE * N_TENSOR)
    owned = row_count // N_DP
    col_count = KV // (TILE * N_TENSOR)
    slot_count = max(1, N_DP // (2 * N_TENSOR))
    table = owner_table(key)
    inverse = jnp.argsort(table, axis=-1).astype(jnp.int32)
    keys = jax.random.split(jax.random.fold_in(key, 23), N_PIPE * N_DP * N_TENSOR)
    perms = jax.vmap(lambda single: jax.random.permutation(single, N_DP))(keys)
    perms = perms.reshape(N_PIPE, N_DP, N_TENSOR, N_DP)[..., :N_TENSOR * slot_count].astype(jnp.int32)
    within = jax.random.randint(jax.random.fold_in(key, 31), perms.shape, 0, owned).astype(jnp.int32)
    target = perms * owned + within
    spread = jnp.broadcast_to(inverse[:, None, :, :], (N_PIPE, N_DP, N_TENSOR, row_count))
    rows = jnp.take_along_axis(spread, target, axis=-1)
    shape = (N_PIPE, N_DP, N_TENSOR, N_TENSOR, slot_count)
    rows = rows.reshape(shape)
    cols = jax.random.randint(jax.random.fold_in(key, 47), shape, 0, col_count).astype(jnp.int32)
    return jnp.stack([rows, cols], axis=-1).astype(jnp.int32)


def level_of(stream_key, shape, cuts, least, largest):
    gain = 1.0
    for axis_at, parts in cuts:
        steps = jax.random.uniform(jax.random.fold_in(jax.random.fold_in(stream_key, 6), axis_at), (parts,), jnp.float32, least / len(cuts), largest / len(cuts))
        gain = gain * jnp.repeat(jnp.exp(steps), shape[axis_at] // parts).reshape((-1,) + (1,) * (len(shape) - 1 - axis_at))
    return gain


def noise(rng, extent, deviation, reach, cuts=(), held_as=jnp.bfloat16):
    array = deviation * jax.random.normal(rng, extent, jnp.float32)
    if cuts:
        array = array * level_of(rng, extent, cuts, -0.22, 0.18)
    return jnp.clip(array, -reach, reach).astype(held_as)


def setup_inputs(seed: int = 0) -> dict:
    key_of = jax.random.split(jax.random.key(seed), 6)
    activations = noise(key_of[0], (N_PIPE, MICRO, TOKENS, D), 1.0, 6.0, ((0, 4), (2, 4), (3, 2)))
    cotangent = noise(key_of[1], (N_PIPE, MICRO, TOKENS, KV), 0.0625, 0.5, ((0, 4), (2, 4), (3, 2)))
    error_tiles = noise(key_of[2], (N_PIPE, N_DP, N_TENSOR, N_TENSOR, SLOTS, TILE, TILE), 0.5, 4.0, ((0, 4), (1, 4), (2, 2)))
    tile_picks = draw_tile_picks(jax.random.fold_in(key_of[5], 71), 0)
    row_owners = draw_row_owners(jax.random.fold_in(key_of[5], 71), 0)
    return {"activations": activations, "cotangent": cotangent, "error_tiles": error_tiles, "tile_picks": tile_picks, "row_owners": row_owners}


def reference(activations, cotangent, error_tiles, tile_picks, row_owners):
    col_blocks = KV // TILE
    returned = jnp.roll(cotangent, -1, axis=0)
    dest_offset = (jnp.arange(N_TENSOR, dtype=jnp.int32) * ROWB)[:, None, None]
    source_offset = (jnp.arange(N_TENSOR, dtype=jnp.int32) * CBLK)[None, :, None]

    def one_section(section_index):
        section_acts = activations[section_index]
        section_grad = returned[section_index]

        def one_replica(running, replica):
            first_row = (replica * TOK_DEV).astype(jnp.int32)
            inputs = lax.dynamic_slice_in_dim(section_acts, first_row, TOK_DEV, 1).reshape(MICRO * TOK_DEV, D // TILE, TILE)
            outputs = lax.dynamic_slice_in_dim(section_grad, first_row, TOK_DEV, 1).reshape(MICRO * TOK_DEV, col_blocks, TILE)
            chosen = tile_picks[section_index, replica]
            row_index = (chosen[..., 0] + dest_offset).reshape(-1).astype(jnp.int32)
            col_index = (chosen[..., 1] + source_offset).reshape(-1).astype(jnp.int32)
            picked_in = jnp.take(inputs, row_index, axis=1).astype(jnp.float32)
            picked_out = jnp.take(outputs, col_index, axis=1).astype(jnp.float32)
            tile_sums = jnp.einsum('tmi,tmk->mik', picked_in, picked_out)
            carried = jnp.transpose(error_tiles[section_index, replica], (1, 0, 2, 3, 4)).reshape(-1, TILE, TILE).astype(jnp.float32)
            running = running.at[row_index, col_index].add(tile_sums + carried)
            return running, None

        dense_grad = jnp.zeros((D // TILE, col_blocks, TILE, TILE), jnp.float32)
        dense_grad, unused = lax.scan(one_replica, dense_grad, jnp.arange(N_DP, dtype=jnp.int32))
        dense_grad = dense_grad.reshape(N_TENSOR, ROWB, col_blocks, TILE, TILE)

        def reorder(stacked, ordering):
            return jnp.zeros_like(stacked).at[ordering].set(stacked)

        ordered = jax.vmap(reorder)(dense_grad, row_owners[section_index])
        return jnp.transpose(ordered, (0, 1, 3, 2, 4)).reshape(N_TENSOR, D // N_TENSOR, KV)

    result = lax.map(one_section, jnp.arange(N_PIPE, dtype=jnp.int32))
    return result.astype(jnp.bfloat16)
```

```python
import functools

import jax
import jax.numpy as jnp
from jax import lax
from jax.experimental import pallas as pl
from jax.experimental.pallas import tpu as pltpu
from jax.sharding import PartitionSpec as P

VMEM = pl.BlockSpec(memory_space=pltpu.VMEM)
SMEM = pl.BlockSpec(memory_space=pltpu.SMEM)
ANY = pl.BlockSpec(memory_space=pl.ANY)
MOST_SHIFTS = 8


def column(index, edge):
    return pl.ds(pl.multiple_of(index * edge, edge), edge)


def prepare(picks, activations, picked, strip, zeros, copied, cleared):
    replica = lax.axis_index("dp")
    groups, slots, edge = picks.shape[3], picks.shape[4], picked.shape[-1]
    reads = []
    for group in range(groups):
        for slot in range(slots):
            at = group * slots + slot
            block = picks[0, replica, 0, group, slot, 0]
            reads.append(
                pltpu.make_async_copy(
                    activations.at[0, :, :, column(block, edge)], picked.at[at], copied.at[at]
                )
            )
    for read in reads:
        read.start()
    zeros[...] = jnp.zeros_like(zeros)
    rows = zeros.shape[0]
    writes = [
        pltpu.make_async_copy(zeros, strip.at[0, 0, pl.ds(part * rows, rows)], cleared.at[part])
        for part in range(strip.shape[2] // rows)
    ]
    for write in writes:
        write.start()
    for read in reads:
        read.wait()
    for write in writes:
        write.wait()


def multiply(groups, picks, owners, picked, error, *refs):
    returned, arrived, outs = refs[:groups], refs[groups : 2 * groups - 1], refs[2 * groups - 1 :]
    replica, mine = lax.axis_index("dp"), lax.axis_index("tensor")
    replicas = picks.shape[1]
    slots, edge = picks.shape[4], picked.shape[-1]
    owned = owners.shape[-1] // replicas
    tokens = picked.shape[1] * picked.shape[2]
    for shift in range(groups):
        group = lax.rem(mine + shift, groups)
        source = error if shift == 0 else arrived[shift - 1]
        for slot in range(slots):
            row = picks[0, replica, 0, group, slot, 0]
            col = picks[0, replica, 0, group, slot, 1]
            left = picked[group * slots + slot].reshape(tokens, edge)
            right = returned[shift][0, :, :, column(col, edge)].reshape(tokens, edge)
            tile = lax.dot_general(
                left, right, (((0,), (0,)), ((), ())), preferred_element_type=jnp.float32
            )
            tile = tile + source[0, 0, 0, mine, slot].astype(jnp.float32)
            away = lax.rem(owners[0, 0, row] // owned - replica + replicas, replicas)
            if len(outs) == 1:
                outs[0][away] = tile
            else:
                for step, out in enumerate(outs):

                    @pl.when(away == step)
                    def _():
                        out[...] = tile


def place(count, picks, owners, *refs):
    blocks, strip, staged, places, sent = refs[:count], refs[-4], refs[-3], refs[-2], refs[-1]
    replica = lax.axis_index("dp")
    replicas, groups, slots = picks.shape[1], picks.shape[3], picks.shape[4]
    edge = staged.shape[-1]
    owned = owners.shape[-1] // replicas
    columns = strip.shape[-1] // edge
    per_group = columns // groups

    def block_of(step):
        return blocks[0][step] if count == 1 else blocks[step][...]

    for step in range(replicas):
        origin = lax.rem(replica - step + replicas, replicas)
        spot = jnp.int32(-1)
        for group in range(groups):
            for slot in range(slots):
                row = owners[0, 0, picks[0, origin, 0, group, slot, 0]]
                col = picks[0, origin, 0, group, slot, 1] + group * per_group
                here = lax.rem(row, owned) * columns + col
                spot = jnp.where(row // owned == replica, here, spot)
        places[step] = spot

    def first_of(step):
        spot = places[step]
        first = spot >= 0
        for earlier in range(step):
            first = first & (places[earlier] != spot)
        return first

    def write_of(step):
        spot = places[step]
        row, col = spot // columns, lax.rem(spot, columns)
        return pltpu.make_async_copy(
            staged.at[step], strip.at[0, 0, column(row, edge), column(col, edge)], sent.at[step]
        )

    for step in range(replicas):

        @pl.when(first_of(step))
        def _():
            total = block_of(step)
            for later in range(step + 1, replicas):
                meets = places[later] == places[step]
                total = total + jnp.where(meets, block_of(later), 0.0)
            staged[step] = total.astype(staged.dtype)
            write_of(step).start()

    for step in range(replicas):

        @pl.when(first_of(step))
        def _():
            write_of(step).wait()


def body(mesh, activations, cotangent, error_tiles, tile_picks, row_owners):
    sections, replicas, groups = mesh.shape["pipe"], mesh.shape["dp"], mesh.shape["tensor"]
    edge = error_tiles.shape[-1]
    slots = tile_picks.shape[4]
    micro, tokens = activations.shape[1:3]
    width = cotangent.shape[-1] * groups
    strip_rows = row_owners.shape[-1] // replicas * edge
    strip_shape = jax.ShapeDtypeStruct((1, 1, strip_rows, width), jnp.bfloat16)

    returned = []
    for shift in range(groups):
        pairs = [
            (
                (section + 1) % sections * groups + (group + shift) % groups,
                section * groups + group,
            )
            for section in range(sections)
            for group in range(groups)
        ]
        returned.append(lax.ppermute(cotangent, ("pipe", "tensor"), pairs))
    arrived = [
        lax.ppermute(
            error_tiles, "tensor", [((group + shift) % groups, group) for group in range(groups)]
        )
        for shift in range(1, groups)
    ]

    zero_rows = min(strip_rows, 256)
    picked, cleared = pl.pallas_call(
        prepare,
        out_shape=(
            jax.ShapeDtypeStruct((groups * slots, micro, tokens, edge), activations.dtype),
            strip_shape,
        ),
        in_specs=[SMEM, ANY],
        out_specs=(VMEM, ANY),
        scratch_shapes=[
            pltpu.VMEM((zero_rows, width), jnp.bfloat16),
            pltpu.SemaphoreType.DMA((groups * slots,)),
            pltpu.SemaphoreType.DMA((strip_rows // zero_rows,)),
        ],
        cost_estimate=pl.CostEstimate(
            flops=0, bytes_accessed=2 * strip_rows * width, transcendentals=0
        ),
        name="prepare",
    )(tile_picks, activations)

    tile_shape = (edge, edge)
    apart = replicas <= MOST_SHIFTS
    out_shape = (
        [jax.ShapeDtypeStruct(tile_shape, jnp.float32)] * replicas
        if apart
        else [jax.ShapeDtypeStruct((replicas,) + tile_shape, jnp.float32)]
    )
    outgoing = pl.pallas_call(
        functools.partial(multiply, groups),
        out_shape=out_shape,
        in_specs=[SMEM, SMEM] + [VMEM] * (2 * groups + 1),
        out_specs=[VMEM] * len(out_shape),
        name="multiply",
    )(tile_picks, row_owners, picked, error_tiles, *returned, *arrived)
    if apart:
        incoming = [outgoing[0]] + [
            lax.ppermute(
                outgoing[shift],
                "dp",
                [(source, (source + shift) % replicas) for source in range(replicas)],
            )
            for shift in range(1, replicas)
        ]
    else:
        replica = lax.axis_index("dp")
        owner = (jnp.arange(replicas, dtype=jnp.int32) - replica) % replicas
        swapped = lax.all_to_all(
            jnp.take(outgoing[0], owner, axis=0), "dp", split_axis=0, concat_axis=0, tiled=True
        )
        origin = (replica - jnp.arange(replicas, dtype=jnp.int32)) % replicas
        incoming = [jnp.take(swapped, origin, axis=0)]

    return pl.pallas_call(
        functools.partial(place, len(incoming)),
        out_shape=strip_shape,
        in_specs=[SMEM, SMEM] + [VMEM] * len(incoming) + [ANY],
        out_specs=ANY,
        scratch_shapes=[
            pltpu.VMEM((replicas,) + tile_shape, jnp.bfloat16),
            pltpu.SMEM((replicas,), jnp.int32),
            pltpu.SemaphoreType.DMA((replicas,)),
        ],
        input_output_aliases={2 + len(incoming): 0},
        name="place",
    )(tile_picks, row_owners, *incoming, cleared)


def solution(mesh):
    in_specs = (
        P("pipe", None, "dp", "tensor"),
        P("pipe", None, "dp", "tensor"),
        P("pipe", "dp", "tensor", None, None, None, None),
        P("pipe", None, "tensor", None, None, None),
        P("pipe", "tensor", None),
    )
    out_specs = P("pipe", "tensor", "dp", None)
    return jax.shard_map(
        functools.partial(body, mesh),
        mesh=mesh,
        in_specs=in_specs,
        out_specs=out_specs,
        check_vma=False,
    )
```

```python
import functools

import jax
import jax.numpy as jnp
from jax import lax
from jax.experimental import pallas as pl
from jax.experimental.pallas import tpu as pltpu
from jax.sharding import PartitionSpec as P

VMEM = pl.BlockSpec(memory_space=pltpu.VMEM)
SMEM = pl.BlockSpec(memory_space=pltpu.SMEM)
ANY = pl.BlockSpec(memory_space=pl.ANY)
MOST_STEPS = 8
SMALL = pltpu.CompilerParams(vmem_limit_bytes=4 << 20)


def column(index, edge):
    return pl.ds(pl.multiple_of(index * edge, edge), edge)


def partner(replica, step, replicas):
    return step if replicas > MOST_STEPS else lax.bitwise_xor(replica, step)


def prepare(picks, activations, picked, strip, zeros, copied, cleared):
    replica = lax.axis_index("dp")
    groups, slots, edge = picks.shape[3], picks.shape[4], picked.shape[-1]
    reads = []
    for group in range(groups):
        for slot in range(slots):
            at = group * slots + slot
            block = picks[0, replica, 0, group, slot, 0]
            reads.append(
                pltpu.make_async_copy(
                    activations.at[0, :, :, column(block, edge)], picked.at[at], copied.at[at]
                )
            )
    for read in reads:
        read.start()
    zeros[...] = jnp.zeros_like(zeros)
    rows = zeros.shape[0]
    writes = [
        pltpu.make_async_copy(zeros, strip.at[0, 0, pl.ds(part * rows, rows)], cleared.at[part])
        for part in range(strip.shape[2] // rows)
    ]
    for write in writes:
        write.start()
    for read in reads:
        read.wait()
    for write in writes:
        write.wait()


def multiply(groups, picks, owners, picked, error, *refs):
    returned, arrived, outs = refs[:groups], refs[groups : 2 * groups - 1], refs[2 * groups - 1 :]
    replica, mine = lax.axis_index("dp"), lax.axis_index("tensor")
    replicas = picks.shape[1]
    slots, edge = picks.shape[4], picked.shape[-1]
    owned = owners.shape[-1] // replicas
    tokens = picked.shape[1] * picked.shape[2]
    for shift in range(groups):
        group = lax.rem(mine + shift, groups)
        source = error if shift == 0 else arrived[shift - 1]
        for slot in range(slots):
            row = picks[0, replica, 0, group, slot, 0]
            col = picks[0, replica, 0, group, slot, 1]
            left = picked[group * slots + slot].reshape(tokens, edge)
            right = returned[shift][0, :, :, column(col, edge)].reshape(tokens, edge)
            tile = lax.dot_general(
                left, right, (((0,), (0,)), ((), ())), preferred_element_type=jnp.float32
            )
            carried = source[0, 0, 0, mine if shift == 0 else 0, slot]
            tile = tile + carried.astype(jnp.float32)
            away = partner(replica, owners[0, 0, row] // owned, replicas)
            if len(outs) == 1:
                outs[0][away] = tile
            else:
                for step, out in enumerate(outs):

                    @pl.when(away == step)
                    def _():
                        out[...] = tile


def place(count, picks, owners, *refs):
    blocks, strip, staged, places, sent = refs[:count], refs[-4], refs[-3], refs[-2], refs[-1]
    replica = lax.axis_index("dp")
    replicas, groups, slots = picks.shape[1], picks.shape[3], picks.shape[4]
    edge = staged.shape[-1]
    owned = owners.shape[-1] // replicas
    columns = strip.shape[-1] // edge
    per_group = columns // groups

    def block_of(step):
        return blocks[0][step] if count == 1 else blocks[step][...]

    for step in range(replicas):
        origin = partner(replica, jnp.int32(step), replicas)
        spot = jnp.int32(-1)
        for group in range(groups):
            for slot in range(slots):
                row = owners[0, 0, picks[0, origin, 0, group, slot, 0]]
                col = picks[0, origin, 0, group, slot, 1] + group * per_group
                here = lax.rem(row, owned) * columns + col
                spot = jnp.where(row // owned == replica, here, spot)
        places[step] = spot

    def first_of(step):
        spot = places[step]
        first = spot >= 0
        for earlier in range(step):
            first = first & (places[earlier] != spot)
        return first

    def write_of(step):
        spot = places[step]
        row, col = spot // columns, lax.rem(spot, columns)
        return pltpu.make_async_copy(
            staged.at[step], strip.at[0, 0, column(row, edge), column(col, edge)], sent.at[step]
        )

    for step in range(replicas):

        @pl.when(first_of(step))
        def _():
            total = block_of(step)
            for later in range(step + 1, replicas):
                meets = places[later] == places[step]
                total = total + jnp.where(meets, block_of(later), 0.0)
            staged[step] = total.astype(staged.dtype)
            write_of(step).start()

    for step in range(replicas):

        @pl.when(first_of(step))
        def _():
            write_of(step).wait()


def body(mesh, activations, cotangent, error_tiles, tile_picks, row_owners):
    sections, replicas, groups = mesh.shape["pipe"], mesh.shape["dp"], mesh.shape["tensor"]
    edge = error_tiles.shape[-1]
    slots = tile_picks.shape[4]
    micro, tokens = activations.shape[1:3]
    width = cotangent.shape[-1] * groups
    strip_rows = row_owners.shape[-1] // replicas * edge
    strip_shape = jax.ShapeDtypeStruct((1, 1, strip_rows, width), jnp.bfloat16)

    mine = lax.axis_index("tensor")
    returned = []
    for shift in range(groups):
        pairs = [
            (
                (section + 1) % sections * groups + (group + shift) % groups,
                section * groups + group,
            )
            for section in range(sections)
            for group in range(groups)
        ]
        returned.append(lax.ppermute(cotangent, ("pipe", "tensor"), pairs))
    arrived = [
        lax.ppermute(
            lax.dynamic_index_in_dim(error_tiles, (mine - shift + groups) % groups, axis=3),
            "tensor",
            [((group + shift) % groups, group) for group in range(groups)],
        )
        for shift in range(1, groups)
    ]

    zero_rows = min(strip_rows, 256)
    picked, cleared = pl.pallas_call(
        prepare,
        out_shape=(
            jax.ShapeDtypeStruct((groups * slots, micro, tokens, edge), activations.dtype),
            strip_shape,
        ),
        in_specs=[SMEM, ANY],
        out_specs=(VMEM, ANY),
        scratch_shapes=[
            pltpu.VMEM((zero_rows, width), jnp.bfloat16),
            pltpu.SemaphoreType.DMA((groups * slots,)),
            pltpu.SemaphoreType.DMA((strip_rows // zero_rows,)),
        ],
        cost_estimate=pl.CostEstimate(
            flops=0, bytes_accessed=2 * strip_rows * width, transcendentals=0
        ),
        name="prepare",
    )(tile_picks, activations)

    tile_shape = (edge, edge)
    apart = replicas <= MOST_STEPS
    out_shape = (
        [jax.ShapeDtypeStruct(tile_shape, jnp.float32)] * replicas
        if apart
        else [jax.ShapeDtypeStruct((replicas,) + tile_shape, jnp.float32)]
    )
    outgoing = pl.pallas_call(
        functools.partial(multiply, groups),
        out_shape=out_shape,
        in_specs=[SMEM, SMEM] + [VMEM] * (2 * groups + 1),
        out_specs=[VMEM] * len(out_shape),
        compiler_params=SMALL,
        name="multiply",
    )(tile_picks, row_owners, picked, error_tiles, *returned, *arrived)
    if apart:
        incoming = list(outgoing)
        for step in sorted(range(1, replicas), key=lambda step: (-step.bit_length(), step)):
            pairs = [(source, source ^ step) for source in range(replicas)]
            incoming[step] = lax.ppermute(outgoing[step], "dp", pairs)
    else:
        incoming = [lax.all_to_all(outgoing[0], "dp", split_axis=0, concat_axis=0, tiled=True)]

    return pl.pallas_call(
        functools.partial(place, len(incoming)),
        out_shape=strip_shape,
        in_specs=[SMEM, SMEM] + [VMEM] * len(incoming) + [ANY],
        out_specs=ANY,
        scratch_shapes=[
            pltpu.VMEM((replicas,) + tile_shape, jnp.bfloat16),
            pltpu.SMEM((replicas,), jnp.int32),
            pltpu.SemaphoreType.DMA((replicas,)),
        ],
        input_output_aliases={2 + len(incoming): 0},
        compiler_params=SMALL,
        name="place",
    )(tile_picks, row_owners, *incoming, cleared)


def solution(mesh):
    in_specs = (
        P("pipe", None, "dp", "tensor"),
        P("pipe", None, "dp", "tensor"),
        P("pipe", "dp", "tensor", None, None, None, None),
        P("pipe", None, "tensor", None, None, None),
        P("pipe", "tensor", None),
    )
    out_specs = P("pipe", "tensor", "dp", None)
    return jax.shard_map(
        functools.partial(body, mesh),
        mesh=mesh,
        in_specs=in_specs,
        out_specs=out_specs,
        check_vma=False,
    )
```

```python
import functools

import jax
import jax.numpy as jnp
from jax import lax
from jax.experimental import pallas as pl
from jax.experimental.pallas import tpu as pltpu
from jax.sharding import PartitionSpec as P

VMEM = pl.BlockSpec(memory_space=pltpu.VMEM)
SMEM = pl.BlockSpec(memory_space=pltpu.SMEM)
ANY = pl.BlockSpec(memory_space=pl.ANY)
MOST_STEPS = 8
SMALL = pltpu.CompilerParams(vmem_limit_bytes=4 << 20)


def column(index, edge):
    return pl.ds(pl.multiple_of(index * edge, edge), edge)


def partner(replica, step, replicas):
    return step if replicas > MOST_STEPS else lax.bitwise_xor(replica, step)


def pick(shifts, picks, *refs):
    asked, (activations, cotangent), (picked, *cuts) = refs[:shifts], refs[shifts:-shifts - 2], refs[-shifts - 2:-1]
    copied = refs[-1]
    replica, mine = lax.axis_index("dp"), lax.axis_index("tensor")
    groups, slots, edge = picks.shape[2], picks.shape[3], picked.shape[-1]
    reads = []

    def read(source, block, target):
        reads.append(
            pltpu.make_async_copy(
                source.at[0, :, :, column(block, edge)], target, copied.at[len(reads)]
            )
        )

    for wanted, cut in zip(asked, cuts):
        for slot in range(slots):
            read(cotangent, wanted[0, 0, mine, slot, 1, replica], cut.at[slot])
    for group in range(groups):
        for slot in range(slots):
            block = picks[0, 0, group, slot, 0, replica]
            read(activations, block, picked.at[group * slots + slot])
    for copy in reads:
        copy.start()
    for copy in reads:
        copy.wait()


def clear(after, strip, zeros, cleared):
    zeros[...] = jnp.zeros_like(zeros)
    rows = zeros.shape[0]
    writes = [
        pltpu.make_async_copy(zeros, strip.at[0, 0, pl.ds(part * rows, rows)], cleared.at[part])
        for part in range(strip.shape[2] // rows)
    ]
    for write in writes:
        write.start()
    for write in writes:
        write.wait()


def multiply(groups, picks, owners, picked, error, returned, *refs):
    cuts, carried, outs = refs[: groups - 1], refs[groups - 1 : 2 * groups - 2], refs[2 * groups - 2 :]
    replica, mine = lax.axis_index("dp"), lax.axis_index("tensor")
    replicas = picks.shape[-1]
    slots, edge = picks.shape[3], picked.shape[-1]
    owned = owners.shape[-1] // replicas
    tokens = picked.shape[1] * picked.shape[2]
    for shift in range(groups):
        group = lax.rem(mine + shift, groups)
        for slot in range(slots):
            row = picks[0, 0, group, slot, 0, replica]
            left = picked[group * slots + slot].reshape(tokens, edge)
            if shift == 0:
                right = returned[0, :, :, column(picks[0, 0, group, slot, 1, replica], edge)]
                extra = error[0, 0, 0, mine, slot]
            else:
                right = cuts[shift - 1][slot]
                extra = carried[shift - 1][0, 0, 0, 0, slot]
            tile = lax.dot_general(
                left,
                right.reshape(tokens, edge),
                (((0,), (0,)), ((), ())),
                preferred_element_type=jnp.float32,
            )
            tile = tile + extra.astype(jnp.float32)
            away = partner(replica, owners[0, 0, row] // owned, replicas)
            if len(outs) == 1:
                outs[0][away] = tile
            else:
                for step, out in enumerate(outs):

                    @pl.when(away == step)
                    def _():
                        out[...] = tile


def place(count, picks, owners, *refs):
    blocks, strip, staged, places, sent = refs[:count], refs[-4], refs[-3], refs[-2], refs[-1]
    replica = lax.axis_index("dp")
    groups, slots, replicas = picks.shape[2], picks.shape[3], picks.shape[-1]
    edge = staged.shape[-1]
    owned = owners.shape[-1] // replicas
    columns = strip.shape[-1] // edge
    per_group = columns // groups

    def block_of(step):
        return blocks[0][step] if count == 1 else blocks[step][...]

    for step in range(replicas):
        origin = partner(replica, jnp.int32(step), replicas)
        spot = jnp.int32(-1)
        for group in range(groups):
            for slot in range(slots):
                row = owners[0, 0, picks[0, 0, group, slot, 0, origin]]
                col = picks[0, 0, group, slot, 1, origin] + group * per_group
                here = lax.rem(row, owned) * columns + col
                spot = jnp.where(row // owned == replica, here, spot)
        places[step] = spot

    def first_of(step):
        spot = places[step]
        first = spot >= 0
        for earlier in range(step):
            first = first & (places[earlier] != spot)
        return first

    def write_of(step):
        spot = places[step]
        row, col = spot // columns, lax.rem(spot, columns)
        return pltpu.make_async_copy(
            staged.at[step], strip.at[0, 0, column(row, edge), column(col, edge)], sent.at[step]
        )

    for step in range(replicas):

        @pl.when(first_of(step))
        def _():
            total = block_of(step)
            for later in range(step + 1, replicas):
                meets = places[later] == places[step]
                total = total + jnp.where(meets, block_of(later), 0.0)
            staged[step] = total.astype(staged.dtype)
            write_of(step).start()

    for step in range(replicas):

        @pl.when(first_of(step))
        def _():
            write_of(step).wait()


def body(mesh, activations, cotangent, error_tiles, tile_picks, row_owners):
    sections, replicas, groups = mesh.shape["pipe"], mesh.shape["dp"], mesh.shape["tensor"]
    edge = error_tiles.shape[-1]
    slots = tile_picks.shape[4]
    micro, tokens = activations.shape[1:3]
    width = cotangent.shape[-1] * groups
    strip_rows = row_owners.shape[-1] // replicas * edge
    mine = lax.axis_index("tensor")
    shifts = groups - 1
    picks = jnp.transpose(tile_picks, (0, 2, 3, 4, 5, 1))

    def to_next(value, shift):
        pairs = [
            (
                section * groups + group,
                (section + 1) % sections * groups + (group + shift) % groups,
            )
            for section in range(sections)
            for group in range(groups)
        ]
        return lax.ppermute(value, ("pipe", "tensor"), pairs)

    def to_previous(value, shift):
        pairs = [
            (
                (section + 1) % sections * groups + (group + shift) % groups,
                section * groups + group,
            )
            for section in range(sections)
            for group in range(groups)
        ]
        return lax.ppermute(value, ("pipe", "tensor"), pairs)

    asked = [to_next(picks, shift) for shift in range(1, groups)]
    returned = to_previous(cotangent, 0)
    block_shape = (micro, tokens, edge)
    picked, *cuts = pl.pallas_call(
        functools.partial(pick, shifts),
        out_shape=[pltpu.VMEM((groups * slots,) + block_shape, activations.dtype)]
        + [pltpu.VMEM((slots,) + block_shape, cotangent.dtype)] * shifts,
        in_specs=[SMEM] * (1 + shifts) + [ANY, ANY],
        out_specs=[VMEM] * (1 + shifts),
        scratch_shapes=[pltpu.SemaphoreType.DMA(((groups + shifts) * slots,))],
        compiler_params=SMALL,
        name="pick",
    )(
        picks,
        *asked,
        pltpu.with_memory_space_constraint(activations, pltpu.HBM),
        pltpu.with_memory_space_constraint(cotangent, pltpu.HBM),
    )
    arrived = [to_previous(cut, shift + 1) for shift, cut in enumerate(cuts)]
    carried = [
        lax.ppermute(
            lax.dynamic_index_in_dim(error_tiles, (mine - shift + groups) % groups, axis=3),
            "tensor",
            [((group + shift) % groups, group) for group in range(groups)],
        )
        for shift in range(1, groups)
    ]

    zero_rows = min(strip_rows, 256)
    strip_shape = (1, 1, strip_rows, width)
    cleared = pl.pallas_call(
        clear,
        out_shape=pltpu.HBM(strip_shape, jnp.bfloat16),
        in_specs=[ANY],
        out_specs=pl.BlockSpec(memory_space=pltpu.HBM),
        scratch_shapes=[
            pltpu.VMEM((zero_rows, width), jnp.bfloat16),
            pltpu.SemaphoreType.DMA((strip_rows // zero_rows,)),
        ],
        compiler_params=SMALL,
        cost_estimate=pl.CostEstimate(
            flops=0, bytes_accessed=2 * strip_rows * width, transcendentals=0
        ),
        name="clear",
    )(cuts[0] if cuts else picked)

    tile_shape = (edge, edge)
    apart = replicas <= MOST_STEPS
    out_shape = (
        [jax.ShapeDtypeStruct(tile_shape, jnp.float32)] * replicas
        if apart
        else [jax.ShapeDtypeStruct((replicas,) + tile_shape, jnp.float32)]
    )
    outgoing = pl.pallas_call(
        functools.partial(multiply, groups),
        out_shape=out_shape,
        in_specs=[SMEM, SMEM] + [VMEM] * (2 * groups + 1),
        out_specs=[VMEM] * len(out_shape),
        compiler_params=SMALL,
        name="multiply",
    )(picks, row_owners, picked, error_tiles, returned, *arrived, *carried)
    if apart:
        incoming = list(outgoing)
        for step in sorted(range(1, replicas), key=lambda step: (-step.bit_length(), step)):
            pairs = [(source, source ^ step) for source in range(replicas)]
            incoming[step] = lax.ppermute(outgoing[step], "dp", pairs)
    else:
        incoming = [lax.all_to_all(outgoing[0], "dp", split_axis=0, concat_axis=0, tiled=True)]

    return pl.pallas_call(
        functools.partial(place, len(incoming)),
        out_shape=jax.ShapeDtypeStruct(strip_shape, jnp.bfloat16),
        in_specs=[SMEM, SMEM] + [VMEM] * len(incoming) + [ANY],
        out_specs=ANY,
        scratch_shapes=[
            pltpu.VMEM((replicas,) + tile_shape, jnp.bfloat16),
            pltpu.SMEM((replicas,), jnp.int32),
            pltpu.SemaphoreType.DMA((replicas,)),
        ],
        input_output_aliases={2 + len(incoming): 0},
        compiler_params=SMALL,
        name="place",
    )(picks, row_owners, *incoming, cleared)


def solution(mesh):
    in_specs = (
        P("pipe", None, "dp", "tensor"),
        P("pipe", None, "dp", "tensor"),
        P("pipe", "dp", "tensor", None, None, None, None),
        P("pipe", None, "tensor", None, None, None),
        P("pipe", "tensor", None),
    )
    out_specs = P("pipe", "tensor", "dp", None)
    return jax.shard_map(
        functools.partial(body, mesh),
        mesh=mesh,
        in_specs=in_specs,
        out_specs=out_specs,
        check_vma=False,
    )
```

```python
import functools

import jax
import jax.numpy as jnp
from jax import lax
from jax.experimental import pallas as pl
from jax.experimental.pallas import tpu as pltpu
from jax.sharding import PartitionSpec as P

VMEM = pl.BlockSpec(memory_space=pltpu.VMEM)
SMEM = pl.BlockSpec(memory_space=pltpu.SMEM)
ANY = pl.BlockSpec(memory_space=pl.ANY)
MOST_STEPS = 8
SMALL = pltpu.CompilerParams(vmem_limit_bytes=4 << 20)


def column(index, edge):
    return pl.ds(pl.multiple_of(index * edge, edge), edge)


def partner(replica, step, replicas):
    return step if replicas > MOST_STEPS else lax.bitwise_xor(replica, step)


def pick(picks, activations, picked, meets, copied, seen):
    replica = lax.axis_index("dp")
    groups, slots, replicas = picks.shape[2], picks.shape[3], picks.shape[-1]
    edge = picked.shape[-1]
    reads = []
    for group in range(groups):
        for slot in range(slots):
            at = group * slots + slot
            block = picks[0, 0, group, slot, 0, replica]
            reads.append(
                pltpu.make_async_copy(
                    activations.at[0, :, :, column(block, edge)], picked.at[at], copied.at[at]
                )
            )
    for read in reads:
        read.start()
    meets[0] = 0
    count = groups * slots * replicas
    per_group = seen.shape[0] // (activations.shape[-1] // edge * groups)

    def spot_of(tile):
        group, slot, origin = tile // (slots * replicas), tile // replicas % slots, tile % replicas
        row, col = picks[0, 0, group, slot, 0, origin], picks[0, 0, group, slot, 1, origin]
        return (row * groups + group) * per_group + col

    def forget(tile, carry):
        seen[spot_of(tile)] = 0
        return carry

    def note(tile, carry):
        spot = spot_of(tile)
        meets[0] = meets[0] | seen[spot]
        seen[spot] = 1
        return carry

    lax.fori_loop(0, count, forget, 0, unroll=count <= 32)
    lax.fori_loop(0, count, note, 0, unroll=count <= 32)
    for read in reads:
        read.wait()


def clear(after, strip, zeros, cleared):
    zeros[...] = jnp.zeros_like(zeros)
    rows = zeros.shape[0]
    writes = [
        pltpu.make_async_copy(zeros, strip.at[0, 0, pl.ds(part * rows, rows)], cleared.at[part])
        for part in range(strip.shape[2] // rows)
    ]
    for write in writes:
        write.start()
    for write in writes:
        write.wait()


def multiply(groups, picks, owners, picked, error, *refs):
    returned, carried, outs = refs[:groups], refs[groups : 2 * groups - 1], refs[2 * groups - 1 :]
    replica, mine = lax.axis_index("dp"), lax.axis_index("tensor")
    replicas = picks.shape[-1]
    slots, edge = picks.shape[3], picked.shape[-1]
    owned = owners.shape[-1] // replicas
    tokens = picked.shape[1] * picked.shape[2]
    for shift in range(groups):
        group = lax.rem(mine + shift, groups)
        for slot in range(slots):
            row = picks[0, 0, group, slot, 0, replica]
            left = picked[group * slots + slot].reshape(tokens, edge)
            right = returned[shift][0, :, :, column(picks[0, 0, group, slot, 1, replica], edge)]
            extra = error[0, 0, 0, mine, slot] if shift == 0 else carried[shift - 1][0, 0, 0, 0, slot]
            tile = lax.dot_general(
                left,
                right.reshape(tokens, edge),
                (((0,), (0,)), ((), ())),
                preferred_element_type=jnp.float32,
            )
            tile = tile + extra.astype(jnp.float32)
            away = partner(replica, owners[0, 0, row] // owned, replicas)
            if len(outs) == 1:
                outs[0][away] = tile
            else:
                for step in range(replicas):

                    @pl.when(away == step)
                    def _():
                        outs[step][...] = tile
                        outs[replicas + step][...] = tile.astype(jnp.bfloat16)


def place(count, alone, picks, owners, *refs):
    blocks, strip, staged, places, sent = refs[:count], refs[-4], refs[-3], refs[-2], refs[-1]
    replica = lax.axis_index("dp")
    groups, slots, replicas = picks.shape[2], picks.shape[3], picks.shape[-1]
    edge = staged.shape[-1]
    owned = owners.shape[-1] // replicas
    columns = strip.shape[-1] // edge
    per_group = columns // groups

    def block_of(step):
        return blocks[0][step] if count == 1 else blocks[step][...]

    for step in range(replicas):
        origin = partner(replica, jnp.int32(step), replicas)
        spot = jnp.int32(-1)
        for group in range(groups):
            for slot in range(slots):
                row = owners[0, 0, picks[0, 0, group, slot, 0, origin]]
                col = picks[0, 0, group, slot, 1, origin] + group * per_group
                here = lax.rem(row, owned) * columns + col
                spot = jnp.where(row // owned == replica, here, spot)
        places[step] = spot

    def first_of(step):
        spot = places[step]
        first = spot >= 0
        for earlier in range(0 if alone else step):
            first = first & (places[earlier] != spot)
        return first

    def write_of(step):
        spot = places[step]
        row, col = spot // columns, lax.rem(spot, columns)
        return pltpu.make_async_copy(
            blocks[step] if alone else staged.at[step],
            strip.at[0, 0, column(row, edge), column(col, edge)],
            sent.at[step],
        )

    for step in range(replicas):

        @pl.when(first_of(step))
        def _():
            if not alone:
                total = block_of(step)
                for later in range(step + 1, replicas):
                    meets = places[later] == places[step]
                    total = total + jnp.where(meets, block_of(later), 0.0)
                staged[step] = total.astype(staged.dtype)
            write_of(step).start()

    for step in range(replicas):

        @pl.when(first_of(step))
        def _():
            write_of(step).wait()


def body(mesh, activations, cotangent, error_tiles, tile_picks, row_owners):
    sections, replicas, groups = mesh.shape["pipe"], mesh.shape["dp"], mesh.shape["tensor"]
    edge = error_tiles.shape[-1]
    slots = tile_picks.shape[4]
    micro, tokens = activations.shape[1:3]
    width = cotangent.shape[-1] * groups
    strip_rows = row_owners.shape[-1] // replicas * edge
    mine = lax.axis_index("tensor")
    picks = jnp.transpose(tile_picks, (0, 2, 3, 4, 5, 1))

    returned = []
    for shift in range(groups):
        pairs = [
            (
                (section + 1) % sections * groups + (group + shift) % groups,
                section * groups + group,
            )
            for section in range(sections)
            for group in range(groups)
        ]
        returned.append(lax.ppermute(cotangent, ("pipe", "tensor"), pairs))
    carried = [
        lax.ppermute(
            lax.dynamic_index_in_dim(error_tiles, (mine - shift + groups) % groups, axis=3),
            "tensor",
            [((group + shift) % groups, group) for group in range(groups)],
        )
        for shift in range(1, groups)
    ]
    picked, meets = pl.pallas_call(
        pick,
        out_shape=[
            pltpu.VMEM((groups * slots, micro, tokens, edge), activations.dtype),
            jax.ShapeDtypeStruct((1,), jnp.int32),
        ],
        in_specs=[SMEM, ANY],
        out_specs=[VMEM, SMEM],
        scratch_shapes=[
            pltpu.SemaphoreType.DMA((groups * slots,)),
            pltpu.SMEM((row_owners.shape[-1] * (width // edge),), jnp.int32),
        ],
        compiler_params=SMALL,
        name="pick",
    )(picks, pltpu.with_memory_space_constraint(activations, pltpu.HBM))

    zero_rows = min(strip_rows, 256)
    strip_shape = (1, 1, strip_rows, width)
    cleared = pl.pallas_call(
        clear,
        out_shape=pltpu.HBM(strip_shape, jnp.bfloat16),
        in_specs=[ANY],
        out_specs=pl.BlockSpec(memory_space=pltpu.HBM),
        scratch_shapes=[
            pltpu.VMEM((zero_rows, width), jnp.bfloat16),
            pltpu.SemaphoreType.DMA((strip_rows // zero_rows,)),
        ],
        compiler_params=SMALL,
        cost_estimate=pl.CostEstimate(
            flops=0, bytes_accessed=2 * strip_rows * width, transcendentals=0
        ),
        name="clear",
    )(picked)

    tile_shape = (edge, edge)
    apart = replicas <= MOST_STEPS
    if apart:
        out_shape = [
            jax.ShapeDtypeStruct(tile_shape, dtype)
            for dtype in (jnp.float32, jnp.bfloat16)
            for step in range(replicas)
        ]
    else:
        out_shape = [jax.ShapeDtypeStruct((replicas,) + tile_shape, jnp.float32)]
    outgoing = pl.pallas_call(
        functools.partial(multiply, groups),
        out_shape=out_shape,
        in_specs=[SMEM, SMEM] + [VMEM] * (2 * groups + 1),
        out_specs=[VMEM] * len(out_shape),
        compiler_params=SMALL,
        name="multiply",
    )(picks, row_owners, picked, error_tiles, *returned, *carried)

    def placed(alone, incoming):
        return pl.pallas_call(
            functools.partial(place, len(incoming), alone),
            out_shape=jax.ShapeDtypeStruct(strip_shape, jnp.bfloat16),
            in_specs=[SMEM, SMEM] + [VMEM] * len(incoming) + [ANY],
            out_specs=ANY,
            scratch_shapes=[
                pltpu.VMEM((replicas,) + tile_shape, jnp.bfloat16),
                pltpu.SMEM((replicas,), jnp.int32),
                pltpu.SemaphoreType.DMA((replicas,)),
            ],
            input_output_aliases={2 + len(incoming): 0},
            compiler_params=SMALL,
            name="place",
        )(picks, row_owners, *incoming, cleared)

    def exchanged(blocks):
        blocks = list(blocks)
        for step in sorted(range(1, replicas), key=lambda step: (-step.bit_length(), step)):
            pairs = [(source, source ^ step) for source in range(replicas)]
            blocks[step] = lax.ppermute(blocks[step], "dp", pairs)
        return blocks

    if not apart:
        swapped = lax.all_to_all(outgoing[0], "dp", split_axis=0, concat_axis=0, tiled=True)
        return placed(False, [swapped])
    return lax.cond(
        meets[0] > 0,
        lambda: placed(False, exchanged(outgoing[:replicas])),
        lambda: placed(True, exchanged(outgoing[replicas:])),
    )


def solution(mesh):
    in_specs = (
        P("pipe", None, "dp", "tensor"),
        P("pipe", None, "dp", "tensor"),
        P("pipe", "dp", "tensor", None, None, None, None),
        P("pipe", None, "tensor", None, None, None),
        P("pipe", "tensor", None),
    )
    out_specs = P("pipe", "tensor", "dp", None)
    return jax.shard_map(
        functools.partial(body, mesh),
        mesh=mesh,
        in_specs=in_specs,
        out_specs=out_specs,
        check_vma=False,
    )
```

```python
import functools

import jax
import jax.numpy as jnp
from jax import lax
from jax.experimental import pallas as pl
from jax.experimental.pallas import tpu as pltpu
from jax.sharding import PartitionSpec as P

VMEM = pl.BlockSpec(memory_space=pltpu.VMEM)
SMEM = pl.BlockSpec(memory_space=pltpu.SMEM)
ANY = pl.BlockSpec(memory_space=pl.ANY)
MOST_GATHERED = 8
SMALL = pltpu.CompilerParams(vmem_limit_bytes=4 << 20)


def column(index, edge):
    return pl.ds(pl.multiple_of(index * edge, edge), edge)


def pick(picks, activations, picked, meets, copied, seen):
    replica = lax.axis_index("dp")
    groups, slots, replicas = picks.shape[2], picks.shape[3], picks.shape[-1]
    edge = picked.shape[-1]
    reads = []
    for group in range(groups):
        for slot in range(slots):
            at = group * slots + slot
            block = picks[0, 0, group, slot, 0, replica]
            reads.append(
                pltpu.make_async_copy(
                    activations.at[0, :, :, column(block, edge)], picked.at[at], copied.at[at]
                )
            )
    for read in reads:
        read.start()
    meets[0] = 0
    count = groups * slots * replicas
    per_group = seen.shape[0] // (activations.shape[-1] // edge * groups)

    def spot_of(tile):
        group, slot, origin = tile // (slots * replicas), tile // replicas % slots, tile % replicas
        row, col = picks[0, 0, group, slot, 0, origin], picks[0, 0, group, slot, 1, origin]
        return (row * groups + group) * per_group + col

    def forget(tile, carry):
        seen[spot_of(tile)] = 0
        return carry

    def note(tile, carry):
        spot = spot_of(tile)
        meets[0] = meets[0] | seen[spot]
        seen[spot] = 1
        return carry

    lax.fori_loop(0, count, forget, 0, unroll=count <= 32)
    lax.fori_loop(0, count, note, 0, unroll=count <= 32)
    for read in reads:
        read.wait()


def clear(after, strip, zeros, cleared):
    zeros[...] = jnp.zeros_like(zeros)
    rows = zeros.shape[0]
    writes = [
        pltpu.make_async_copy(zeros, strip.at[0, 0, pl.ds(part * rows, rows)], cleared.at[part])
        for part in range(strip.shape[2] // rows)
    ]
    for write in writes:
        write.start()
    for write in writes:
        write.wait()


def multiply(groups, picks, owners, picked, error, *refs):
    returned, carried, outs = refs[:groups], refs[groups : 2 * groups - 1], refs[2 * groups - 1 :]
    replica, mine = lax.axis_index("dp"), lax.axis_index("tensor")
    replicas = picks.shape[-1]
    slots, edge = picks.shape[3], picked.shape[-1]
    owned = owners.shape[-1] // replicas
    tokens = picked.shape[1] * picked.shape[2]
    for shift in range(groups):
        group = lax.rem(mine + shift, groups)
        for slot in range(slots):
            row = picks[0, 0, group, slot, 0, replica]
            left = picked[group * slots + slot].reshape(tokens, edge)
            right = returned[shift][0, :, :, column(picks[0, 0, group, slot, 1, replica], edge)]
            extra = error[0, 0, 0, mine, slot] if shift == 0 else carried[shift - 1][0, 0, 0, 0, slot]
            tile = lax.dot_general(
                left,
                right.reshape(tokens, edge),
                (((0,), (0,)), ((), ())),
                preferred_element_type=jnp.float32,
            )
            tile = tile + extra.astype(jnp.float32)
            if len(outs) == 1:
                outs[0][owners[0, 0, row] // owned] = tile
            else:
                outs[0][group * slots + slot] = tile
                outs[1][group * slots + slot] = tile.astype(jnp.bfloat16)


def place(alone, picks, owners, blocks, cleared, strip, staged, places, held, sent):
    replica = lax.axis_index("dp")
    groups, slots, replicas = picks.shape[2], picks.shape[3], picks.shape[-1]
    edge = staged.shape[-1]
    owned = owners.shape[-1] // replicas
    columns = strip.shape[-1] // edge
    per_group = columns // groups

    def block_of(origin):
        return blocks.at[origin, held[origin]]

    for origin in range(replicas):
        spot, tile = jnp.int32(-1), jnp.int32(0)
        for group in range(groups):
            for slot in range(slots):
                row = owners[0, 0, picks[0, 0, group, slot, 0, origin]]
                col = picks[0, 0, group, slot, 1, origin] + group * per_group
                mine = row // owned == replica
                spot = jnp.where(mine, lax.rem(row, owned) * columns + col, spot)
                if blocks.shape[1] > 1:
                    tile = jnp.where(mine, group * slots + slot, tile)
        places[origin], held[origin] = spot, tile

    def first_of(step):
        spot = places[step]
        first = spot >= 0
        for earlier in range(0 if alone else step):
            first = first & (places[earlier] != spot)
        return first

    def write_of(step):
        spot = places[step]
        row, col = spot // columns, lax.rem(spot, columns)
        return pltpu.make_async_copy(
            block_of(step) if alone else staged.at[step],
            strip.at[0, 0, column(row, edge), column(col, edge)],
            sent.at[step],
        )

    for step in range(replicas):

        @pl.when(first_of(step))
        def _():
            if not alone:
                total = block_of(step)[...]
                for later in range(step + 1, replicas):
                    meets = places[later] == places[step]
                    total = total + jnp.where(meets, block_of(later)[...], 0.0)
                staged[step] = total.astype(staged.dtype)
            write_of(step).start()

    for step in range(replicas):

        @pl.when(first_of(step))
        def _():
            write_of(step).wait()


def body(mesh, activations, cotangent, error_tiles, tile_picks, row_owners):
    sections, replicas, groups = mesh.shape["pipe"], mesh.shape["dp"], mesh.shape["tensor"]
    edge = error_tiles.shape[-1]
    slots = tile_picks.shape[4]
    micro, tokens = activations.shape[1:3]
    width = cotangent.shape[-1] * groups
    strip_rows = row_owners.shape[-1] // replicas * edge
    mine = lax.axis_index("tensor")
    picks = jnp.transpose(tile_picks, (0, 2, 3, 4, 5, 1))

    returned = []
    for shift in range(groups):
        pairs = [
            (
                (section + 1) % sections * groups + (group + shift) % groups,
                section * groups + group,
            )
            for section in range(sections)
            for group in range(groups)
        ]
        returned.append(lax.ppermute(cotangent, ("pipe", "tensor"), pairs))
    carried = [
        lax.ppermute(
            lax.dynamic_index_in_dim(error_tiles, (mine - shift + groups) % groups, axis=3),
            "tensor",
            [((group + shift) % groups, group) for group in range(groups)],
        )
        for shift in range(1, groups)
    ]
    picked, meets = pl.pallas_call(
        pick,
        out_shape=[
            pltpu.VMEM((groups * slots, micro, tokens, edge), activations.dtype),
            jax.ShapeDtypeStruct((1,), jnp.int32),
        ],
        in_specs=[SMEM, ANY],
        out_specs=[VMEM, SMEM],
        scratch_shapes=[
            pltpu.SemaphoreType.DMA((groups * slots,)),
            pltpu.SMEM((row_owners.shape[-1] * (width // edge),), jnp.int32),
        ],
        compiler_params=SMALL,
        name="pick",
    )(picks, pltpu.with_memory_space_constraint(activations, pltpu.HBM))

    zero_rows = min(strip_rows, 256)
    strip_shape = (1, 1, strip_rows, width)
    cleared = pl.pallas_call(
        clear,
        out_shape=pltpu.HBM(strip_shape, jnp.bfloat16),
        in_specs=[ANY],
        out_specs=pl.BlockSpec(memory_space=pltpu.HBM),
        scratch_shapes=[
            pltpu.VMEM((zero_rows, width), jnp.bfloat16),
            pltpu.SemaphoreType.DMA((strip_rows // zero_rows,)),
        ],
        compiler_params=SMALL,
        cost_estimate=pl.CostEstimate(
            flops=0, bytes_accessed=2 * strip_rows * width, transcendentals=0
        ),
        name="clear",
    )(picked)

    tile_shape = (edge, edge)
    gathered = replicas <= MOST_GATHERED
    if gathered:
        out_shape = [
            jax.ShapeDtypeStruct((groups * slots,) + tile_shape, dtype)
            for dtype in (jnp.float32, jnp.bfloat16)
        ]
    else:
        out_shape = [jax.ShapeDtypeStruct((replicas,) + tile_shape, jnp.float32)]
    outgoing = pl.pallas_call(
        functools.partial(multiply, groups),
        out_shape=out_shape,
        in_specs=[SMEM, SMEM] + [VMEM] * (2 * groups + 1),
        out_specs=[VMEM] * len(out_shape),
        compiler_params=SMALL,
        name="multiply",
    )(picks, row_owners, picked, error_tiles, *returned, *carried)

    def placed(alone, blocks):
        return pl.pallas_call(
            functools.partial(place, alone),
            out_shape=jax.ShapeDtypeStruct(strip_shape, jnp.bfloat16),
            in_specs=[SMEM, SMEM, ANY if alone else VMEM, ANY],
            out_specs=ANY,
            scratch_shapes=[
                pltpu.VMEM((replicas,) + tile_shape, jnp.bfloat16),
                pltpu.SMEM((replicas,), jnp.int32),
                pltpu.SMEM((replicas,), jnp.int32),
                pltpu.SemaphoreType.DMA((replicas,)),
            ],
            input_output_aliases={3: 0},
            compiler_params=SMALL,
            name="place",
        )(picks, row_owners, blocks, cleared)

    if not gathered:
        swapped = lax.all_to_all(outgoing[0], "dp", split_axis=0, concat_axis=0, tiled=True)
        return placed(False, swapped[:, None])
    return lax.cond(
        meets[0] > 0,
        lambda: placed(False, lax.all_gather(outgoing[0], "dp")),
        lambda: placed(True, lax.all_gather(outgoing[1], "dp")),
    )


def solution(mesh):
    in_specs = (
        P("pipe", None, "dp", "tensor"),
        P("pipe", None, "dp", "tensor"),
        P("pipe", "dp", "tensor", None, None, None, None),
        P("pipe", None, "tensor", None, None, None),
        P("pipe", "tensor", None),
    )
    out_specs = P("pipe", "tensor", "dp", None)
    return jax.shard_map(
        functools.partial(body, mesh),
        mesh=mesh,
        in_specs=in_specs,
        out_specs=out_specs,
        check_vma=False,
    )
```

```python
import functools

import jax
import jax.numpy as jnp
from jax import lax
from jax.experimental import pallas as pl
from jax.experimental.pallas import tpu as pltpu
from jax.sharding import PartitionSpec as P

VMEM = pl.BlockSpec(memory_space=pltpu.VMEM)
SMEM = pl.BlockSpec(memory_space=pltpu.SMEM)
ANY = pl.BlockSpec(memory_space=pl.ANY)
MOST_STEPS = 8
SMALL = pltpu.CompilerParams(vmem_limit_bytes=4 << 20)


def column(index, edge):
    return pl.ds(pl.multiple_of(index * edge, edge), edge)


def partner(replica, step, replicas):
    return step if replicas > MOST_STEPS else lax.bitwise_xor(replica, step)


def pick(picks, activations, picked, meets, copied, seen):
    replica = lax.axis_index("dp")
    groups, slots, replicas = picks.shape[2], picks.shape[3], picks.shape[-1]
    edge = picked.shape[-1]
    reads = []
    for group in range(groups):
        for slot in range(slots):
            at = group * slots + slot
            block = picks[0, 0, group, slot, 0, replica]
            reads.append(
                pltpu.make_async_copy(
                    activations.at[0, :, :, column(block, edge)], picked.at[at], copied.at[at]
                )
            )
    for read in reads:
        read.start()
    meets[0] = 0
    count = groups * slots * replicas
    per_group = seen.shape[0] // (activations.shape[-1] // edge * groups)

    def spot_of(tile):
        group, slot, origin = tile // (slots * replicas), tile // replicas % slots, tile % replicas
        row, col = picks[0, 0, group, slot, 0, origin], picks[0, 0, group, slot, 1, origin]
        return (row * groups + group) * per_group + col

    def forget(tile, carry):
        seen[spot_of(tile)] = 0
        return carry

    def note(tile, carry):
        spot = spot_of(tile)
        meets[0] = meets[0] | seen[spot]
        seen[spot] = 1
        return carry

    lax.fori_loop(0, count, forget, 0, unroll=count <= 32)
    lax.fori_loop(0, count, note, 0, unroll=count <= 32)
    for read in reads:
        read.wait()


def clear(after, strip, zeros, cleared):
    zeros[...] = jnp.zeros_like(zeros)
    rows = zeros.shape[0]
    writes = [
        pltpu.make_async_copy(zeros, strip.at[0, 0, pl.ds(part * rows, rows)], cleared.at[part])
        for part in range(strip.shape[2] // rows)
    ]
    for write in writes:
        write.start()
    for write in writes:
        write.wait()


def multiply(groups, picks, owners, picked, error, *refs):
    returned, carried, outs = refs[:groups], refs[groups : 2 * groups - 1], refs[2 * groups - 1 :]
    replica, mine = lax.axis_index("dp"), lax.axis_index("tensor")
    replicas = picks.shape[-1]
    slots, edge = picks.shape[3], picked.shape[-1]
    owned = owners.shape[-1] // replicas
    tokens = picked.shape[1] * picked.shape[2]
    for shift in range(groups):
        group = lax.rem(mine + shift, groups)
        for slot in range(slots):
            row = picks[0, 0, group, slot, 0, replica]
            left = picked[group * slots + slot].reshape(tokens, edge)
            right = returned[shift][0, :, :, column(picks[0, 0, group, slot, 1, replica], edge)]
            extra = error[0, 0, 0, mine, slot] if shift == 0 else carried[shift - 1][0, 0, 0, 0, slot]
            tile = lax.dot_general(
                left,
                right.reshape(tokens, edge),
                (((0,), (0,)), ((), ())),
                preferred_element_type=jnp.float32,
            )
            tile = tile + extra.astype(jnp.float32)
            away = partner(replica, owners[0, 0, row] // owned, replicas)
            if len(outs) == 1:
                outs[0][away] = tile
            else:
                for step in range(replicas):

                    @pl.when(away == step)
                    def _():
                        outs[step][...] = tile
                        outs[replicas + step][...] = tile.astype(jnp.bfloat16)


def place(count, alone, picks, owners, *refs):
    blocks, strip, staged, places, sent = refs[:count], refs[-4], refs[-3], refs[-2], refs[-1]
    replica = lax.axis_index("dp")
    groups, slots, replicas = picks.shape[2], picks.shape[3], picks.shape[-1]
    edge = staged.shape[-1]
    owned = owners.shape[-1] // replicas
    columns = strip.shape[-1] // edge
    per_group = columns // groups

    def block_of(step):
        return blocks[0][step] if count == 1 else blocks[step][...]

    for step in range(replicas):
        origin = partner(replica, jnp.int32(step), replicas)
        spot = jnp.int32(-1)
        for group in range(groups):
            for slot in range(slots):
                row = owners[0, 0, picks[0, 0, group, slot, 0, origin]]
                col = picks[0, 0, group, slot, 1, origin] + group * per_group
                here = lax.rem(row, owned) * columns + col
                spot = jnp.where(row // owned == replica, here, spot)
        places[step] = spot

    def first_of(step):
        spot = places[step]
        first = spot >= 0
        for earlier in range(0 if alone else step):
            first = first & (places[earlier] != spot)
        return first

    def write_of(step):
        spot = places[step]
        row, col = spot // columns, lax.rem(spot, columns)
        return pltpu.make_async_copy(
            blocks[step] if alone else staged.at[step],
            strip.at[0, 0, column(row, edge), column(col, edge)],
            sent.at[step],
        )

    for step in range(replicas):

        @pl.when(first_of(step))
        def _():
            if not alone:
                total = block_of(step)
                for later in range(step + 1, replicas):
                    meets = places[later] == places[step]
                    total = total + jnp.where(meets, block_of(later), 0.0)
                staged[step] = total.astype(staged.dtype)
            write_of(step).start()

    for step in range(replicas):

        @pl.when(first_of(step))
        def _():
            write_of(step).wait()


def body(mesh, activations, cotangent, error_tiles, tile_picks, row_owners):
    sections, replicas, groups = mesh.shape["pipe"], mesh.shape["dp"], mesh.shape["tensor"]
    edge = error_tiles.shape[-1]
    slots = tile_picks.shape[4]
    micro, tokens = activations.shape[1:3]
    width = cotangent.shape[-1] * groups
    strip_rows = row_owners.shape[-1] // replicas * edge
    mine = lax.axis_index("tensor")
    picks = jnp.transpose(tile_picks, (0, 2, 3, 4, 5, 1))

    returned = []
    for shift in range(groups):
        pairs = [
            (
                (section + 1) % sections * groups + (group + shift) % groups,
                section * groups + group,
            )
            for section in range(sections)
            for group in range(groups)
        ]
        returned.append(lax.ppermute(cotangent, ("pipe", "tensor"), pairs))
    carried = [
        lax.ppermute(
            lax.dynamic_index_in_dim(error_tiles, (mine - shift + groups) % groups, axis=3),
            "tensor",
            [((group + shift) % groups, group) for group in range(groups)],
        )
        for shift in range(1, groups)
    ]
    picked, meets = pl.pallas_call(
        pick,
        out_shape=[
            pltpu.VMEM((groups * slots, micro, tokens, edge), activations.dtype),
            jax.ShapeDtypeStruct((1,), jnp.int32),
        ],
        in_specs=[SMEM, ANY],
        out_specs=[VMEM, SMEM],
        scratch_shapes=[
            pltpu.SemaphoreType.DMA((groups * slots,)),
            pltpu.SMEM((row_owners.shape[-1] * (width // edge),), jnp.int32),
        ],
        compiler_params=SMALL,
        name="pick",
    )(picks, pltpu.with_memory_space_constraint(activations, pltpu.HBM))

    zero_rows = min(strip_rows, 256)
    strip_shape = (1, 1, strip_rows, width)
    cleared = pl.pallas_call(
        clear,
        out_shape=pltpu.HBM(strip_shape, jnp.bfloat16),
        in_specs=[ANY],
        out_specs=pl.BlockSpec(memory_space=pltpu.HBM),
        scratch_shapes=[
            pltpu.VMEM((zero_rows, width), jnp.bfloat16),
            pltpu.SemaphoreType.DMA((strip_rows // zero_rows,)),
        ],
        compiler_params=SMALL,
        cost_estimate=pl.CostEstimate(
            flops=0, bytes_accessed=2 * strip_rows * width, transcendentals=0
        ),
        name="clear",
    )(picked)

    tile_shape = (edge, edge)
    apart = replicas <= MOST_STEPS
    if apart:
        out_shape = [
            jax.ShapeDtypeStruct(tile_shape, dtype)
            for dtype in (jnp.float32, jnp.bfloat16)
            for step in range(replicas)
        ]
    else:
        out_shape = [jax.ShapeDtypeStruct((replicas,) + tile_shape, jnp.float32)]
    outgoing = pl.pallas_call(
        functools.partial(multiply, groups),
        out_shape=out_shape,
        in_specs=[SMEM, SMEM] + [VMEM] * (2 * groups + 1),
        out_specs=[VMEM] * len(out_shape),
        compiler_params=SMALL,
        name="multiply",
    )(picks, row_owners, picked, error_tiles, *returned, *carried)

    def placed(alone, incoming):
        return pl.pallas_call(
            functools.partial(place, len(incoming), alone),
            out_shape=jax.ShapeDtypeStruct(strip_shape, jnp.bfloat16),
            in_specs=[SMEM, SMEM] + [VMEM] * len(incoming) + [ANY],
            out_specs=ANY,
            scratch_shapes=[
                pltpu.VMEM((replicas,) + tile_shape, jnp.bfloat16),
                pltpu.SMEM((replicas,), jnp.int32),
                pltpu.SemaphoreType.DMA((replicas,)),
            ],
            input_output_aliases={2 + len(incoming): 0},
            compiler_params=SMALL,
            name="place",
        )(picks, row_owners, *incoming, cleared)

    def exchanged(blocks):
        blocks = list(blocks)
        for step in range(1, replicas):
            pairs = [(source, source ^ step) for source in range(replicas)]
            blocks[step] = lax.ppermute(blocks[step], "dp", pairs)
        return blocks

    if not apart:
        swapped = lax.all_to_all(outgoing[0], "dp", split_axis=0, concat_axis=0, tiled=True)
        return placed(False, [swapped])
    return lax.cond(
        meets[0] > 0,
        lambda: placed(False, exchanged(outgoing[:replicas])),
        lambda: placed(True, exchanged(outgoing[replicas:])),
    )


def solution(mesh):
    in_specs = (
        P("pipe", None, "dp", "tensor"),
        P("pipe", None, "dp", "tensor"),
        P("pipe", "dp", "tensor", None, None, None, None),
        P("pipe", None, "tensor", None, None, None),
        P("pipe", "tensor", None),
    )
    out_specs = P("pipe", "tensor", "dp", None)
    return jax.shard_map(
        functools.partial(body, mesh),
        mesh=mesh,
        in_specs=in_specs,
        out_specs=out_specs,
        check_vma=False,
    )
```

```python
import functools

import jax
import jax.numpy as jnp
from jax import lax
from jax.experimental import pallas as pl
from jax.experimental.pallas import tpu as pltpu
from jax.sharding import PartitionSpec as P

VMEM = pl.BlockSpec(memory_space=pltpu.VMEM)
SMEM = pl.BlockSpec(memory_space=pltpu.SMEM)
ANY = pl.BlockSpec(memory_space=pl.ANY)
MOST_STEPS = 8
SMALL = pltpu.CompilerParams(vmem_limit_bytes=4 << 20)


def column(index, edge):
    return pl.ds(pl.multiple_of(index * edge, edge), edge)


def pick(picks, activations, picked, meets, copied, seen):
    replica = lax.axis_index("dp")
    groups, slots, replicas = picks.shape[2], picks.shape[3], picks.shape[-1]
    edge = picked.shape[-1]
    reads = []
    for group in range(groups):
        for slot in range(slots):
            at = group * slots + slot
            block = picks[0, 0, group, slot, 0, replica]
            reads.append(
                pltpu.make_async_copy(
                    activations.at[0, :, :, column(block, edge)], picked.at[at], copied.at[at]
                )
            )
    for read in reads:
        read.start()
    meets[0] = 0
    count = groups * slots * replicas
    per_group = seen.shape[0] // (activations.shape[-1] // edge * groups)

    def spot_of(tile):
        group, slot, origin = tile // (slots * replicas), tile // replicas % slots, tile % replicas
        row, col = picks[0, 0, group, slot, 0, origin], picks[0, 0, group, slot, 1, origin]
        return (row * groups + group) * per_group + col

    def forget(tile, carry):
        seen[spot_of(tile)] = 0
        return carry

    def note(tile, carry):
        spot = spot_of(tile)
        meets[0] = meets[0] | seen[spot]
        seen[spot] = 1
        return carry

    lax.fori_loop(0, count, forget, 0, unroll=count <= 32)
    lax.fori_loop(0, count, note, 0, unroll=count <= 32)
    for read in reads:
        read.wait()


def clear(after, strip, zeros, cleared):
    zeros[...] = jnp.zeros_like(zeros)
    rows = zeros.shape[0]
    writes = [
        pltpu.make_async_copy(zeros, strip.at[0, 0, pl.ds(part * rows, rows)], cleared.at[part])
        for part in range(strip.shape[2] // rows)
    ]
    for write in writes:
        write.start()
    for write in writes:
        write.wait()


def multiply(groups, picks, owners, picked, error, *refs):
    returned, carried, outs = refs[:groups], refs[groups : 2 * groups - 1], refs[2 * groups - 1 :]
    replica, mine = lax.axis_index("dp"), lax.axis_index("tensor")
    replicas = picks.shape[-1]
    slots, edge = picks.shape[3], picked.shape[-1]
    owned = owners.shape[-1] // replicas
    tokens = picked.shape[1] * picked.shape[2]
    for shift in range(groups):
        group = lax.rem(mine + shift, groups)
        for slot in range(slots):
            row = picks[0, 0, group, slot, 0, replica]
            left = picked[group * slots + slot].reshape(tokens, edge)
            right = returned[shift][0, :, :, column(picks[0, 0, group, slot, 1, replica], edge)]
            extra = error[0, 0, 0, mine, slot] if shift == 0 else carried[shift - 1][0, 0, 0, 0, slot]
            tile = lax.dot_general(
                left,
                right.reshape(tokens, edge),
                (((0,), (0,)), ((), ())),
                preferred_element_type=jnp.float32,
            )
            tile = tile + extra.astype(jnp.float32)
            away = owners[0, 0, row] // owned
            if len(outs) > 1:
                away = lax.rem(away - replica + replicas, replicas)
            if len(outs) == 1:
                outs[0][away] = tile
            else:
                for step in range(replicas):

                    @pl.when(away == step)
                    def _():
                        outs[step][...] = tile
                        outs[replicas + step][...] = tile.astype(jnp.bfloat16)


def place(count, alone, picks, owners, *refs):
    blocks, strip, staged, places, sent = refs[:count], refs[-4], refs[-3], refs[-2], refs[-1]
    replica = lax.axis_index("dp")
    groups, slots, replicas = picks.shape[2], picks.shape[3], picks.shape[-1]
    edge = staged.shape[-1]
    owned = owners.shape[-1] // replicas
    columns = strip.shape[-1] // edge
    per_group = columns // groups

    def block_of(step):
        return blocks[0][step] if count == 1 else blocks[step][...]

    for step in range(replicas):
        origin = step if count == 1 else lax.rem(replica - step + replicas, replicas)
        spot = jnp.int32(-1)
        for group in range(groups):
            for slot in range(slots):
                row = owners[0, 0, picks[0, 0, group, slot, 0, origin]]
                col = picks[0, 0, group, slot, 1, origin] + group * per_group
                here = lax.rem(row, owned) * columns + col
                spot = jnp.where(row // owned == replica, here, spot)
        places[step] = spot

    def first_of(step):
        spot = places[step]
        first = spot >= 0
        for earlier in range(0 if alone else step):
            first = first & (places[earlier] != spot)
        return first

    def write_of(step):
        spot = places[step]
        row, col = spot // columns, lax.rem(spot, columns)
        return pltpu.make_async_copy(
            blocks[step] if alone else staged.at[step],
            strip.at[0, 0, column(row, edge), column(col, edge)],
            sent.at[step],
        )

    for step in range(replicas):

        @pl.when(first_of(step))
        def _():
            if not alone:
                total = block_of(step)
                for later in range(step + 1, replicas):
                    meets = places[later] == places[step]
                    total = total + jnp.where(meets, block_of(later), 0.0)
                staged[step] = total.astype(staged.dtype)
            write_of(step).start()

    for step in range(replicas):

        @pl.when(first_of(step))
        def _():
            write_of(step).wait()


def body(mesh, activations, cotangent, error_tiles, tile_picks, row_owners):
    sections, replicas, groups = mesh.shape["pipe"], mesh.shape["dp"], mesh.shape["tensor"]
    edge = error_tiles.shape[-1]
    slots = tile_picks.shape[4]
    micro, tokens = activations.shape[1:3]
    width = cotangent.shape[-1] * groups
    strip_rows = row_owners.shape[-1] // replicas * edge
    mine = lax.axis_index("tensor")
    picks = jnp.transpose(tile_picks, (0, 2, 3, 4, 5, 1))

    returned = []
    for shift in range(groups):
        pairs = [
            (
                (section + 1) % sections * groups + (group + shift) % groups,
                section * groups + group,
            )
            for section in range(sections)
            for group in range(groups)
        ]
        returned.append(lax.ppermute(cotangent, ("pipe", "tensor"), pairs))
    carried = [
        lax.ppermute(
            lax.dynamic_index_in_dim(error_tiles, (mine - shift + groups) % groups, axis=3),
            "tensor",
            [((group + shift) % groups, group) for group in range(groups)],
        )
        for shift in range(1, groups)
    ]
    picked, meets = pl.pallas_call(
        pick,
        out_shape=[
            pltpu.VMEM((groups * slots, micro, tokens, edge), activations.dtype),
            jax.ShapeDtypeStruct((1,), jnp.int32),
        ],
        in_specs=[SMEM, ANY],
        out_specs=[VMEM, SMEM],
        scratch_shapes=[
            pltpu.SemaphoreType.DMA((groups * slots,)),
            pltpu.SMEM((row_owners.shape[-1] * (width // edge),), jnp.int32),
        ],
        compiler_params=SMALL,
        name="pick",
    )(picks, pltpu.with_memory_space_constraint(activations, pltpu.HBM))

    zero_rows = min(strip_rows, 256)
    strip_shape = (1, 1, strip_rows, width)
    cleared = pl.pallas_call(
        clear,
        out_shape=pltpu.HBM(strip_shape, jnp.bfloat16),
        in_specs=[ANY],
        out_specs=pl.BlockSpec(memory_space=pltpu.HBM),
        scratch_shapes=[
            pltpu.VMEM((zero_rows, width), jnp.bfloat16),
            pltpu.SemaphoreType.DMA((strip_rows // zero_rows,)),
        ],
        compiler_params=SMALL,
        cost_estimate=pl.CostEstimate(
            flops=0, bytes_accessed=2 * strip_rows * width, transcendentals=0
        ),
        name="clear",
    )(picked)

    tile_shape = (edge, edge)
    apart = replicas <= MOST_STEPS
    if apart:
        out_shape = [
            jax.ShapeDtypeStruct(tile_shape, dtype)
            for dtype in (jnp.float32, jnp.bfloat16)
            for step in range(replicas)
        ]
    else:
        out_shape = [jax.ShapeDtypeStruct((replicas,) + tile_shape, jnp.float32)]
    outgoing = pl.pallas_call(
        functools.partial(multiply, groups),
        out_shape=out_shape,
        in_specs=[SMEM, SMEM] + [VMEM] * (2 * groups + 1),
        out_specs=[VMEM] * len(out_shape),
        compiler_params=SMALL,
        name="multiply",
    )(picks, row_owners, picked, error_tiles, *returned, *carried)

    def placed(alone, incoming):
        return pl.pallas_call(
            functools.partial(place, len(incoming), alone),
            out_shape=jax.ShapeDtypeStruct(strip_shape, jnp.bfloat16),
            in_specs=[SMEM, SMEM] + [VMEM] * len(incoming) + [ANY],
            out_specs=ANY,
            scratch_shapes=[
                pltpu.VMEM((replicas,) + tile_shape, jnp.bfloat16),
                pltpu.SMEM((replicas,), jnp.int32),
                pltpu.SemaphoreType.DMA((replicas,)),
            ],
            input_output_aliases={2 + len(incoming): 0},
            compiler_params=SMALL,
            name="place",
        )(picks, row_owners, *incoming, cleared)

    def exchanged(blocks):
        blocks = list(blocks)
        for step in range(1, replicas):
            pairs = [(source, (source + step) % replicas) for source in range(replicas)]
            blocks[step] = lax.ppermute(blocks[step], "dp", pairs)
        return blocks

    if not apart:
        swapped = lax.all_to_all(outgoing[0], "dp", split_axis=0, concat_axis=0, tiled=True)
        return placed(False, [swapped])
    return lax.cond(
        meets[0] > 0,
        lambda: placed(False, exchanged(outgoing[:replicas])),
        lambda: placed(True, exchanged(outgoing[replicas:])),
    )


def solution(mesh):
    in_specs = (
        P("pipe", None, "dp", "tensor"),
        P("pipe", None, "dp", "tensor"),
        P("pipe", "dp", "tensor", None, None, None, None),
        P("pipe", None, "tensor", None, None, None),
        P("pipe", "tensor", None),
    )
    out_specs = P("pipe", "tensor", "dp", None)
    return jax.shard_map(
        functools.partial(body, mesh),
        mesh=mesh,
        in_specs=in_specs,
        out_specs=out_specs,
        check_vma=False,
    )
```

```python
import functools

import jax
import jax.numpy as jnp
from jax import lax
from jax.experimental import pallas as pl
from jax.experimental.pallas import tpu as pltpu
from jax.sharding import PartitionSpec as P

VMEM = pl.BlockSpec(memory_space=pltpu.VMEM)
SMEM = pl.BlockSpec(memory_space=pltpu.SMEM)
ANY = pl.BlockSpec(memory_space=pl.ANY)
MOST_STEPS = 8
SMALL = pltpu.CompilerParams(vmem_limit_bytes=4 << 20)


def column(index, edge):
    return pl.ds(pl.multiple_of(index * edge, edge), edge)


def route_of(offset, replicas):
    far = jnp.where(offset < 0, -offset, replicas - 2 + offset)
    cyclic = (offset == 1) | (offset == 1 - replicas)
    return jnp.where(offset == 0, 0, jnp.where(cyclic, replicas - 1, far))


def routes(replicas):
    everyone = range(replicas)
    down = [[(one, one - hop) for one in everyone if one >= hop] for hop in range(1, replicas - 1)]
    up = [[(one, one + hop) for one in everyone if one + hop < replicas] for hop in range(2, replicas)]
    return down + [[(one, (one + 1) % replicas) for one in everyone]] + up


def pick(picks, activations, picked, meets, copied, seen):
    replica = lax.axis_index("dp")
    groups, slots, replicas = picks.shape[2], picks.shape[3], picks.shape[-1]
    edge = picked.shape[-1]
    reads = []
    for group in range(groups):
        for slot in range(slots):
            at = group * slots + slot
            block = picks[0, 0, group, slot, 0, replica]
            reads.append(
                pltpu.make_async_copy(
                    activations.at[0, :, :, column(block, edge)], picked.at[at], copied.at[at]
                )
            )
    for read in reads:
        read.start()
    meets[0] = 0
    count = groups * slots * replicas
    per_group = seen.shape[0] // (activations.shape[-1] // edge * groups)

    def spot_of(tile):
        group, slot, origin = tile // (slots * replicas), tile // replicas % slots, tile % replicas
        row, col = picks[0, 0, group, slot, 0, origin], picks[0, 0, group, slot, 1, origin]
        return (row * groups + group) * per_group + col

    def forget(tile, carry):
        seen[spot_of(tile)] = 0
        return carry

    def note(tile, carry):
        spot = spot_of(tile)
        meets[0] = meets[0] | seen[spot]
        seen[spot] = 1
        return carry

    lax.fori_loop(0, count, forget, 0, unroll=count <= 32)
    lax.fori_loop(0, count, note, 0, unroll=count <= 32)
    for read in reads:
        read.wait()


def clear(after, strip, zeros, cleared):
    zeros[...] = jnp.zeros_like(zeros)
    rows = zeros.shape[0]
    writes = [
        pltpu.make_async_copy(zeros, strip.at[0, 0, pl.ds(part * rows, rows)], cleared.at[part])
        for part in range(strip.shape[2] // rows)
    ]
    for write in writes:
        write.start()
    for write in writes:
        write.wait()


def multiply(groups, picks, owners, picked, error, *refs):
    returned, carried, outs = refs[:groups], refs[groups : 2 * groups - 1], refs[2 * groups - 1 :]
    replica, mine = lax.axis_index("dp"), lax.axis_index("tensor")
    replicas = picks.shape[-1]
    slots, edge = picks.shape[3], picked.shape[-1]
    owned = owners.shape[-1] // replicas
    tokens = picked.shape[1] * picked.shape[2]
    for shift in range(groups):
        group = lax.rem(mine + shift, groups)
        for slot in range(slots):
            row = picks[0, 0, group, slot, 0, replica]
            left = picked[group * slots + slot].reshape(tokens, edge)
            right = returned[shift][0, :, :, column(picks[0, 0, group, slot, 1, replica], edge)]
            extra = error[0, 0, 0, mine, slot] if shift == 0 else carried[shift - 1][0, 0, 0, 0, slot]
            tile = lax.dot_general(
                left,
                right.reshape(tokens, edge),
                (((0,), (0,)), ((), ())),
                preferred_element_type=jnp.float32,
            )
            tile = tile + extra.astype(jnp.float32)
            owner = owners[0, 0, row] // owned
            if len(outs) == 1:
                outs[0][owner] = tile
            else:
                outs[0][group * slots + slot] = tile
                store(tile.astype(jnp.bfloat16), owner - replica, replicas, outs[1:])


def store(tile, offset, replicas, buffers):
    route = route_of(offset, replicas)
    for at, buffer in enumerate(buffers):

        @pl.when(route == at)
        def _():
            buffer[...] = tile


def spread(picks, owners, tiles, *buffers):
    replica = lax.axis_index("dp")
    groups, slots, replicas = picks.shape[2], picks.shape[3], picks.shape[-1]
    owned = owners.shape[-1] // replicas
    for group in range(groups):
        for slot in range(slots):
            owner = owners[0, 0, picks[0, 0, group, slot, 0, replica]] // owned
            store(tiles[group * slots + slot], owner - replica, replicas, buffers)


def place(count, alone, picks, owners, *refs):
    blocks, strip, staged, places, sent = refs[:count], refs[-4], refs[-3], refs[-2], refs[-1]
    replica = lax.axis_index("dp")
    groups, slots, replicas = picks.shape[2], picks.shape[3], picks.shape[-1]
    edge = staged.shape[-1]
    owned = owners.shape[-1] // replicas
    columns = strip.shape[-1] // edge
    per_group = columns // groups

    def block_of(step):
        return blocks[0][step] if count == 1 else blocks[step][...]

    steps = replicas if count == 1 else count
    for step in range(steps):
        places[step] = jnp.int32(-1)
    for origin in range(replicas):
        spot = jnp.int32(-1)
        for group in range(groups):
            for slot in range(slots):
                row = owners[0, 0, picks[0, 0, group, slot, 0, origin]]
                col = picks[0, 0, group, slot, 1, origin] + group * per_group
                here = lax.rem(row, owned) * columns + col
                spot = jnp.where(row // owned == replica, here, spot)
        places[origin if count == 1 else route_of(replica - origin, replicas)] = spot

    def first_of(step):
        spot = places[step]
        first = spot >= 0
        for earlier in range(0 if alone else step):
            first = first & (places[earlier] != spot)
        return first

    def write_of(step):
        spot = places[step]
        row, col = spot // columns, lax.rem(spot, columns)
        return pltpu.make_async_copy(
            blocks[step] if alone else staged.at[step],
            strip.at[0, 0, column(row, edge), column(col, edge)],
            sent.at[step],
        )

    for step in range(steps):

        @pl.when(first_of(step))
        def _():
            if not alone:
                total = block_of(step)
                for later in range(step + 1, steps):
                    meets = places[later] == places[step]
                    total = total + jnp.where(meets, block_of(later), 0.0)
                staged[step] = total.astype(staged.dtype)
            write_of(step).start()

    for step in range(steps):

        @pl.when(first_of(step))
        def _():
            write_of(step).wait()


def body(mesh, activations, cotangent, error_tiles, tile_picks, row_owners):
    sections, replicas, groups = mesh.shape["pipe"], mesh.shape["dp"], mesh.shape["tensor"]
    edge = error_tiles.shape[-1]
    slots = tile_picks.shape[4]
    micro, tokens = activations.shape[1:3]
    width = cotangent.shape[-1] * groups
    strip_rows = row_owners.shape[-1] // replicas * edge
    mine = lax.axis_index("tensor")
    picks = jnp.transpose(tile_picks, (0, 2, 3, 4, 5, 1))

    returned = []
    for shift in range(groups):
        pairs = [
            (
                (section + 1) % sections * groups + (group + shift) % groups,
                section * groups + group,
            )
            for section in range(sections)
            for group in range(groups)
        ]
        returned.append(lax.ppermute(cotangent, ("pipe", "tensor"), pairs))
    carried = [
        lax.ppermute(
            lax.dynamic_index_in_dim(error_tiles, (mine - shift + groups) % groups, axis=3),
            "tensor",
            [((group + shift) % groups, group) for group in range(groups)],
        )
        for shift in range(1, groups)
    ]
    picked, meets = pl.pallas_call(
        pick,
        out_shape=[
            pltpu.VMEM((groups * slots, micro, tokens, edge), activations.dtype),
            jax.ShapeDtypeStruct((1,), jnp.int32),
        ],
        in_specs=[SMEM, ANY],
        out_specs=[VMEM, SMEM],
        scratch_shapes=[
            pltpu.SemaphoreType.DMA((groups * slots,)),
            pltpu.SMEM((row_owners.shape[-1] * (width // edge),), jnp.int32),
        ],
        compiler_params=SMALL,
        name="pick",
    )(picks, pltpu.with_memory_space_constraint(activations, pltpu.HBM))

    zero_rows = min(strip_rows, 256)
    strip_shape = (1, 1, strip_rows, width)
    cleared = pl.pallas_call(
        clear,
        out_shape=pltpu.HBM(strip_shape, jnp.bfloat16),
        in_specs=[ANY],
        out_specs=pl.BlockSpec(memory_space=pltpu.HBM),
        scratch_shapes=[
            pltpu.VMEM((zero_rows, width), jnp.bfloat16),
            pltpu.SemaphoreType.DMA((strip_rows // zero_rows,)),
        ],
        compiler_params=SMALL,
        cost_estimate=pl.CostEstimate(
            flops=0, bytes_accessed=2 * strip_rows * width, transcendentals=0
        ),
        name="clear",
    )(picked)

    tile_shape = (edge, edge)
    apart = replicas <= MOST_STEPS
    buffers = max(1, 2 * replicas - 2)
    if apart:
        out_shape = [jax.ShapeDtypeStruct((groups * slots,) + tile_shape, jnp.float32)]
        out_shape += [jax.ShapeDtypeStruct(tile_shape, jnp.bfloat16)] * buffers
    else:
        out_shape = [jax.ShapeDtypeStruct((replicas,) + tile_shape, jnp.float32)]
    outgoing = pl.pallas_call(
        functools.partial(multiply, groups),
        out_shape=out_shape,
        in_specs=[SMEM, SMEM] + [VMEM] * (2 * groups + 1),
        out_specs=[VMEM] * len(out_shape),
        compiler_params=SMALL,
        name="multiply",
    )(picks, row_owners, picked, error_tiles, *returned, *carried)

    steps = buffers if apart else replicas

    def placed(alone, incoming):
        return pl.pallas_call(
            functools.partial(place, len(incoming), alone),
            out_shape=jax.ShapeDtypeStruct(strip_shape, jnp.bfloat16),
            in_specs=[SMEM, SMEM] + [VMEM] * len(incoming) + [ANY],
            out_specs=ANY,
            scratch_shapes=[
                pltpu.VMEM((steps,) + tile_shape, jnp.bfloat16),
                pltpu.SMEM((steps,), jnp.int32),
                pltpu.SemaphoreType.DMA((steps,)),
            ],
            input_output_aliases={2 + len(incoming): 0},
            compiler_params=SMALL,
            name="place",
        )(picks, row_owners, *incoming, cleared)

    def exchanged(blocks):
        moved = [
            lax.ppermute(block, "dp", pairs) for block, pairs in zip(blocks[1:], routes(replicas))
        ]
        return [blocks[0], *moved]

    def in_full():
        blocks = pl.pallas_call(
            spread,
            out_shape=[jax.ShapeDtypeStruct(tile_shape, jnp.float32)] * buffers,
            in_specs=[SMEM, SMEM, VMEM],
            out_specs=[VMEM] * buffers,
            compiler_params=SMALL,
            name="spread",
        )(picks, row_owners, outgoing[0])
        return placed(False, exchanged(blocks))

    if not apart:
        swapped = lax.all_to_all(outgoing[0], "dp", split_axis=0, concat_axis=0, tiled=True)
        return placed(False, [swapped])
    return lax.cond(
        meets[0] > 0,
        in_full,
        lambda: placed(True, exchanged(outgoing[1:])),
    )


def solution(mesh):
    in_specs = (
        P("pipe", None, "dp", "tensor"),
        P("pipe", None, "dp", "tensor"),
        P("pipe", "dp", "tensor", None, None, None, None),
        P("pipe", None, "tensor", None, None, None),
        P("pipe", "tensor", None),
    )
    out_specs = P("pipe", "tensor", "dp", None)
    return jax.shard_map(
        functools.partial(body, mesh),
        mesh=mesh,
        in_specs=in_specs,
        out_specs=out_specs,
        check_vma=False,
    )
```

```python
import functools

import jax
import jax.numpy as jnp
from jax import lax
from jax.experimental import pallas as pl
from jax.experimental.pallas import tpu as pltpu
from jax.sharding import PartitionSpec as P

VMEM = pl.BlockSpec(memory_space=pltpu.VMEM)
SMEM = pl.BlockSpec(memory_space=pltpu.SMEM)
ANY = pl.BlockSpec(memory_space=pl.ANY)
MOST_STEPS = 8
SMALL = pltpu.CompilerParams(vmem_limit_bytes=4 << 20)
ROUNDS = {4: [(1, 2, 0, 3), (2, 1, 3, 0), (3, 0, 1, 2), (0, 3, 2, 1)]}


def column(index, edge):
    return pl.ds(pl.multiple_of(index * edge, edge), edge)


def rounds(replicas):
    shifts = [
        tuple((one + step) % replicas for one in range(replicas)) for step in range(1, replicas)
    ]
    return ROUNDS.get(replicas, shifts)


def buffers_of(replicas):
    rows = []
    for source in range(replicas):
        at = [0] * replicas
        for number, targets in enumerate(rounds(replicas)):
            if targets[source] != source:
                at[targets[source]] = number + 1
        rows.append(sum(number << 4 * target for target, number in enumerate(at)))
    return rows


def plan_sizes(picks, apart):
    replicas, tiles = picks.shape[-1], picks.shape[2] * picks.shape[3]
    steps = len(rounds(replicas)) + 1 if apart else replicas
    return 1, 1 + tiles, 1 + 2 * tiles, 1 + 2 * tiles + steps


def pick(picks, activations, picked, read, copied):
    replica = lax.axis_index("dp")
    groups, slots, edge = picks.shape[2], picks.shape[3], picked.shape[1]
    reads = []
    for group in range(groups):
        for slot in range(slots):
            at = group * slots + slot
            block = picks[0, 0, group, slot, 0, replica]
            reads.append(
                pltpu.make_async_copy(
                    activations.at[0, :, :, column(block, edge)], read.at[at], copied.at[at]
                )
            )
    for copy in reads:
        copy.start()
    for at, copy in enumerate(reads):
        copy.wait()
        picked[at] = read[at].reshape(-1, edge).T


def clear(apart, picks, owners, after, strip, plan, zeros, seen, cleared):
    zeros[...] = jnp.zeros_like(zeros)
    rows, edge = zeros.shape[0], after.shape[1]
    writes = [
        pltpu.make_async_copy(zeros, strip.at[0, 0, pl.ds(part * rows, rows)], cleared.at[part])
        for part in range(strip.shape[2] // rows)
    ]
    for write in writes:
        write.start()

    replica = lax.axis_index("dp")
    groups, slots, replicas = picks.shape[2], picks.shape[3], picks.shape[-1]
    tiles = [(group, slot) for group in range(groups) for slot in range(slots)]
    owned = owners.shape[-1] // replicas
    columns = strip.shape[-1] // edge
    per_group = columns // groups
    to_buffer, to_column, to_place, end = plan_sizes(picks, apart)
    table = buffers_of(replicas) if apart else None
    for at in range(to_place, end):
        plan[at] = -1

    for at, (group, slot) in enumerate(tiles):
        owner = owners[0, 0, picks[0, 0, group, slot, 0, replica]] // owned
        if apart:
            mine = jnp.int32(table[0])
            for source in range(1, replicas):
                mine = jnp.where(replica == source, table[source], mine)
            owner = lax.shift_right_logical(mine, 4 * owner) & 15
        plan[to_buffer + at] = owner
        plan[to_column + at] = picks[0, 0, group, slot, 1, replica]

    for origin in range(replicas):
        spot = jnp.int32(-1)
        for group, slot in tiles:
            row = owners[0, 0, picks[0, 0, group, slot, 0, origin]]
            col = picks[0, 0, group, slot, 1, origin] + group * per_group
            here = lax.rem(row, owned) * columns + col
            spot = jnp.where(row // owned == replica, here, spot)
        at = lax.shift_right_logical(jnp.int32(table[origin]), 4 * replica) & 15 if apart else origin
        plan[to_place + at] = spot

    plan[0] = 0
    if apart:
        spots = [
            picks[0, 0, group, slot, 0, origin] * columns
            + picks[0, 0, group, slot, 1, origin]
            + group * per_group
            for group, slot in tiles
            for origin in range(replicas)
        ]
        for spot in spots:
            seen[spot] = 0
        for spot in spots:
            plan[0] = plan[0] | seen[spot]
            seen[spot] = 1
    for write in writes:
        write.wait()


def multiply(groups, apart, to_buffer, to_column, plan, picked, error, *refs):
    returned, carried, outs = refs[:groups], refs[groups : 2 * groups - 1], refs[2 * groups - 1 :]
    mine = lax.axis_index("tensor")
    slots, (edge, tokens) = error.shape[4], picked.shape[1:]
    for shift in range(groups):
        group = lax.rem(mine + shift, groups)
        for slot in range(slots):
            at = group * slots + slot
            right = returned[shift][0, :, :, column(plan[to_column + at], edge)]
            extra = error[0, 0, 0, mine, slot] if shift == 0 else carried[shift - 1][0, 0, 0, 0, slot]
            tile = jnp.dot(
                picked[at], right.reshape(tokens, edge), preferred_element_type=jnp.float32
            )
            tile = tile + extra.astype(jnp.float32)
            buffer = plan[to_buffer + at]
            if apart:
                outs[0][at] = tile
                store(tile.astype(jnp.bfloat16), buffer, outs[1:])
            else:
                outs[0][buffer] = tile


def store(tile, buffer, buffers):
    for at, out in enumerate(buffers):

        @pl.when(buffer == at)
        def _():
            out[...] = tile


def spread(to_buffer, plan, tiles, *buffers):
    for at in range(tiles.shape[0]):
        store(tiles[at], plan[to_buffer + at], buffers)


def place(count, alone, to_place, plan, *refs):
    blocks, strip, staged, sent = refs[:count], refs[-3], refs[-2], refs[-1]
    steps, edge = staged.shape[0], staged.shape[-1]
    columns = strip.shape[-1] // edge

    def block_of(step):
        return blocks[0][step] if count == 1 else blocks[step][...]

    def first_of(step):
        spot = plan[to_place + step]
        first = spot >= 0
        for earlier in range(0 if alone else step):
            first = first & (plan[to_place + earlier] != spot)
        return first

    def write_of(step):
        spot = plan[to_place + step]
        row, col = spot // columns, lax.rem(spot, columns)
        return pltpu.make_async_copy(
            blocks[step] if alone else staged.at[step],
            strip.at[0, 0, column(row, edge), column(col, edge)],
            sent.at[step],
        )

    for step in range(steps):

        @pl.when(first_of(step))
        def _():
            if not alone:
                total = block_of(step)
                for later in range(step + 1, steps):
                    meets = plan[to_place + later] == plan[to_place + step]
                    total = total + jnp.where(meets, block_of(later), 0.0)
                staged[step] = total.astype(staged.dtype)
            write_of(step).start()

    for step in range(steps):

        @pl.when(first_of(step))
        def _():
            write_of(step).wait()


def body(mesh, activations, cotangent, error_tiles, tile_picks, row_owners):
    sections, replicas, groups = mesh.shape["pipe"], mesh.shape["dp"], mesh.shape["tensor"]
    edge = error_tiles.shape[-1]
    slots = tile_picks.shape[4]
    micro, tokens = activations.shape[1:3]
    width = cotangent.shape[-1] * groups
    strip_rows = row_owners.shape[-1] // replicas * edge
    mine = lax.axis_index("tensor")
    picks = jnp.transpose(tile_picks, (0, 2, 3, 4, 5, 1))

    returned = []
    for shift in range(groups):
        pairs = [
            (
                (section + 1) % sections * groups + (group + shift) % groups,
                section * groups + group,
            )
            for section in range(sections)
            for group in range(groups)
        ]
        returned.append(lax.ppermute(cotangent, ("pipe", "tensor"), pairs))
    carried = [
        lax.ppermute(
            lax.dynamic_index_in_dim(error_tiles, (mine - shift + groups) % groups, axis=3),
            "tensor",
            [((group + shift) % groups, group) for group in range(groups)],
        )
        for shift in range(1, groups)
    ]
    apart = replicas <= MOST_STEPS
    tiles = groups * slots
    picked = pl.pallas_call(
        pick,
        out_shape=pltpu.VMEM((tiles, edge, micro * tokens), activations.dtype),
        in_specs=[SMEM, ANY],
        out_specs=VMEM,
        scratch_shapes=[
            pltpu.VMEM((tiles, micro, tokens, edge), activations.dtype),
            pltpu.SemaphoreType.DMA((tiles,)),
        ],
        compiler_params=SMALL,
        name="pick",
    )(picks, pltpu.with_memory_space_constraint(activations, pltpu.HBM))

    zero_rows = min(strip_rows, 256)
    strip_shape = (1, 1, strip_rows, width)
    to_buffer, to_column, to_place, planned = plan_sizes(picks, apart)
    cleared, plan = pl.pallas_call(
        functools.partial(clear, apart),
        out_shape=[
            pltpu.HBM(strip_shape, jnp.bfloat16),
            jax.ShapeDtypeStruct((planned,), jnp.int32),
        ],
        in_specs=[SMEM, SMEM, ANY],
        out_specs=[pl.BlockSpec(memory_space=pltpu.HBM), SMEM],
        scratch_shapes=[
            pltpu.VMEM((zero_rows, width), jnp.bfloat16),
            pltpu.SMEM((row_owners.shape[-1] * (width // edge),), jnp.int32),
            pltpu.SemaphoreType.DMA((strip_rows // zero_rows,)),
        ],
        compiler_params=SMALL,
        cost_estimate=pl.CostEstimate(
            flops=0, bytes_accessed=2 * strip_rows * width, transcendentals=0
        ),
        name="clear",
    )(picks, row_owners, picked)

    tile_shape = (edge, edge)
    steps = planned - to_place
    if apart:
        out_shape = [jax.ShapeDtypeStruct((tiles,) + tile_shape, jnp.float32)]
        out_shape += [jax.ShapeDtypeStruct(tile_shape, jnp.bfloat16)] * steps
    else:
        out_shape = [jax.ShapeDtypeStruct((replicas,) + tile_shape, jnp.float32)]
    outgoing = pl.pallas_call(
        functools.partial(multiply, groups, apart, to_buffer, to_column),
        out_shape=out_shape,
        in_specs=[SMEM] + [VMEM] * (2 * groups + 1),
        out_specs=[VMEM] * len(out_shape),
        compiler_params=SMALL,
        name="multiply",
    )(plan, picked, error_tiles, *returned, *carried)

    def placed(alone, incoming):
        return pl.pallas_call(
            functools.partial(place, len(incoming), alone, to_place),
            out_shape=jax.ShapeDtypeStruct(strip_shape, jnp.bfloat16),
            in_specs=[SMEM] + [VMEM] * len(incoming) + [ANY],
            out_specs=ANY,
            scratch_shapes=[
                pltpu.VMEM((steps,) + tile_shape, jnp.bfloat16),
                pltpu.SemaphoreType.DMA((steps,)),
            ],
            input_output_aliases={1 + len(incoming): 0},
            compiler_params=SMALL,
            name="place",
        )(plan, *incoming, cleared)

    def exchanged(blocks):
        moved = [
            lax.ppermute(block, "dp", list(enumerate(targets)))
            for block, targets in zip(blocks[1:], rounds(replicas))
        ]
        return [blocks[0], *moved]

    def in_full():
        blocks = pl.pallas_call(
            functools.partial(spread, to_buffer),
            out_shape=[jax.ShapeDtypeStruct(tile_shape, jnp.float32)] * steps,
            in_specs=[SMEM, VMEM],
            out_specs=[VMEM] * steps,
            compiler_params=SMALL,
            name="spread",
        )(plan, outgoing[0])
        return placed(False, exchanged(blocks))

    if not apart:
        swapped = lax.all_to_all(outgoing[0], "dp", split_axis=0, concat_axis=0, tiled=True)
        return placed(False, [swapped])
    return lax.cond(plan[0] > 0, in_full, lambda: placed(True, exchanged(outgoing[1:])))


def solution(mesh):
    in_specs = (
        P("pipe", None, "dp", "tensor"),
        P("pipe", None, "dp", "tensor"),
        P("pipe", "dp", "tensor", None, None, None, None),
        P("pipe", None, "tensor", None, None, None),
        P("pipe", "tensor", None),
    )
    out_specs = P("pipe", "tensor", "dp", None)
    return jax.shard_map(
        functools.partial(body, mesh),
        mesh=mesh,
        in_specs=in_specs,
        out_specs=out_specs,
        check_vma=False,
    )
```

```python
import functools

import jax
import jax.numpy as jnp
from jax import lax
from jax.experimental import pallas as pl
from jax.experimental.pallas import tpu as pltpu
from jax.sharding import PartitionSpec as P

VMEM = pl.BlockSpec(memory_space=pltpu.VMEM)
SMEM = pl.BlockSpec(memory_space=pltpu.SMEM)
ANY = pl.BlockSpec(memory_space=pl.ANY)
MOST_STEPS = 8
SMALL = pltpu.CompilerParams(vmem_limit_bytes=4 << 20)


def column(index, edge):
    return pl.ds(pl.multiple_of(index * edge, edge), edge)


def plan_sizes(tiles, steps):
    return 1, 1 + tiles, 1 + 2 * tiles, 1 + 2 * tiles + steps, 1 + 2 * tiles + 2 * steps


def pick(shifts, picks, activations, errors, picked, *refs):
    cuts, read, copied = refs[:shifts], refs[-2], refs[-1]
    replica, mine = lax.axis_index("dp"), lax.axis_index("tensor")
    groups, slots, edge = picks.shape[2], picks.shape[3], picked.shape[1]
    reads = []
    for group in range(groups):
        for slot in range(slots):
            at = group * slots + slot
            block = picks[0, 0, group, slot, 0, replica]
            reads.append(
                pltpu.make_async_copy(
                    activations.at[0, :, :, column(block, edge)], read.at[at], copied.at[at]
                )
            )
    for shift, cut in enumerate(cuts):
        other = lax.rem(mine + groups - shift - 1, groups)
        reads.append(
            pltpu.make_async_copy(errors.at[0, 0, 0, other], cut, copied.at[groups * slots + shift])
        )
    for copy in reads:
        copy.start()
    for at, copy in enumerate(reads):
        copy.wait()
        if at < groups * slots:
            picked[at] = read[at].reshape(-1, edge).T


def clear(apart, picks, owners, after, strip, plan, zeros, seen, cleared):
    zeros[...] = jnp.zeros_like(zeros)
    rows, edge = zeros.shape[0], after.shape[1]
    writes = [
        pltpu.make_async_copy(zeros, strip.at[0, 0, pl.ds(part * rows, rows)], cleared.at[part])
        for part in range(strip.shape[2] // rows)
    ]
    for write in writes:
        write.start()

    replica = lax.axis_index("dp")
    groups, slots, replicas = picks.shape[2], picks.shape[3], picks.shape[-1]
    tiles = [(group, slot) for group in range(groups) for slot in range(slots)]
    owned = owners.shape[-1] // replicas
    columns = strip.shape[-1] // edge
    per_group = columns // groups
    to_step, to_column, to_row, to_col, _ = plan_sizes(len(tiles), replicas)

    def step_from(source, target):
        ahead = target - source
        return jnp.where(ahead < 0, ahead + replicas, ahead) if apart else target

    for at, (group, slot) in enumerate(tiles):
        row = owners[0, 0, picks[0, 0, group, slot, 0, replica]]
        owner = jnp.int32(0)
        for one in range(1, replicas):
            owner += (row >= one * owned).astype(jnp.int32)
        plan[to_step + at] = step_from(replica, owner)
        plan[to_column + at] = picks[0, 0, group, slot, 1, replica]

    for origin in range(replicas):
        place_row, place_col = jnp.int32(-1), jnp.int32(0)
        for group, slot in tiles:
            row = owners[0, 0, picks[0, 0, group, slot, 0, origin]] - replica * owned
            here = (row >= 0) & (row < owned)
            place_row = jnp.where(here, row, place_row)
            place_col = jnp.where(
                here, picks[0, 0, group, slot, 1, origin] + group * per_group, place_col
            )
        step = step_from(origin, replica) if apart else origin
        plan[to_row + step] = place_row
        plan[to_col + step] = place_col

    meets = jnp.int32(0)
    if apart:
        spots = [
            picks[0, 0, group, slot, 0, origin] * columns
            + picks[0, 0, group, slot, 1, origin]
            + group * per_group
            for group, slot in tiles
            for origin in range(replicas)
        ]
        for spot in spots:
            seen[spot] = 0
        for spot in spots:
            meets = meets | seen[spot]
            seen[spot] = 1
    plan[0] = meets
    for write in writes:
        write.wait()


def multiply(groups, apart, to_step, to_column, plan, picked, error, *refs):
    returned, carried, outs = refs[:groups], refs[groups : 2 * groups - 1], refs[2 * groups - 1 :]
    mine = lax.axis_index("tensor")
    slots, (edge, tokens) = error.shape[4], picked.shape[1:]
    for shift in range(groups):
        group = lax.rem(mine + shift, groups)
        for slot in range(slots):
            at = group * slots + slot
            right = returned[shift][0, :, :, column(plan[to_column + at], edge)]
            extra = error[0, 0, 0, mine, slot] if shift == 0 else carried[shift - 1][slot]
            tile = jnp.dot(
                picked[at], right.reshape(tokens, edge), preferred_element_type=jnp.float32
            )
            tile = tile + extra.astype(jnp.float32)
            step = plan[to_step + at]
            if apart:
                outs[0][at] = tile
                store(tile.astype(jnp.bfloat16), step, outs[1:])
            else:
                outs[0][step] = tile


def store(tile, step, buffers):
    for at, buffer in enumerate(buffers):

        @pl.when(step == at)
        def _():
            buffer[...] = tile


def spread(to_step, plan, tiles, *buffers):
    for at in range(tiles.shape[0]):
        store(tiles[at], plan[to_step + at], buffers)


def place(count, alone, to_row, to_col, plan, *refs):
    blocks, strip, staged, sent = refs[:count], refs[-3], refs[-2], refs[-1]
    steps, edge = staged.shape[0], staged.shape[-1]

    def meets(one, other):
        return (plan[to_row + one] == plan[to_row + other]) & (
            plan[to_col + one] == plan[to_col + other]
        )

    def block_of(step):
        return blocks[0][step] if count == 1 else blocks[step][...]

    def first_of(step):
        first = plan[to_row + step] >= 0
        for earlier in range(0 if alone else step):
            first = first & jnp.logical_not(meets(earlier, step))
        return first

    def write_of(step):
        row, col = plan[to_row + step], plan[to_col + step]
        return pltpu.make_async_copy(
            blocks[step] if alone else staged.at[step],
            strip.at[0, 0, column(row, edge), column(col, edge)],
            sent.at[step],
        )

    for step in range(steps):

        @pl.when(first_of(step))
        def _():
            if not alone:
                total = block_of(step)
                for later in range(step + 1, steps):
                    total = total + jnp.where(meets(step, later), block_of(later), 0.0)
                staged[step] = total.astype(staged.dtype)
            write_of(step).start()

    for step in range(steps):

        @pl.when(first_of(step))
        def _():
            write_of(step).wait()


def body(mesh, activations, cotangent, error_tiles, tile_picks, row_owners):
    sections, replicas, groups = mesh.shape["pipe"], mesh.shape["dp"], mesh.shape["tensor"]
    edge = error_tiles.shape[-1]
    slots = tile_picks.shape[4]
    micro, tokens = activations.shape[1:3]
    width = cotangent.shape[-1] * groups
    strip_rows = row_owners.shape[-1] // replicas * edge
    picks = jnp.transpose(tile_picks, (0, 2, 3, 4, 5, 1))

    returned = []
    for shift in range(groups):
        pairs = [
            (
                (section + 1) % sections * groups + (group + shift) % groups,
                section * groups + group,
            )
            for section in range(sections)
            for group in range(groups)
        ]
        returned.append(lax.ppermute(cotangent, ("pipe", "tensor"), pairs))
    apart = replicas <= MOST_STEPS
    tiles = groups * slots
    picked, *cuts = pl.pallas_call(
        functools.partial(pick, groups - 1),
        out_shape=[pltpu.VMEM((tiles, edge, micro * tokens), activations.dtype)]
        + [pltpu.VMEM((slots, edge, edge), error_tiles.dtype)] * (groups - 1),
        in_specs=[SMEM, ANY, ANY],
        out_specs=[VMEM] * groups,
        scratch_shapes=[
            pltpu.VMEM((tiles, micro, tokens, edge), activations.dtype),
            pltpu.SemaphoreType.DMA((tiles + groups - 1,)),
        ],
        compiler_params=SMALL,
        name="pick",
    )(picks, pltpu.with_memory_space_constraint(activations, pltpu.HBM), error_tiles)
    carried = [
        lax.ppermute(
            cut, "tensor", [((group + shift + 1) % groups, group) for group in range(groups)]
        )
        for shift, cut in enumerate(cuts)
    ]

    zero_rows = min(strip_rows, 256)
    strip_shape = (1, 1, strip_rows, width)
    to_step, to_column, to_row, to_col, planned = plan_sizes(tiles, replicas)
    cleared, plan = pl.pallas_call(
        functools.partial(clear, apart),
        out_shape=[
            pltpu.HBM(strip_shape, jnp.bfloat16),
            jax.ShapeDtypeStruct((planned,), jnp.int32),
        ],
        in_specs=[SMEM, SMEM, ANY],
        out_specs=[pl.BlockSpec(memory_space=pltpu.HBM), SMEM],
        scratch_shapes=[
            pltpu.VMEM((zero_rows, width), jnp.bfloat16),
            pltpu.SMEM((row_owners.shape[-1] * (width // edge),), jnp.int32),
            pltpu.SemaphoreType.DMA((strip_rows // zero_rows,)),
        ],
        compiler_params=SMALL,
        cost_estimate=pl.CostEstimate(
            flops=0, bytes_accessed=2 * strip_rows * width, transcendentals=0
        ),
        name="clear",
    )(picks, row_owners, picked)

    tile_shape = (edge, edge)
    if apart:
        out_shape = [jax.ShapeDtypeStruct((tiles,) + tile_shape, jnp.float32)]
        out_shape += [jax.ShapeDtypeStruct(tile_shape, jnp.bfloat16)] * replicas
    else:
        out_shape = [jax.ShapeDtypeStruct((replicas,) + tile_shape, jnp.float32)]
    outgoing = pl.pallas_call(
        functools.partial(multiply, groups, apart, to_step, to_column),
        out_shape=out_shape,
        in_specs=[SMEM] + [VMEM] * (2 * groups + 1),
        out_specs=[VMEM] * len(out_shape),
        compiler_params=SMALL,
        name="multiply",
    )(plan, picked, error_tiles, *returned, *carried)

    def placed(alone, incoming):
        return pl.pallas_call(
            functools.partial(place, len(incoming), alone, to_row, to_col),
            out_shape=jax.ShapeDtypeStruct(strip_shape, jnp.bfloat16),
            in_specs=[SMEM] + [VMEM] * len(incoming) + [ANY],
            out_specs=ANY,
            scratch_shapes=[
                pltpu.VMEM((replicas,) + tile_shape, jnp.bfloat16),
                pltpu.SemaphoreType.DMA((replicas,)),
            ],
            input_output_aliases={1 + len(incoming): 0},
            compiler_params=SMALL,
            name="place",
        )(plan, *incoming, cleared)

    def exchanged(blocks):
        moved = [
            lax.ppermute(
                blocks[step], "dp", [(one, (one + step) % replicas) for one in range(replicas)]
            )
            for step in range(1, replicas)
        ]
        return [blocks[0], *moved]

    def in_full():
        blocks = pl.pallas_call(
            functools.partial(spread, to_step),
            out_shape=[jax.ShapeDtypeStruct(tile_shape, jnp.float32)] * replicas,
            in_specs=[SMEM, VMEM],
            out_specs=[VMEM] * replicas,
            compiler_params=SMALL,
            name="spread",
        )(plan, outgoing[0])
        return placed(False, exchanged(blocks))

    if not apart:
        swapped = lax.all_to_all(outgoing[0], "dp", split_axis=0, concat_axis=0, tiled=True)
        return placed(False, [swapped])
    return lax.cond(plan[0] > 0, in_full, lambda: placed(True, exchanged(outgoing[1:])))


def solution(mesh):
    in_specs = (
        P("pipe", None, "dp", "tensor"),
        P("pipe", None, "dp", "tensor"),
        P("pipe", "dp", "tensor", None, None, None, None),
        P("pipe", None, "tensor", None, None, None),
        P("pipe", "tensor", None),
    )
    out_specs = P("pipe", "tensor", "dp", None)
    return jax.shard_map(
        functools.partial(body, mesh),
        mesh=mesh,
        in_specs=in_specs,
        out_specs=out_specs,
        check_vma=False,
    )
```

```python
import functools

import jax
import jax.numpy as jnp
from jax import lax
from jax.experimental import pallas as pl
from jax.experimental.pallas import tpu as pltpu
from jax.sharding import PartitionSpec as P

VMEM = pl.BlockSpec(memory_space=pltpu.VMEM)
SMEM = pl.BlockSpec(memory_space=pltpu.SMEM)
ANY = pl.BlockSpec(memory_space=pl.ANY)
MOST_STEPS = 8
SMALL = pltpu.CompilerParams(vmem_limit_bytes=4 << 20)
EARLY = pl.CostEstimate(flops=10**11, bytes_accessed=0, transcendentals=0)


def in_hbm(value):
    return pltpu.with_memory_space_constraint(value, pltpu.HBM)


def column(index, edge):
    return pl.ds(pl.multiple_of(index * edge, edge), edge)


def plan_sizes(tiles, steps):
    return 1, 1 + tiles, 1 + 2 * tiles, 1 + 2 * tiles + steps, 1 + 2 * tiles + 2 * steps


def pick(apart, columns, picks, owners, activations, after, picked, plan, read, seen, copied):
    replica = lax.axis_index("dp")
    groups, slots, replicas = picks.shape[2], picks.shape[3], picks.shape[-1]
    edge = picked.shape[1]
    tiles = [(group, slot) for group in range(groups) for slot in range(slots)]
    reads = []
    for at, (group, slot) in enumerate(tiles):
        block = picks[0, 0, group, slot, 0, replica]
        reads.append(
            pltpu.make_async_copy(
                activations.at[0, :, :, column(block, edge)], read.at[at], copied.at[at]
            )
        )
    for copy in reads:
        copy.start()

    owned = owners.shape[-1] // replicas
    per_group = columns // groups
    to_step, to_column, to_row, to_col, _ = plan_sizes(len(tiles), replicas)

    def step_from(source, target):
        ahead = target - source
        return jnp.where(ahead < 0, ahead + replicas, ahead) if apart else target

    for at, (group, slot) in enumerate(tiles):
        row = owners[0, 0, picks[0, 0, group, slot, 0, replica]]
        owner = jnp.int32(0)
        for one in range(1, replicas):
            owner += (row >= one * owned).astype(jnp.int32)
        plan[to_step + at] = step_from(replica, owner)
        plan[to_column + at] = picks[0, 0, group, slot, 1, replica]

    for origin in range(replicas):
        place_row, place_col = jnp.int32(-1), jnp.int32(0)
        for group, slot in tiles:
            row = owners[0, 0, picks[0, 0, group, slot, 0, origin]] - replica * owned
            here = (row >= 0) & (row < owned)
            place_row = jnp.where(here, row, place_row)
            place_col = jnp.where(
                here, picks[0, 0, group, slot, 1, origin] + group * per_group, place_col
            )
        step = step_from(origin, replica) if apart else origin
        plan[to_row + step] = place_row
        plan[to_col + step] = place_col

    meets = jnp.int32(0)
    if apart:
        spots = [
            picks[0, 0, group, slot, 0, origin] * columns
            + picks[0, 0, group, slot, 1, origin]
            + group * per_group
            for group, slot in tiles
            for origin in range(replicas)
        ]
        for spot in spots:
            seen[spot] = 0
        for spot in spots:
            meets = meets | seen[spot]
            seen[spot] = 1
    plan[0] = meets

    for at, copy in enumerate(reads):
        copy.wait()
        picked[at] = read[at].reshape(-1, edge).T


def cut_out(shifts, *refs):
    asked, (cotangent, errors), outs, copied = refs[:shifts], refs[shifts : shifts + 2], refs[shifts + 2 : -1], refs[-1]
    replica, mine = lax.axis_index("dp"), lax.axis_index("tensor")
    groups, slots, rest, edge = shifts + 1, outs[0].shape[0], outs[0].shape[1], outs[0].shape[-1]
    whole = cotangent.shape[1] - rest
    copies = []
    for shift, wanted in enumerate(asked):
        for slot in range(slots):
            block = column(wanted[0, 0, mine, slot, 1, replica], edge)
            copies.append((cotangent.at[0, pl.ds(whole, rest), :, block], outs[shift].at[slot]))
    for shift in range(shifts):
        other = lax.rem(mine + groups - shift - 1, groups)
        copies.append((errors.at[0, 0, 0, other], outs[shifts + shift]))
    copies = [
        pltpu.make_async_copy(source, target, copied.at[at])
        for at, (source, target) in enumerate(copies)
    ]
    for copy in copies:
        copy.start()
    for copy in copies:
        copy.wait()


def clear(after, strip, zeros, cleared):
    zeros[...] = jnp.zeros_like(zeros)
    rows = zeros.shape[0]
    writes = [
        pltpu.make_async_copy(zeros, strip.at[0, 0, pl.ds(part * rows, rows)], cleared.at[part])
        for part in range(strip.shape[2] // rows)
    ]
    for write in writes:
        write.start()
    for write in writes:
        write.wait()


def multiply(groups, whole, apart, to_step, to_column, plan, picked, error, *refs):
    shifts = groups - 1
    returned, heads = refs[0], refs[1:groups] if whole else []
    rests, refs = refs[1 + len(heads) :][:shifts], refs[1 + len(heads) + shifts :]
    carried, outs = refs[:shifts], refs[shifts:]
    mine = lax.axis_index("tensor")
    slots, edge = error.shape[4], picked.shape[1]
    for shift in range(groups):
        group = lax.rem(mine + shift, groups)
        for slot in range(slots):
            at = group * slots + slot
            block = column(plan[to_column + at], edge)
            if shift == 0:
                extra, parts = error[0, 0, 0, mine, slot], [returned[0, :, :, block]]
            else:
                extra, parts = carried[shift - 1][slot], [rests[shift - 1][slot]]
                if heads:
                    parts.insert(0, heads[shift - 1][0, :, :, block])
            tile, done = extra.astype(jnp.float32), 0
            for part in parts:
                part = part.reshape(-1, edge)
                left = picked[at, :, done : done + part.shape[0]]
                tile += jnp.dot(left, part, preferred_element_type=jnp.float32)
                done += part.shape[0]
            step = plan[to_step + at]
            if apart:
                outs[0][at] = tile
                store(tile.astype(jnp.bfloat16), step, outs[1:])
            else:
                outs[0][step] = tile


def store(tile, step, buffers):
    for at, buffer in enumerate(buffers):

        @pl.when(step == at)
        def _():
            buffer[...] = tile


def spread(to_step, plan, tiles, *buffers):
    for at in range(tiles.shape[0]):
        store(tiles[at], plan[to_step + at], buffers)


def place(count, alone, to_row, to_col, plan, *refs):
    blocks, strip, staged, sent = refs[:count], refs[-3], refs[-2], refs[-1]
    steps, edge = staged.shape[0], staged.shape[-1]

    def meets(one, other):
        return (plan[to_row + one] == plan[to_row + other]) & (
            plan[to_col + one] == plan[to_col + other]
        )

    def block_of(step):
        return blocks[0][step] if count == 1 else blocks[step][...]

    def first_of(step):
        first = plan[to_row + step] >= 0
        for earlier in range(0 if alone else step):
            first = first & jnp.logical_not(meets(earlier, step))
        return first

    def write_of(step):
        row, col = plan[to_row + step], plan[to_col + step]
        return pltpu.make_async_copy(
            blocks[step] if alone else staged.at[step],
            strip.at[0, 0, column(row, edge), column(col, edge)],
            sent.at[step],
        )

    for step in range(steps):

        @pl.when(first_of(step))
        def _():
            if not alone:
                total = block_of(step)
                for later in range(step + 1, steps):
                    total = total + jnp.where(meets(step, later), block_of(later), 0.0)
                staged[step] = total.astype(staged.dtype)
            write_of(step).start()

    for step in range(steps):

        @pl.when(first_of(step))
        def _():
            write_of(step).wait()


def body(mesh, activations, cotangent, error_tiles, tile_picks, row_owners):
    sections, replicas, groups = mesh.shape["pipe"], mesh.shape["dp"], mesh.shape["tensor"]
    edge = error_tiles.shape[-1]
    slots = tile_picks.shape[4]
    micro, tokens = activations.shape[1:3]
    width = cotangent.shape[-1] * groups
    strip_rows = row_owners.shape[-1] // replicas * edge
    picks = jnp.transpose(tile_picks, (0, 2, 3, 4, 5, 1))

    def moved(value, hop, shift):
        pairs = [
            (
                section * groups + group,
                (section + hop) % sections * groups + (group + shift) % groups,
            )
            for section in range(sections)
            for group in range(groups)
        ]
        return lax.ppermute(value, ("pipe", "tensor"), pairs)

    apart = replicas <= MOST_STEPS
    tiles, shifts = groups * slots, groups - 1
    whole = micro // 2
    asked = [moved(picks, 1, shift) for shift in range(1, groups)]
    returned = [moved(cotangent, -1, 0)]
    if whole:
        returned += [moved(cotangent[:, :whole], -1, -shift) for shift in range(1, groups)]
    cuts = pl.pallas_call(
        functools.partial(cut_out, shifts),
        out_shape=[pltpu.VMEM((slots, micro - whole, tokens, edge), cotangent.dtype)] * shifts
        + [pltpu.VMEM((slots, edge, edge), error_tiles.dtype)] * shifts,
        in_specs=[SMEM] * shifts + [ANY, ANY],
        out_specs=[VMEM] * (2 * shifts),
        scratch_shapes=[pltpu.SemaphoreType.DMA((shifts * slots + shifts,))],
        compiler_params=SMALL,
        cost_estimate=EARLY,
        name="cut_out",
    )(*asked, in_hbm(cotangent), in_hbm(error_tiles))
    rests = [moved(cuts[shift - 1], -1, -shift) for shift in range(1, groups)]
    carried = [
        lax.ppermute(
            cuts[shifts + shift - 1],
            "tensor",
            [((group + shift) % groups, group) for group in range(groups)],
        )
        for shift in range(1, groups)
    ]
    picked, plan = pl.pallas_call(
        functools.partial(pick, apart, width // edge),
        out_shape=[
            pltpu.VMEM((tiles, edge, micro * tokens), activations.dtype),
            jax.ShapeDtypeStruct((plan_sizes(tiles, replicas)[-1],), jnp.int32),
        ],
        in_specs=[SMEM, SMEM, ANY, ANY],
        out_specs=[VMEM, SMEM],
        scratch_shapes=[
            pltpu.VMEM((tiles, micro, tokens, edge), activations.dtype),
            pltpu.SMEM((row_owners.shape[-1] * (width // edge),), jnp.int32),
            pltpu.SemaphoreType.DMA((tiles,)),
        ],
        compiler_params=SMALL,
        name="pick",
    )(in_hbm(picks), in_hbm(row_owners), in_hbm(activations), cuts[0])

    zero_rows = min(strip_rows, 256)
    strip_shape = (1, 1, strip_rows, width)

    def cleared(after):
        return pl.pallas_call(
            clear,
            out_shape=pltpu.HBM(strip_shape, jnp.bfloat16),
            in_specs=[ANY],
            out_specs=pl.BlockSpec(memory_space=pltpu.HBM),
            scratch_shapes=[
                pltpu.VMEM((zero_rows, width), jnp.bfloat16),
                pltpu.SemaphoreType.DMA((strip_rows // zero_rows,)),
            ],
            compiler_params=SMALL,
            cost_estimate=pl.CostEstimate(
                flops=0, bytes_accessed=2 * strip_rows * width, transcendentals=0
            ),
            name="clear",
        )(after)

    to_step, to_column, to_row, to_col, _ = plan_sizes(tiles, replicas)
    tile_shape = (edge, edge)
    if apart:
        out_shape = [jax.ShapeDtypeStruct((tiles,) + tile_shape, jnp.float32)]
        out_shape += [jax.ShapeDtypeStruct(tile_shape, jnp.bfloat16)] * replicas
    else:
        out_shape = [jax.ShapeDtypeStruct((replicas,) + tile_shape, jnp.float32)]
    outgoing = pl.pallas_call(
        functools.partial(multiply, groups, whole, apart, to_step, to_column),
        out_shape=out_shape,
        in_specs=[SMEM] + [VMEM] * (2 + len(returned) + 2 * shifts),
        out_specs=[VMEM] * len(out_shape),
        compiler_params=SMALL,
        name="multiply",
    )(plan, picked, error_tiles, *returned, *rests, *carried)

    def placed(alone, incoming):
        return pl.pallas_call(
            functools.partial(place, len(incoming), alone, to_row, to_col),
            out_shape=jax.ShapeDtypeStruct(strip_shape, jnp.bfloat16),
            in_specs=[SMEM] + [VMEM] * len(incoming) + [ANY],
            out_specs=ANY,
            scratch_shapes=[
                pltpu.VMEM((replicas,) + tile_shape, jnp.bfloat16),
                pltpu.SemaphoreType.DMA((replicas,)),
            ],
            input_output_aliases={1 + len(incoming): 0},
            compiler_params=SMALL,
            name="place",
        )(plan, *incoming, cleared(outgoing[0]))

    def exchanged(blocks):
        moved = [
            lax.ppermute(
                blocks[step], "dp", [(one, (one + step) % replicas) for one in range(replicas)]
            )
            for step in range(1, replicas)
        ]
        return [blocks[0], *moved]

    def in_full():
        blocks = pl.pallas_call(
            functools.partial(spread, to_step),
            out_shape=[jax.ShapeDtypeStruct(tile_shape, jnp.float32)] * replicas,
            in_specs=[SMEM, VMEM],
            out_specs=[VMEM] * replicas,
            compiler_params=SMALL,
            name="spread",
        )(plan, outgoing[0])
        return placed(False, exchanged(blocks))

    if not apart:
        swapped = lax.all_to_all(outgoing[0], "dp", split_axis=0, concat_axis=0, tiled=True)
        return placed(False, [swapped])
    return lax.cond(plan[0] > 0, in_full, lambda: placed(True, exchanged(outgoing[1:])))


def solution(mesh):
    in_specs = (
        P("pipe", None, "dp", "tensor"),
        P("pipe", None, "dp", "tensor"),
        P("pipe", "dp", "tensor", None, None, None, None),
        P("pipe", None, "tensor", None, None, None),
        P("pipe", "tensor", None),
    )
    out_specs = P("pipe", "tensor", "dp", None)
    return jax.shard_map(
        functools.partial(body, mesh),
        mesh=mesh,
        in_specs=in_specs,
        out_specs=out_specs,
        check_vma=False,
    )
```

```python
import functools

import jax
import jax.numpy as jnp
from jax import lax
from jax.experimental import pallas as pl
from jax.experimental.pallas import tpu as pltpu
from jax.sharding import PartitionSpec as P

VMEM = pl.BlockSpec(memory_space=pltpu.VMEM)
SMEM = pl.BlockSpec(memory_space=pltpu.SMEM)
ANY = pl.BlockSpec(memory_space=pl.ANY)
MOST_STEPS = 8
SMALL = pltpu.CompilerParams(vmem_limit_bytes=4 << 20)


def in_hbm(value):
    return pltpu.with_memory_space_constraint(value, pltpu.HBM)


def column(index, edge):
    return pl.ds(pl.multiple_of(index * edge, edge), edge)


def step_between(source, target, replicas):
    if replicas & (replicas - 1):
        ahead = target - source
        return jnp.where(ahead < 0, ahead + replicas, ahead)
    apart = lax.bitwise_xor(jnp.int32(source), jnp.int32(target))
    return jnp.where(apart == 0, 0, replicas - apart)


def target_at(source, step, replicas):
    if replicas & (replicas - 1):
        return (source + step) % replicas
    return source ^ (replicas - step)


def plan_sizes(tiles, steps):
    return 1, 1 + tiles, 1 + 2 * tiles, 1 + 2 * tiles + steps, 1 + 2 * tiles + 2 * steps


def pick(shifts, apart, columns, picks, owners, activations, errors, picked, plan, *refs):
    cuts, (read, seen, copied) = refs[:shifts], refs[shifts:]
    replica, mine = lax.axis_index("dp"), lax.axis_index("tensor")
    groups, slots, replicas = picks.shape[2], picks.shape[3], picks.shape[-1]
    edge = picked.shape[1]
    tiles = [(group, slot) for group in range(groups) for slot in range(slots)]
    reads = []
    for at, (group, slot) in enumerate(tiles):
        block = picks[0, 0, group, slot, 0, replica]
        reads.append(
            pltpu.make_async_copy(
                activations.at[0, :, :, column(block, edge)], read.at[at], copied.at[at]
            )
        )
    for shift, cut in enumerate(cuts):
        other = lax.rem(mine + groups - shift - 1, groups)
        reads.append(
            pltpu.make_async_copy(errors.at[0, 0, 0, other], cut, copied.at[len(tiles) + shift])
        )
    for copy in reads:
        copy.start()

    owned = owners.shape[-1] // replicas
    per_group = columns // groups
    to_step, to_column, to_row, to_col, _ = plan_sizes(len(tiles), replicas)

    def step_from(source, target):
        return step_between(source, target, replicas) if apart else target

    for at, (group, slot) in enumerate(tiles):
        row = owners[0, 0, picks[0, 0, group, slot, 0, replica]]
        owner = jnp.int32(0)
        for one in range(1, replicas):
            owner += (row >= one * owned).astype(jnp.int32)
        plan[to_step + at] = step_from(replica, owner)
        plan[to_column + at] = picks[0, 0, group, slot, 1, replica]

    for origin in range(replicas):
        place_row, place_col = jnp.int32(-1), jnp.int32(0)
        for group, slot in tiles:
            row = owners[0, 0, picks[0, 0, group, slot, 0, origin]] - replica * owned
            here = (row >= 0) & (row < owned)
            place_row = jnp.where(here, row, place_row)
            place_col = jnp.where(
                here, picks[0, 0, group, slot, 1, origin] + group * per_group, place_col
            )
        step = step_from(origin, replica) if apart else origin
        plan[to_row + step] = place_row
        plan[to_col + step] = place_col

    meets = jnp.int32(0)
    if apart:
        spots = [
            picks[0, 0, group, slot, 0, origin] * columns
            + picks[0, 0, group, slot, 1, origin]
            + group * per_group
            for group, slot in tiles
            for origin in range(replicas)
        ]
        for spot in spots:
            seen[spot] = 0
        for spot in spots:
            meets = meets | seen[spot]
            seen[spot] = 1
    plan[0] = meets

    for at, copy in enumerate(reads):
        copy.wait()
        if at < len(tiles):
            picked[at] = read[at].reshape(-1, edge).T


def clear(after, strip, zeros, cleared):
    zeros[...] = jnp.zeros_like(zeros)
    rows = zeros.shape[0]
    writes = [
        pltpu.make_async_copy(zeros, strip.at[0, 0, pl.ds(part * rows, rows)], cleared.at[part])
        for part in range(strip.shape[2] // rows)
    ]
    for write in writes:
        write.start()
    for write in writes:
        write.wait()


def multiply(groups, apart, to_step, to_column, plan, picked, error, *refs):
    returned, carried, outs = refs[:groups], refs[groups : 2 * groups - 1], refs[2 * groups - 1 :]
    mine = lax.axis_index("tensor")
    slots, (edge, tokens) = error.shape[4], picked.shape[1:]
    for shift in range(groups):
        group = lax.rem(mine + shift, groups)
        for slot in range(slots):
            at = group * slots + slot
            right = returned[shift][0, :, :, column(plan[to_column + at], edge)]
            extra = error[0, 0, 0, mine, slot] if shift == 0 else carried[shift - 1][slot]
            tile = jnp.dot(
                picked[at], right.reshape(tokens, edge), preferred_element_type=jnp.float32
            )
            tile = tile + extra.astype(jnp.float32)
            step = plan[to_step + at]
            if apart:
                outs[0][at] = tile
                store(tile.astype(jnp.bfloat16), step, outs[1:])
            else:
                outs[0][step] = tile


def store(tile, step, buffers):
    for at, buffer in enumerate(buffers):

        @pl.when(step == at)
        def _():
            buffer[...] = tile


def spread(to_step, plan, tiles, *buffers):
    for at in range(tiles.shape[0]):
        store(tiles[at], plan[to_step + at], buffers)


def place(count, alone, to_row, to_col, plan, *refs):
    blocks, strip, staged, sent = refs[:count], refs[-3], refs[-2], refs[-1]
    steps, edge = staged.shape[0], staged.shape[-1]

    def meets(one, other):
        return (plan[to_row + one] == plan[to_row + other]) & (
            plan[to_col + one] == plan[to_col + other]
        )

    def block_of(step):
        return blocks[0][step] if count == 1 else blocks[step][...]

    def first_of(step):
        first = plan[to_row + step] >= 0
        for earlier in range(0 if alone else step):
            first = first & jnp.logical_not(meets(earlier, step))
        return first

    def write_of(step):
        row, col = plan[to_row + step], plan[to_col + step]
        return pltpu.make_async_copy(
            blocks[step] if alone else staged.at[step],
            strip.at[0, 0, column(row, edge), column(col, edge)],
            sent.at[step],
        )

    for step in range(steps):

        @pl.when(first_of(step))
        def _():
            if not alone:
                total = block_of(step)
                for later in range(step + 1, steps):
                    total = total + jnp.where(meets(step, later), block_of(later), 0.0)
                staged[step] = total.astype(staged.dtype)
            write_of(step).start()

    for step in range(steps):

        @pl.when(first_of(step))
        def _():
            write_of(step).wait()


def body(mesh, activations, cotangent, error_tiles, tile_picks, row_owners):
    sections, replicas, groups = mesh.shape["pipe"], mesh.shape["dp"], mesh.shape["tensor"]
    edge = error_tiles.shape[-1]
    slots = tile_picks.shape[4]
    micro, tokens = activations.shape[1:3]
    width = cotangent.shape[-1] * groups
    strip_rows = row_owners.shape[-1] // replicas * edge
    picks = jnp.transpose(tile_picks, (0, 2, 3, 4, 5, 1))

    returned = []
    for shift in range(groups):
        pairs = [
            (
                (section + 1) % sections * groups + (group + shift) % groups,
                section * groups + group,
            )
            for section in range(sections)
            for group in range(groups)
        ]
        returned.append(lax.ppermute(cotangent, ("pipe", "tensor"), pairs))
    apart = replicas <= MOST_STEPS
    tiles, shifts = groups * slots, groups - 1
    picked, plan, *errors = pl.pallas_call(
        functools.partial(pick, shifts, apart, width // edge),
        out_shape=[
            pltpu.VMEM((tiles, edge, micro * tokens), activations.dtype),
            jax.ShapeDtypeStruct((plan_sizes(tiles, replicas)[-1],), jnp.int32),
        ]
        + [pltpu.VMEM((slots, edge, edge), error_tiles.dtype)] * shifts,
        in_specs=[SMEM, SMEM, ANY, ANY],
        out_specs=[VMEM, SMEM] + [VMEM] * shifts,
        scratch_shapes=[
            pltpu.VMEM((tiles, micro, tokens, edge), activations.dtype),
            pltpu.SMEM((row_owners.shape[-1] * (width // edge),), jnp.int32),
            pltpu.SemaphoreType.DMA((tiles + shifts,)),
        ],
        compiler_params=SMALL,
        name="pick",
    )(in_hbm(picks), in_hbm(row_owners), in_hbm(activations), in_hbm(error_tiles))
    carried = [
        lax.ppermute(
            error, "tensor", [((group + shift + 1) % groups, group) for group in range(groups)]
        )
        for shift, error in enumerate(errors)
    ]

    zero_rows = min(strip_rows, 256)
    strip_shape = (1, 1, strip_rows, width)
    cleared = pl.pallas_call(
        clear,
        out_shape=pltpu.HBM(strip_shape, jnp.bfloat16),
        in_specs=[ANY],
        out_specs=pl.BlockSpec(memory_space=pltpu.HBM),
        scratch_shapes=[
            pltpu.VMEM((zero_rows, width), jnp.bfloat16),
            pltpu.SemaphoreType.DMA((strip_rows // zero_rows,)),
        ],
        compiler_params=SMALL,
        cost_estimate=pl.CostEstimate(
            flops=0, bytes_accessed=2 * strip_rows * width, transcendentals=0
        ),
        name="clear",
    )(picked)

    to_step, to_column, to_row, to_col, _ = plan_sizes(tiles, replicas)
    tile_shape = (edge, edge)
    if apart:
        out_shape = [jax.ShapeDtypeStruct((tiles,) + tile_shape, jnp.float32)]
        out_shape += [jax.ShapeDtypeStruct(tile_shape, jnp.bfloat16)] * replicas
    else:
        out_shape = [jax.ShapeDtypeStruct((replicas,) + tile_shape, jnp.float32)]
    outgoing = pl.pallas_call(
        functools.partial(multiply, groups, apart, to_step, to_column),
        out_shape=out_shape,
        in_specs=[SMEM] + [VMEM] * (2 * groups + 1),
        out_specs=[VMEM] * len(out_shape),
        compiler_params=SMALL,
        name="multiply",
    )(plan, picked, error_tiles, *returned, *carried)

    def placed(alone, incoming):
        return pl.pallas_call(
            functools.partial(place, len(incoming), alone, to_row, to_col),
            out_shape=jax.ShapeDtypeStruct(strip_shape, jnp.bfloat16),
            in_specs=[SMEM] + [VMEM] * len(incoming) + [ANY],
            out_specs=ANY,
            scratch_shapes=[
                pltpu.VMEM((replicas,) + tile_shape, jnp.bfloat16),
                pltpu.SemaphoreType.DMA((replicas,)),
            ],
            input_output_aliases={1 + len(incoming): 0},
            compiler_params=SMALL,
            name="place",
        )(plan, *incoming, cleared)

    def exchanged(blocks):
        moved = [
            lax.ppermute(
                blocks[step], "dp", [(one, target_at(one, step, replicas)) for one in range(replicas)]
            )
            for step in range(1, replicas)
        ]
        return [blocks[0], *moved]

    def in_full():
        blocks = pl.pallas_call(
            functools.partial(spread, to_step),
            out_shape=[jax.ShapeDtypeStruct(tile_shape, jnp.float32)] * replicas,
            in_specs=[SMEM, VMEM],
            out_specs=[VMEM] * replicas,
            compiler_params=SMALL,
            name="spread",
        )(plan, outgoing[0])
        return placed(False, exchanged(blocks))

    if not apart:
        swapped = lax.all_to_all(outgoing[0], "dp", split_axis=0, concat_axis=0, tiled=True)
        return placed(False, [swapped])
    return lax.cond(plan[0] > 0, in_full, lambda: placed(True, exchanged(outgoing[1:])))


def solution(mesh):
    in_specs = (
        P("pipe", None, "dp", "tensor"),
        P("pipe", None, "dp", "tensor"),
        P("pipe", "dp", "tensor", None, None, None, None),
        P("pipe", None, "tensor", None, None, None),
        P("pipe", "tensor", None),
    )
    out_specs = P("pipe", "tensor", "dp", None)
    return jax.shard_map(
        functools.partial(body, mesh),
        mesh=mesh,
        in_specs=in_specs,
        out_specs=out_specs,
        check_vma=False,
    )
```

```python
import functools

import jax
import jax.numpy as jnp
from jax import lax
from jax.experimental import pallas as pl
from jax.experimental.pallas import tpu as pltpu
from jax.sharding import PartitionSpec as P

VMEM = pl.BlockSpec(memory_space=pltpu.VMEM)
SMEM = pl.BlockSpec(memory_space=pltpu.SMEM)
ANY = pl.BlockSpec(memory_space=pl.ANY)
MOST_STEPS = 8
ROUNDS = {4: [(2, 3, 1, 0), (2, 0, 3, 1), (1, 3, 0, 2), (3, 2, 0, 1)]}
SMALL = pltpu.CompilerParams(vmem_limit_bytes=4 << 20)


def in_hbm(value):
    return pltpu.with_memory_space_constraint(value, pltpu.HBM)


def column(index, edge):
    return pl.ds(pl.multiple_of(index * edge, edge), edge)


def rounds(replicas):
    shifts = [
        tuple((one + step) % replicas for one in range(replicas)) for step in range(1, replicas)
    ]
    return ROUNDS.get(replicas, shifts)


def step_table(replicas):
    table = []
    for source in range(replicas):
        steps = [0] * replicas
        for step, targets in reversed(list(enumerate(rounds(replicas), 1))):
            steps[targets[source]] = step
        table.append(sum(step << 4 * target for target, step in enumerate(steps)))
    return table


def plan_sizes(tiles, steps):
    return 1, 1 + tiles, 1 + 2 * tiles, 1 + 2 * tiles + steps, 1 + 2 * tiles + 2 * steps


def pick(shifts, apart, columns, picks, owners, activations, errors, picked, plan, *refs):
    cuts, (read, seen, copied) = refs[:shifts], refs[shifts:]
    replica, group_at = lax.axis_index("dp"), lax.axis_index("tensor")
    groups, slots, replicas = picks.shape[2], picks.shape[3], picks.shape[-1]
    edge = picked.shape[1]
    tiles = [(group, slot) for group in range(groups) for slot in range(slots)]
    reads = []
    for at, (group, slot) in enumerate(tiles):
        block = picks[0, 0, group, slot, 0, replica]
        reads.append(
            pltpu.make_async_copy(
                activations.at[0, :, :, column(block, edge)], read.at[at], copied.at[at]
            )
        )
    for shift, cut in enumerate(cuts):
        other = lax.rem(group_at + groups - shift - 1, groups)
        reads.append(
            pltpu.make_async_copy(errors.at[0, 0, 0, other], cut, copied.at[len(tiles) + shift])
        )
    for copy in reads:
        copy.start()

    owned = owners.shape[-1] // replicas
    per_group = columns // groups
    steps = len(rounds(replicas)) + 1 if apart else replicas
    to_step, to_column, to_row, to_col, end = plan_sizes(len(tiles), steps)
    table = step_table(replicas) if apart else []
    mine = jnp.int32(0)
    for source, packed in enumerate(table):
        mine = jnp.where(replica == source, packed, mine)
    for at in range(to_row, end):
        plan[at] = -1

    for at, (group, slot) in enumerate(tiles):
        row = owners[0, 0, picks[0, 0, group, slot, 0, replica]]
        owner = jnp.int32(0)
        for one in range(1, replicas):
            owner += (row >= one * owned).astype(jnp.int32)
        plan[to_step + at] = (mine >> 4 * owner) & 15 if apart else owner
        plan[to_column + at] = picks[0, 0, group, slot, 1, replica]

    for origin in range(replicas):
        place_row, place_col = jnp.int32(-1), jnp.int32(0)
        for group, slot in tiles:
            row = owners[0, 0, picks[0, 0, group, slot, 0, origin]] - replica * owned
            here = (row >= 0) & (row < owned)
            place_row = jnp.where(here, row, place_row)
            place_col = jnp.where(
                here, picks[0, 0, group, slot, 1, origin] + group * per_group, place_col
            )
        step = (jnp.int32(table[origin]) >> 4 * replica) & 15 if apart else origin
        plan[to_row + step] = place_row
        plan[to_col + step] = place_col

    meets = jnp.int32(0)
    if apart:
        spots = [
            picks[0, 0, group, slot, 0, origin] * columns
            + picks[0, 0, group, slot, 1, origin]
            + group * per_group
            for group, slot in tiles
            for origin in range(replicas)
        ]
        for spot in spots:
            seen[spot] = 0
        for spot in spots:
            meets = meets | seen[spot]
            seen[spot] = 1
    plan[0] = meets

    for at, copy in enumerate(reads):
        copy.wait()
        if at < len(tiles):
            picked[at] = read[at].reshape(-1, edge).T


def clear(after, strip, zeros, cleared):
    zeros[...] = jnp.zeros_like(zeros)
    rows = zeros.shape[0]
    writes = [
        pltpu.make_async_copy(zeros, strip.at[0, 0, pl.ds(part * rows, rows)], cleared.at[part])
        for part in range(strip.shape[2] // rows)
    ]
    for write in writes:
        write.start()
    for write in writes:
        write.wait()


def multiply(groups, apart, to_step, to_column, plan, picked, error, *refs):
    returned, carried, outs = refs[:groups], refs[groups : 2 * groups - 1], refs[2 * groups - 1 :]
    mine = lax.axis_index("tensor")
    slots, (edge, tokens) = error.shape[4], picked.shape[1:]
    for shift in range(groups):
        group = lax.rem(mine + shift, groups)
        for slot in range(slots):
            at = group * slots + slot
            right = returned[shift][0, :, :, column(plan[to_column + at], edge)]
            extra = error[0, 0, 0, mine, slot] if shift == 0 else carried[shift - 1][slot]
            tile = jnp.dot(
                picked[at], right.reshape(tokens, edge), preferred_element_type=jnp.float32
            )
            tile = tile + extra.astype(jnp.float32)
            step = plan[to_step + at]
            if apart:
                outs[0][at] = tile
                store(tile.astype(jnp.bfloat16), step, outs[1:])
            else:
                outs[0][step] = tile


def store(tile, step, buffers):
    for at, buffer in enumerate(buffers):

        @pl.when(step == at)
        def _():
            buffer[...] = tile


def spread(to_step, plan, tiles, *buffers):
    for at in range(tiles.shape[0]):
        store(tiles[at], plan[to_step + at], buffers)


def place(count, alone, to_row, to_col, plan, *refs):
    blocks, strip, staged, sent = refs[:count], refs[-3], refs[-2], refs[-1]
    steps, edge = staged.shape[0], staged.shape[-1]

    def meets(one, other):
        return (plan[to_row + one] == plan[to_row + other]) & (
            plan[to_col + one] == plan[to_col + other]
        )

    def block_of(step):
        return blocks[0][step] if count == 1 else blocks[step][...]

    def first_of(step):
        first = plan[to_row + step] >= 0
        for earlier in range(0 if alone else step):
            first = first & jnp.logical_not(meets(earlier, step))
        return first

    def write_of(step):
        row, col = plan[to_row + step], plan[to_col + step]
        return pltpu.make_async_copy(
            blocks[step] if alone else staged.at[step],
            strip.at[0, 0, column(row, edge), column(col, edge)],
            sent.at[step],
        )

    for step in range(steps):

        @pl.when(first_of(step))
        def _():
            if not alone:
                total = block_of(step)
                for later in range(step + 1, steps):
                    total = total + jnp.where(meets(step, later), block_of(later), 0.0)
                staged[step] = total.astype(staged.dtype)
            write_of(step).start()

    for step in range(steps):

        @pl.when(first_of(step))
        def _():
            write_of(step).wait()


def body(mesh, activations, cotangent, error_tiles, tile_picks, row_owners):
    sections, replicas, groups = mesh.shape["pipe"], mesh.shape["dp"], mesh.shape["tensor"]
    edge = error_tiles.shape[-1]
    slots = tile_picks.shape[4]
    micro, tokens = activations.shape[1:3]
    width = cotangent.shape[-1] * groups
    strip_rows = row_owners.shape[-1] // replicas * edge
    picks = jnp.transpose(tile_picks, (0, 2, 3, 4, 5, 1))

    returned = []
    for shift in range(groups):
        pairs = [
            (
                (section + 1) % sections * groups + (group + shift) % groups,
                section * groups + group,
            )
            for section in range(sections)
            for group in range(groups)
        ]
        returned.append(lax.ppermute(cotangent, ("pipe", "tensor"), pairs))
    apart = replicas <= MOST_STEPS
    tiles, shifts = groups * slots, groups - 1
    steps = len(rounds(replicas)) + 1 if apart else replicas
    picked, plan, *errors = pl.pallas_call(
        functools.partial(pick, shifts, apart, width // edge),
        out_shape=[
            pltpu.VMEM((tiles, edge, micro * tokens), activations.dtype),
            jax.ShapeDtypeStruct((plan_sizes(tiles, steps)[-1],), jnp.int32),
        ]
        + [pltpu.VMEM((slots, edge, edge), error_tiles.dtype)] * shifts,
        in_specs=[SMEM, SMEM, ANY, ANY],
        out_specs=[VMEM, SMEM] + [VMEM] * shifts,
        scratch_shapes=[
            pltpu.VMEM((tiles, micro, tokens, edge), activations.dtype),
            pltpu.SMEM((row_owners.shape[-1] * (width // edge),), jnp.int32),
            pltpu.SemaphoreType.DMA((tiles + shifts,)),
        ],
        compiler_params=SMALL,
        name="pick",
    )(in_hbm(picks), in_hbm(row_owners), in_hbm(activations), in_hbm(error_tiles))
    carried = [
        lax.ppermute(
            error, "tensor", [((group + shift + 1) % groups, group) for group in range(groups)]
        )
        for shift, error in enumerate(errors)
    ]

    zero_rows = min(strip_rows, 256)
    strip_shape = (1, 1, strip_rows, width)
    cleared = pl.pallas_call(
        clear,
        out_shape=pltpu.HBM(strip_shape, jnp.bfloat16),
        in_specs=[ANY],
        out_specs=pl.BlockSpec(memory_space=pltpu.HBM),
        scratch_shapes=[
            pltpu.VMEM((zero_rows, width), jnp.bfloat16),
            pltpu.SemaphoreType.DMA((strip_rows // zero_rows,)),
        ],
        compiler_params=SMALL,
        cost_estimate=pl.CostEstimate(
            flops=0, bytes_accessed=2 * strip_rows * width, transcendentals=0
        ),
        name="clear",
    )(picked)

    to_step, to_column, to_row, to_col, _ = plan_sizes(tiles, steps)
    tile_shape = (edge, edge)
    if apart:
        out_shape = [jax.ShapeDtypeStruct((tiles,) + tile_shape, jnp.float32)]
        out_shape += [jax.ShapeDtypeStruct(tile_shape, jnp.bfloat16)] * steps
    else:
        out_shape = [jax.ShapeDtypeStruct((replicas,) + tile_shape, jnp.float32)]
    outgoing = pl.pallas_call(
        functools.partial(multiply, groups, apart, to_step, to_column),
        out_shape=out_shape,
        in_specs=[SMEM] + [VMEM] * (2 * groups + 1),
        out_specs=[VMEM] * len(out_shape),
        compiler_params=SMALL,
        name="multiply",
    )(plan, picked, error_tiles, *returned, *carried)

    def placed(alone, incoming):
        return pl.pallas_call(
            functools.partial(place, len(incoming), alone, to_row, to_col),
            out_shape=jax.ShapeDtypeStruct(strip_shape, jnp.bfloat16),
            in_specs=[SMEM] + [VMEM] * len(incoming) + [ANY],
            out_specs=ANY,
            scratch_shapes=[
                pltpu.VMEM((steps,) + tile_shape, jnp.bfloat16),
                pltpu.SemaphoreType.DMA((steps,)),
            ],
            input_output_aliases={1 + len(incoming): 0},
            compiler_params=SMALL,
            name="place",
        )(plan, *incoming, cleared)

    def exchanged(blocks):
        moved = [
            lax.ppermute(block, "dp", list(enumerate(targets)))
            for block, targets in zip(blocks[1:], rounds(replicas))
        ]
        return [blocks[0], *moved]

    def in_full():
        blocks = pl.pallas_call(
            functools.partial(spread, to_step),
            out_shape=[jax.ShapeDtypeStruct(tile_shape, jnp.float32)] * steps,
            in_specs=[SMEM, VMEM],
            out_specs=[VMEM] * steps,
            compiler_params=SMALL,
            name="spread",
        )(plan, outgoing[0])
        return placed(False, exchanged(blocks))

    if not apart:
        swapped = lax.all_to_all(outgoing[0], "dp", split_axis=0, concat_axis=0, tiled=True)
        return placed(False, [swapped])
    return lax.cond(plan[0] > 0, in_full, lambda: placed(True, exchanged(outgoing[1:])))


def solution(mesh):
    in_specs = (
        P("pipe", None, "dp", "tensor"),
        P("pipe", None, "dp", "tensor"),
        P("pipe", "dp", "tensor", None, None, None, None),
        P("pipe", None, "tensor", None, None, None),
        P("pipe", "tensor", None),
    )
    out_specs = P("pipe", "tensor", "dp", None)
    return jax.shard_map(
        functools.partial(body, mesh),
        mesh=mesh,
        in_specs=in_specs,
        out_specs=out_specs,
        check_vma=False,
    )
```

```python
import functools

import jax
import jax.numpy as jnp
from jax import lax
from jax.experimental import pallas as pl
from jax.experimental.pallas import tpu as pltpu
from jax.sharding import PartitionSpec as P

VMEM = pl.BlockSpec(memory_space=pltpu.VMEM)
SMEM = pl.BlockSpec(memory_space=pltpu.SMEM)
ANY = pl.BlockSpec(memory_space=pl.ANY)
MOST_STEPS = 8
ROUNDS = {4: [(2, 3, 1, 0), (3, 2, 0, 1), (1, 0, 3, 2)]}
SMALL = pltpu.CompilerParams(vmem_limit_bytes=4 << 20)


def in_hbm(value):
    return pltpu.with_memory_space_constraint(value, pltpu.HBM)


def column(index, edge):
    return pl.ds(pl.multiple_of(index * edge, edge), edge)


def rounds(replicas):
    shifts = [
        tuple((one + step) % replicas for one in range(replicas)) for step in range(1, replicas)
    ]
    return ROUNDS.get(replicas, shifts)


def step_table(replicas):
    table = []
    for source in range(replicas):
        steps = [0] * replicas
        for step, targets in reversed(list(enumerate(rounds(replicas), 1))):
            steps[targets[source]] = step
        table.append(sum(step << 4 * target for target, step in enumerate(steps)))
    return table


def plan_sizes(tiles, steps):
    return 1, 1 + tiles, 1 + 2 * tiles, 1 + 2 * tiles + steps, 1 + 2 * tiles + 2 * steps


def pick(shifts, apart, columns, picks, owners, activations, errors, picked, plan, *refs):
    cuts, (read, seen, copied) = refs[:shifts], refs[shifts:]
    replica, group_at = lax.axis_index("dp"), lax.axis_index("tensor")
    groups, slots, replicas = picks.shape[2], picks.shape[3], picks.shape[-1]
    edge = picked.shape[1]
    tiles = [(group, slot) for group in range(groups) for slot in range(slots)]
    reads = []
    for at, (group, slot) in enumerate(tiles):
        block = picks[0, 0, group, slot, 0, replica]
        reads.append(
            pltpu.make_async_copy(
                activations.at[0, :, :, column(block, edge)], read.at[at], copied.at[at]
            )
        )
    for shift, cut in enumerate(cuts):
        other = lax.rem(group_at + groups - shift - 1, groups)
        reads.append(
            pltpu.make_async_copy(errors.at[0, 0, 0, other], cut, copied.at[len(tiles) + shift])
        )
    for copy in reads:
        copy.start()

    owned = owners.shape[-1] // replicas
    per_group = columns // groups
    steps = len(rounds(replicas)) + 1 if apart else replicas
    to_step, to_column, to_row, to_col, end = plan_sizes(len(tiles), steps)
    table = step_table(replicas) if apart else []
    mine = jnp.int32(0)
    for source, packed in enumerate(table):
        mine = jnp.where(replica == source, packed, mine)
    for at in range(to_row, end):
        plan[at] = -1

    for at, (group, slot) in enumerate(tiles):
        row = owners[0, 0, picks[0, 0, group, slot, 0, replica]]
        owner = jnp.int32(0)
        for one in range(1, replicas):
            owner += (row >= one * owned).astype(jnp.int32)
        plan[to_step + at] = (mine >> 4 * owner) & 15 if apart else owner
        plan[to_column + at] = picks[0, 0, group, slot, 1, replica]

    for origin in range(replicas):
        place_row, place_col = jnp.int32(-1), jnp.int32(0)
        for group, slot in tiles:
            row = owners[0, 0, picks[0, 0, group, slot, 0, origin]] - replica * owned
            here = (row >= 0) & (row < owned)
            place_row = jnp.where(here, row, place_row)
            place_col = jnp.where(
                here, picks[0, 0, group, slot, 1, origin] + group * per_group, place_col
            )
        step = (jnp.int32(table[origin]) >> 4 * replica) & 15 if apart else origin
        plan[to_row + step] = place_row
        plan[to_col + step] = place_col

    meets = jnp.int32(0)
    if apart:
        spots = [
            picks[0, 0, group, slot, 0, origin] * columns
            + picks[0, 0, group, slot, 1, origin]
            + group * per_group
            for group, slot in tiles
            for origin in range(replicas)
        ]
        for spot in spots:
            seen[spot] = 0
        for spot in spots:
            meets = meets | seen[spot]
            seen[spot] = 1
    plan[0] = meets

    for at, copy in enumerate(reads):
        copy.wait()
        if at < len(tiles):
            picked[at] = read[at].reshape(-1, edge).T


def clear(after, strip, zeros, cleared):
    zeros[...] = jnp.zeros_like(zeros)
    rows = zeros.shape[0]
    writes = [
        pltpu.make_async_copy(zeros, strip.at[0, 0, pl.ds(part * rows, rows)], cleared.at[part])
        for part in range(strip.shape[2] // rows)
    ]
    for write in writes:
        write.start()
    for write in writes:
        write.wait()


def multiply(groups, apart, to_step, to_column, plan, picked, error, *refs):
    returned, carried, outs = refs[:groups], refs[groups : 2 * groups - 1], refs[2 * groups - 1 :]
    mine = lax.axis_index("tensor")
    slots, (edge, tokens) = error.shape[4], picked.shape[1:]
    for shift in range(groups):
        group = lax.rem(mine + shift, groups)
        for slot in range(slots):
            at = group * slots + slot
            right = returned[shift][0, :, :, column(plan[to_column + at], edge)]
            extra = error[0, 0, 0, mine, slot] if shift == 0 else carried[shift - 1][slot]
            tile = jnp.dot(
                picked[at], right.reshape(tokens, edge), preferred_element_type=jnp.float32
            )
            tile = tile + extra.astype(jnp.float32)
            step = plan[to_step + at]
            if apart:
                outs[0][at] = tile
                store(tile.astype(jnp.bfloat16), step, outs[1:])
            else:
                outs[0][step] = tile


def store(tile, step, buffers):
    for at, buffer in enumerate(buffers):

        @pl.when(step == at)
        def _():
            buffer[...] = tile


def spread(to_step, plan, tiles, *buffers):
    for at in range(tiles.shape[0]):
        store(tiles[at], plan[to_step + at], buffers)


def place(count, alone, to_row, to_col, plan, *refs):
    blocks, strip, staged, sent = refs[:count], refs[-3], refs[-2], refs[-1]
    steps, edge = staged.shape[0], staged.shape[-1]

    def meets(one, other):
        return (plan[to_row + one] == plan[to_row + other]) & (
            plan[to_col + one] == plan[to_col + other]
        )

    def block_of(step):
        return blocks[0][step] if count == 1 else blocks[step][...]

    def first_of(step):
        first = plan[to_row + step] >= 0
        for earlier in range(0 if alone else step):
            first = first & jnp.logical_not(meets(earlier, step))
        return first

    def write_of(step):
        row, col = plan[to_row + step], plan[to_col + step]
        return pltpu.make_async_copy(
            blocks[step] if alone else staged.at[step],
            strip.at[0, 0, column(row, edge), column(col, edge)],
            sent.at[step],
        )

    for step in range(steps):

        @pl.when(first_of(step))
        def _():
            if not alone:
                total = block_of(step)
                for later in range(step + 1, steps):
                    total = total + jnp.where(meets(step, later), block_of(later), 0.0)
                staged[step] = total.astype(staged.dtype)
            write_of(step).start()

    for step in range(steps):

        @pl.when(first_of(step))
        def _():
            write_of(step).wait()


def body(mesh, activations, cotangent, error_tiles, tile_picks, row_owners):
    sections, replicas, groups = mesh.shape["pipe"], mesh.shape["dp"], mesh.shape["tensor"]
    edge = error_tiles.shape[-1]
    slots = tile_picks.shape[4]
    micro, tokens = activations.shape[1:3]
    width = cotangent.shape[-1] * groups
    strip_rows = row_owners.shape[-1] // replicas * edge
    picks = jnp.transpose(tile_picks, (0, 2, 3, 4, 5, 1))

    returned = []
    for shift in range(groups):
        pairs = [
            (
                (section + 1) % sections * groups + (group + shift) % groups,
                section * groups + group,
            )
            for section in range(sections)
            for group in range(groups)
        ]
        returned.append(lax.ppermute(cotangent, ("pipe", "tensor"), pairs))
    apart = replicas <= MOST_STEPS
    tiles, shifts = groups * slots, groups - 1
    steps = len(rounds(replicas)) + 1 if apart else replicas
    picked, plan, *errors = pl.pallas_call(
        functools.partial(pick, shifts, apart, width // edge),
        out_shape=[
            pltpu.VMEM((tiles, edge, micro * tokens), activations.dtype),
            jax.ShapeDtypeStruct((plan_sizes(tiles, steps)[-1],), jnp.int32),
        ]
        + [pltpu.VMEM((slots, edge, edge), error_tiles.dtype)] * shifts,
        in_specs=[SMEM, SMEM, ANY, ANY],
        out_specs=[VMEM, SMEM] + [VMEM] * shifts,
        scratch_shapes=[
            pltpu.VMEM((tiles, micro, tokens, edge), activations.dtype),
            pltpu.SMEM((row_owners.shape[-1] * (width // edge),), jnp.int32),
            pltpu.SemaphoreType.DMA((tiles + shifts,)),
        ],
        compiler_params=SMALL,
        name="pick",
    )(in_hbm(picks), in_hbm(row_owners), in_hbm(activations), in_hbm(error_tiles))
    carried = [
        lax.ppermute(
            error, "tensor", [((group + shift + 1) % groups, group) for group in range(groups)]
        )
        for shift, error in enumerate(errors)
    ]

    zero_rows = min(strip_rows, 256)
    strip_shape = (1, 1, strip_rows, width)
    cleared = pl.pallas_call(
        clear,
        out_shape=pltpu.HBM(strip_shape, jnp.bfloat16),
        in_specs=[ANY],
        out_specs=pl.BlockSpec(memory_space=pltpu.HBM),
        scratch_shapes=[
            pltpu.VMEM((zero_rows, width), jnp.bfloat16),
            pltpu.SemaphoreType.DMA((strip_rows // zero_rows,)),
        ],
        compiler_params=SMALL,
        cost_estimate=pl.CostEstimate(
            flops=0, bytes_accessed=2 * strip_rows * width, transcendentals=0
        ),
        name="clear",
    )(picked)

    to_step, to_column, to_row, to_col, _ = plan_sizes(tiles, steps)
    tile_shape = (edge, edge)
    if apart:
        out_shape = [jax.ShapeDtypeStruct((tiles,) + tile_shape, jnp.float32)]
        out_shape += [jax.ShapeDtypeStruct(tile_shape, jnp.bfloat16)] * steps
    else:
        out_shape = [jax.ShapeDtypeStruct((replicas,) + tile_shape, jnp.float32)]
    outgoing = pl.pallas_call(
        functools.partial(multiply, groups, apart, to_step, to_column),
        out_shape=out_shape,
        in_specs=[SMEM] + [VMEM] * (2 * groups + 1),
        out_specs=[VMEM] * len(out_shape),
        compiler_params=SMALL,
        name="multiply",
    )(plan, picked, error_tiles, *returned, *carried)

    def placed(alone, incoming):
        return pl.pallas_call(
            functools.partial(place, len(incoming), alone, to_row, to_col),
            out_shape=jax.ShapeDtypeStruct(strip_shape, jnp.bfloat16),
            in_specs=[SMEM] + [VMEM] * len(incoming) + [ANY],
            out_specs=ANY,
            scratch_shapes=[
                pltpu.VMEM((steps,) + tile_shape, jnp.bfloat16),
                pltpu.SemaphoreType.DMA((steps,)),
            ],
            input_output_aliases={1 + len(incoming): 0},
            compiler_params=SMALL,
            name="place",
        )(plan, *incoming, cleared)

    def exchanged(blocks):
        moved = [
            lax.ppermute(block, "dp", list(enumerate(targets)))
            for block, targets in zip(blocks[1:], rounds(replicas))
        ]
        return [blocks[0], *moved]

    def in_full():
        blocks = pl.pallas_call(
            functools.partial(spread, to_step),
            out_shape=[jax.ShapeDtypeStruct(tile_shape, jnp.float32)] * steps,
            in_specs=[SMEM, VMEM],
            out_specs=[VMEM] * steps,
            compiler_params=SMALL,
            name="spread",
        )(plan, outgoing[0])
        return placed(False, exchanged(blocks))

    if not apart:
        swapped = lax.all_to_all(outgoing[0], "dp", split_axis=0, concat_axis=0, tiled=True)
        return placed(False, [swapped])
    return lax.cond(plan[0] > 0, in_full, lambda: placed(True, exchanged(outgoing[1:])))


def solution(mesh):
    in_specs = (
        P("pipe", None, "dp", "tensor"),
        P("pipe", None, "dp", "tensor"),
        P("pipe", "dp", "tensor", None, None, None, None),
        P("pipe", None, "tensor", None, None, None),
        P("pipe", "tensor", None),
    )
    out_specs = P("pipe", "tensor", "dp", None)
    return jax.shard_map(
        functools.partial(body, mesh),
        mesh=mesh,
        in_specs=in_specs,
        out_specs=out_specs,
        check_vma=False,
    )
```

```python
import functools

import jax
import jax.numpy as jnp
from jax import lax
from jax.experimental import pallas as pl
from jax.experimental.pallas import tpu as pltpu
from jax.sharding import PartitionSpec as P

VMEM = pl.BlockSpec(memory_space=pltpu.VMEM)
SMEM = pl.BlockSpec(memory_space=pltpu.SMEM)
ANY = pl.BlockSpec(memory_space=pl.ANY)
MOST_STEPS = 8
ROUNDS = {4: [(2, 3, 1, 0), (3, 2, 0, 1), (1, 0, 3, 2)]}
SMALL = pltpu.CompilerParams(vmem_limit_bytes=4 << 20)


def in_hbm(value):
    return pltpu.with_memory_space_constraint(value, pltpu.HBM)


def column(index, edge):
    return pl.ds(pl.multiple_of(index * edge, edge), edge)


def rounds(replicas):
    shifts = [
        tuple((one + step) % replicas for one in range(replicas)) for step in range(1, replicas)
    ]
    return ROUNDS.get(replicas, shifts)


def step_table(replicas):
    table = []
    for source in range(replicas):
        steps = [0] * replicas
        for step, targets in reversed(list(enumerate(rounds(replicas), 1))):
            steps[targets[source]] = step
        table.append(sum(step << 4 * target for target, step in enumerate(steps)))
    return table


def plan_sizes(tiles, steps):
    return 1, 1 + tiles, 1 + 2 * tiles, 1 + 2 * tiles + steps, 1 + 2 * tiles + 2 * steps


def pick(shifts, apart, columns, picks, owners, activations, errors, picked, plan, *refs):
    cuts, (read, seen, copied) = refs[:shifts], refs[shifts:]
    replica, group_at = lax.axis_index("dp"), lax.axis_index("tensor")
    groups, slots, replicas = picks.shape[2], picks.shape[3], picks.shape[-1]
    edge = picked.shape[1]
    tiles = [
        (lax.rem(group_at + shift, groups), slot) for shift in range(groups) for slot in range(slots)
    ]
    reads = []
    for at, (group, slot) in enumerate(tiles):
        block = picks[0, 0, group, slot, 0, replica]
        reads.append(
            pltpu.make_async_copy(
                activations.at[0, :, :, column(block, edge)], read.at[at], copied.at[at]
            )
        )
    for shift, cut in enumerate(cuts):
        other = lax.rem(group_at + groups - shift - 1, groups)
        reads.append(
            pltpu.make_async_copy(errors.at[0, 0, 0, other], cut, copied.at[len(tiles) + shift])
        )
    for copy in reads:
        copy.start()

    owned = owners.shape[-1] // replicas
    per_group = columns // groups
    steps = len(rounds(replicas)) + 1 if apart else replicas
    to_step, to_column, to_row, to_col, end = plan_sizes(len(tiles), steps)
    table = step_table(replicas) if apart else []
    mine = jnp.int32(0)
    for source, packed in enumerate(table):
        mine = jnp.where(replica == source, packed, mine)
    lane = lax.broadcasted_iota(jnp.int32, plan.shape, 1)
    planned = jnp.where((lane >= to_row) & (lane < end), -1, 0)

    for at, (group, slot) in enumerate(tiles):
        row = owners[0, 0, picks[0, 0, group, slot, 0, replica]]
        owner = jnp.int32(0)
        for one in range(1, replicas):
            owner += (row >= one * owned).astype(jnp.int32)
        step = (mine >> 4 * owner) & 15 if apart else owner
        planned = jnp.where(lane == to_step + at, step, planned)
        planned = jnp.where(lane == to_column + at, picks[0, 0, group, slot, 1, replica], planned)

    for origin in range(replicas):
        place_row, place_col = jnp.int32(-1), jnp.int32(0)
        for group, slot in tiles:
            row = owners[0, 0, picks[0, 0, group, slot, 0, origin]] - replica * owned
            here = (row >= 0) & (row < owned)
            place_row = jnp.where(here, row, place_row)
            place_col = jnp.where(
                here, picks[0, 0, group, slot, 1, origin] + group * per_group, place_col
            )
        step = (jnp.int32(table[origin]) >> 4 * replica) & 15 if apart else origin
        planned = jnp.where(lane == to_row + step, place_row, planned)
        planned = jnp.where(lane == to_col + step, place_col, planned)

    meets = jnp.int32(0)
    if apart:
        spots = [
            picks[0, 0, group, slot, 0, origin] * columns
            + picks[0, 0, group, slot, 1, origin]
            + group * per_group
            for group, slot in tiles
            for origin in range(replicas)
        ]
        for spot in spots:
            seen[spot] = 0
        for spot in spots:
            meets = meets | seen[spot]
            seen[spot] = 1
    plan[...] = jnp.where(lane == 0, meets, planned)

    for at, copy in enumerate(reads):
        copy.wait()
        if at < len(tiles):
            picked[at] = read[at].reshape(-1, edge).T


def clear(after, strip, zeros, cleared):
    zeros[...] = jnp.zeros_like(zeros)
    rows = zeros.shape[0]
    writes = [
        pltpu.make_async_copy(zeros, strip.at[0, 0, pl.ds(part * rows, rows)], cleared.at[part])
        for part in range(strip.shape[2] // rows)
    ]
    for write in writes:
        write.start()
    for write in writes:
        write.wait()


def multiply(groups, apart, to_step, to_column, plan, picked, error, *refs):
    returned, carried, outs = refs[:groups], refs[groups : 2 * groups - 1], refs[2 * groups - 1 :]
    mine = lax.axis_index("tensor")
    slots, (edge, tokens) = error.shape[4], picked.shape[1:]
    for shift in range(groups):
        for slot in range(slots):
            at = shift * slots + slot
            right = returned[shift][0, :, :, column(plan[0, to_column + at], edge)]
            extra = error[0, 0, 0, mine, slot] if shift == 0 else carried[shift - 1][slot]
            tile = jnp.dot(
                picked[at], right.reshape(tokens, edge), preferred_element_type=jnp.float32
            )
            tile = tile + extra.astype(jnp.float32)
            step = plan[0, to_step + at]
            if apart:
                outs[0][at] = tile
                store(tile.astype(jnp.bfloat16), step, outs[1:])
            else:
                outs[0][step] = tile


def store(tile, step, buffers):
    for at, buffer in enumerate(buffers):

        @pl.when(step == at)
        def _():
            buffer[...] = tile


def spread(to_step, plan, tiles, *buffers):
    for at in range(tiles.shape[0]):
        store(tiles[at], plan[0, to_step + at], buffers)


def place(count, alone, to_row, to_col, plan, *refs):
    blocks, strip, staged, sent = refs[:count], refs[-3], refs[-2], refs[-1]
    steps, edge = staged.shape[0], staged.shape[-1]

    def meets(one, other):
        return (plan[0, to_row + one] == plan[0, to_row + other]) & (
            plan[0, to_col + one] == plan[0, to_col + other]
        )

    def block_of(step):
        return blocks[0][step] if count == 1 else blocks[step][...]

    def first_of(step):
        first = plan[0, to_row + step] >= 0
        for earlier in range(0 if alone else step):
            first = first & jnp.logical_not(meets(earlier, step))
        return first

    def write_of(step):
        row, col = plan[0, to_row + step], plan[0, to_col + step]
        return pltpu.make_async_copy(
            blocks[step] if alone else staged.at[step],
            strip.at[0, 0, column(row, edge), column(col, edge)],
            sent.at[step],
        )

    for step in range(steps):

        @pl.when(first_of(step))
        def _():
            if not alone:
                total = block_of(step)
                for later in range(step + 1, steps):
                    total = total + jnp.where(meets(step, later), block_of(later), 0.0)
                staged[step] = total.astype(staged.dtype)
            write_of(step).start()

    for step in range(steps):

        @pl.when(first_of(step))
        def _():
            write_of(step).wait()


def body(mesh, activations, cotangent, error_tiles, tile_picks, row_owners):
    sections, replicas, groups = mesh.shape["pipe"], mesh.shape["dp"], mesh.shape["tensor"]
    edge = error_tiles.shape[-1]
    slots = tile_picks.shape[4]
    micro, tokens = activations.shape[1:3]
    width = cotangent.shape[-1] * groups
    strip_rows = row_owners.shape[-1] // replicas * edge
    picks = jnp.transpose(tile_picks, (0, 2, 3, 4, 5, 1))

    returned = []
    for shift in range(groups):
        pairs = [
            (
                (section + 1) % sections * groups + (group + shift) % groups,
                section * groups + group,
            )
            for section in range(sections)
            for group in range(groups)
        ]
        returned.append(lax.ppermute(cotangent, ("pipe", "tensor"), pairs))
    apart = replicas <= MOST_STEPS
    tiles, shifts = groups * slots, groups - 1
    steps = len(rounds(replicas)) + 1 if apart else replicas
    picked, plan, *errors = pl.pallas_call(
        functools.partial(pick, shifts, apart, width // edge),
        out_shape=[
            pltpu.VMEM((tiles, edge, micro * tokens), activations.dtype),
            pltpu.VMEM((1, -(-plan_sizes(tiles, steps)[-1] // 128) * 128), jnp.int32),
        ]
        + [pltpu.VMEM((slots, edge, edge), error_tiles.dtype)] * shifts,
        in_specs=[SMEM, SMEM, ANY, ANY],
        out_specs=[VMEM] * (2 + shifts),
        scratch_shapes=[
            pltpu.VMEM((tiles, micro, tokens, edge), activations.dtype),
            pltpu.SMEM((row_owners.shape[-1] * (width // edge),), jnp.int32),
            pltpu.SemaphoreType.DMA((tiles + shifts,)),
        ],
        compiler_params=SMALL,
        name="pick",
    )(in_hbm(picks), in_hbm(row_owners), in_hbm(activations), in_hbm(error_tiles))
    carried = [
        lax.ppermute(
            error, "tensor", [((group + shift + 1) % groups, group) for group in range(groups)]
        )
        for shift, error in enumerate(errors)
    ]

    zero_rows = min(strip_rows, 256)
    strip_shape = (1, 1, strip_rows, width)
    cleared = pl.pallas_call(
        clear,
        out_shape=pltpu.HBM(strip_shape, jnp.bfloat16),
        in_specs=[ANY],
        out_specs=pl.BlockSpec(memory_space=pltpu.HBM),
        scratch_shapes=[
            pltpu.VMEM((zero_rows, width), jnp.bfloat16),
            pltpu.SemaphoreType.DMA((strip_rows // zero_rows,)),
        ],
        compiler_params=SMALL,
        cost_estimate=pl.CostEstimate(
            flops=0, bytes_accessed=2 * strip_rows * width, transcendentals=0
        ),
        name="clear",
    )(picked)

    to_step, to_column, to_row, to_col, _ = plan_sizes(tiles, steps)
    tile_shape = (edge, edge)
    if apart:
        out_shape = [jax.ShapeDtypeStruct((tiles,) + tile_shape, jnp.float32)]
        out_shape += [jax.ShapeDtypeStruct(tile_shape, jnp.bfloat16)] * steps
    else:
        out_shape = [jax.ShapeDtypeStruct((replicas,) + tile_shape, jnp.float32)]
    outgoing = pl.pallas_call(
        functools.partial(multiply, groups, apart, to_step, to_column),
        out_shape=out_shape,
        in_specs=[VMEM] * (2 * groups + 2),
        out_specs=[VMEM] * len(out_shape),
        compiler_params=SMALL,
        name="multiply",
    )(plan, picked, error_tiles, *returned, *carried)

    def placed(alone, incoming):
        return pl.pallas_call(
            functools.partial(place, len(incoming), alone, to_row, to_col),
            out_shape=jax.ShapeDtypeStruct(strip_shape, jnp.bfloat16),
            in_specs=[VMEM] * (1 + len(incoming)) + [ANY],
            out_specs=ANY,
            scratch_shapes=[
                pltpu.VMEM((steps,) + tile_shape, jnp.bfloat16),
                pltpu.SemaphoreType.DMA((steps,)),
            ],
            input_output_aliases={1 + len(incoming): 0},
            compiler_params=SMALL,
            name="place",
        )(plan, *incoming, cleared)

    def exchanged(blocks):
        moved = [
            lax.ppermute(block, "dp", list(enumerate(targets)))
            for block, targets in zip(blocks[1:], rounds(replicas))
        ]
        return [blocks[0], *moved]

    def in_full():
        blocks = pl.pallas_call(
            functools.partial(spread, to_step),
            out_shape=[jax.ShapeDtypeStruct(tile_shape, jnp.float32)] * steps,
            in_specs=[VMEM, VMEM],
            out_specs=[VMEM] * steps,
            compiler_params=SMALL,
            name="spread",
        )(plan, outgoing[0])
        return placed(False, exchanged(blocks))

    if not apart:
        swapped = lax.all_to_all(outgoing[0], "dp", split_axis=0, concat_axis=0, tiled=True)
        return placed(False, [swapped])
    return lax.cond(plan[0, 0] > 0, in_full, lambda: placed(True, exchanged(outgoing[1:])))


def solution(mesh):
    in_specs = (
        P("pipe", None, "dp", "tensor"),
        P("pipe", None, "dp", "tensor"),
        P("pipe", "dp", "tensor", None, None, None, None),
        P("pipe", None, "tensor", None, None, None),
        P("pipe", "tensor", None),
    )
    out_specs = P("pipe", "tensor", "dp", None)
    return jax.shard_map(
        functools.partial(body, mesh),
        mesh=mesh,
        in_specs=in_specs,
        out_specs=out_specs,
        check_vma=False,
    )
```

```python
import functools

import jax
import jax.numpy as jnp
from jax import lax
from jax.experimental import pallas as pl
from jax.experimental.pallas import tpu as pltpu
from jax.sharding import PartitionSpec as P

VMEM = pl.BlockSpec(memory_space=pltpu.VMEM)
SMEM = pl.BlockSpec(memory_space=pltpu.SMEM)
ANY = pl.BlockSpec(memory_space=pl.ANY)
MOST_STEPS = 8
ROUNDS = {4: [(2, 3, 1, 0), (3, 2, 0, 1), (1, 0, 3, 2)]}
SMALL = pltpu.CompilerParams(vmem_limit_bytes=4 << 20)


def in_hbm(value):
    return pltpu.with_memory_space_constraint(value, pltpu.HBM)


def column(index, edge):
    return pl.ds(pl.multiple_of(index * edge, edge), edge)


def rounds(replicas):
    shifts = [
        tuple((one + step) % replicas for one in range(replicas)) for step in range(1, replicas)
    ]
    return ROUNDS.get(replicas, shifts)


def step_table(replicas):
    table = []
    for source in range(replicas):
        steps = [0] * replicas
        for step, targets in reversed(list(enumerate(rounds(replicas), 1))):
            steps[targets[source]] = step
        table.append(sum(step << 4 * target for target, step in enumerate(steps)))
    return table


def plan_sizes(tiles, steps):
    return 1, 1 + tiles, 1 + 2 * tiles, 1 + 2 * tiles + steps, 1 + 2 * tiles + 2 * steps


def pick(shifts, apart, columns, picks, owners, activations, errors, picked, plan, *refs):
    cuts, (read, seen, copied) = refs[:shifts], refs[shifts:]
    replica, group_at = lax.axis_index("dp"), lax.axis_index("tensor")
    groups, slots, replicas = picks.shape[2], picks.shape[3], picks.shape[-1]
    edge = picked.shape[1]
    tiles = [
        (lax.rem(group_at + shift, groups), slot) for shift in range(groups) for slot in range(slots)
    ]
    reads = []
    for at, (group, slot) in enumerate(tiles):
        block = picks[0, 0, group, slot, 0, replica]
        reads.append(
            pltpu.make_async_copy(
                activations.at[0, :, :, column(block, edge)], read.at[at], copied.at[at]
            )
        )
    for shift, cut in enumerate(cuts):
        other = lax.rem(group_at + groups - shift - 1, groups)
        reads.append(
            pltpu.make_async_copy(errors.at[0, 0, 0, other], cut, copied.at[len(tiles) + shift])
        )
    for copy in reads:
        copy.start()

    owned = owners.shape[-1] // replicas
    per_group = columns // groups
    steps = len(rounds(replicas)) + 1 if apart else replicas
    to_step, to_column, to_row, to_col, end = plan_sizes(len(tiles), steps)
    table = step_table(replicas) if apart else []
    mine = jnp.int32(0)
    for source, packed in enumerate(table):
        mine = jnp.where(replica == source, packed, mine)
    lane = lax.broadcasted_iota(jnp.int32, plan.shape, 1)
    planned = jnp.where((lane >= to_row) & (lane < end), -1, 0)

    for at, (group, slot) in enumerate(tiles):
        row = owners[0, 0, picks[0, 0, group, slot, 0, replica]]
        owner = jnp.int32(0)
        for one in range(1, replicas):
            owner += (row >= one * owned).astype(jnp.int32)
        step = (mine >> 4 * owner) & 15 if apart else owner
        planned = jnp.where(lane == to_step + at, step, planned)
        planned = jnp.where(lane == to_column + at, picks[0, 0, group, slot, 1, replica], planned)

    for origin in range(replicas):
        place_row, place_col = jnp.int32(-1), jnp.int32(0)
        for group, slot in tiles:
            row = owners[0, 0, picks[0, 0, group, slot, 0, origin]] - replica * owned
            here = (row >= 0) & (row < owned)
            place_row = jnp.where(here, row, place_row)
            place_col = jnp.where(
                here, picks[0, 0, group, slot, 1, origin] + group * per_group, place_col
            )
        step = (jnp.int32(table[origin]) >> 4 * replica) & 15 if apart else origin
        planned = jnp.where(lane == to_row + step, place_row, planned)
        planned = jnp.where(lane == to_col + step, place_col, planned)

    meets = jnp.int32(0)
    if apart:
        spots = [
            picks[0, 0, group, slot, 0, origin] * columns
            + picks[0, 0, group, slot, 1, origin]
            + group * per_group
            for group, slot in tiles
            for origin in range(replicas)
        ]
        for spot in spots:
            seen[spot] = 0
        for spot in spots:
            meets = meets | seen[spot]
            seen[spot] = 1
    plan[...] = jnp.where(lane == 0, meets, planned)

    for at, copy in enumerate(reads):
        copy.wait()
        if at < len(tiles):
            picked[at] = read[at].reshape(-1, edge).T


def clear(after, strip, zeros, cleared):
    zeros[...] = jnp.zeros_like(zeros)
    rows = zeros.shape[0]
    writes = [
        pltpu.make_async_copy(zeros, strip.at[0, 0, pl.ds(part * rows, rows)], cleared.at[part])
        for part in range(strip.shape[2] // rows)
    ]
    for write in writes:
        write.start()
    for write in writes:
        write.wait()


def multiply(groups, apart, to_step, to_column, plan, picked, error, *refs):
    returned, carried, outs = refs[:groups], refs[groups : 2 * groups - 1], refs[2 * groups - 1 :]
    mine = lax.axis_index("tensor")
    slots, (edge, tokens) = error.shape[4], picked.shape[1:]
    for shift in range(groups):
        for slot in range(slots):
            at = shift * slots + slot
            right = returned[shift][0, :, :, column(plan[0, to_column + at], edge)]
            extra = error[0, 0, 0, mine, slot] if shift == 0 else carried[shift - 1][slot]
            tile = jnp.dot(
                picked[at], right.reshape(tokens, edge), preferred_element_type=jnp.float32
            )
            tile = tile + extra.astype(jnp.float32)
            step = plan[0, to_step + at]
            if apart:
                outs[0][at] = tile
                store(tile.astype(jnp.bfloat16), step, outs[1:])
            else:
                outs[0][step] = tile


def store(tile, step, buffers):
    for at, buffer in enumerate(buffers):

        @pl.when(step == at)
        def _():
            buffer[...] = tile


def spread(to_step, plan, tiles, *buffers):
    for at in range(tiles.shape[0]):
        store(tiles[at], plan[0, to_step + at], buffers)


def place(count, alone, to_row, to_col, plan, *refs):
    blocks, strip, staged, sent = refs[:count], refs[-3], refs[-2], refs[-1]
    steps, edge = staged.shape[0], staged.shape[-1]

    rows = [plan[0, to_row + step] for step in range(steps)]
    cols = [plan[0, to_col + step] for step in range(steps)]

    def meets(one, other):
        return (rows[one] == rows[other]) & (cols[one] == cols[other])

    def block_of(step):
        return blocks[0][step] if count == 1 else blocks[step][...]

    def first_of(step):
        first = rows[step] >= 0
        for earlier in range(0 if alone else step):
            first = first & jnp.logical_not(meets(earlier, step))
        return first

    def write_of(step):
        return pltpu.make_async_copy(
            blocks[step] if alone else staged.at[step],
            strip.at[0, 0, column(rows[step], edge), column(cols[step], edge)],
            sent.at[step],
        )

    for step in range(steps):

        @pl.when(first_of(step))
        def _():
            if not alone:
                total = block_of(step)
                for later in range(step + 1, steps):
                    total = total + jnp.where(meets(step, later), block_of(later), 0.0)
                staged[step] = total.astype(staged.dtype)
            write_of(step).start()

    for step in range(steps):

        @pl.when(first_of(step))
        def _():
            write_of(step).wait()


def body(mesh, activations, cotangent, error_tiles, tile_picks, row_owners):
    sections, replicas, groups = mesh.shape["pipe"], mesh.shape["dp"], mesh.shape["tensor"]
    edge = error_tiles.shape[-1]
    slots = tile_picks.shape[4]
    micro, tokens = activations.shape[1:3]
    width = cotangent.shape[-1] * groups
    strip_rows = row_owners.shape[-1] // replicas * edge
    picks = jnp.transpose(tile_picks, (0, 2, 3, 4, 5, 1))

    returned = []
    for shift in range(groups):
        pairs = [
            (
                (section + 1) % sections * groups + (group + shift) % groups,
                section * groups + group,
            )
            for section in range(sections)
            for group in range(groups)
        ]
        returned.append(lax.ppermute(cotangent, ("pipe", "tensor"), pairs))
    apart = replicas <= MOST_STEPS
    tiles, shifts = groups * slots, groups - 1
    steps = len(rounds(replicas)) + 1 if apart else replicas
    picked, plan, *errors = pl.pallas_call(
        functools.partial(pick, shifts, apart, width // edge),
        out_shape=[
            pltpu.VMEM((tiles, edge, micro * tokens), activations.dtype),
            pltpu.VMEM((1, -(-plan_sizes(tiles, steps)[-1] // 128) * 128), jnp.int32),
        ]
        + [pltpu.VMEM((slots, edge, edge), error_tiles.dtype)] * shifts,
        in_specs=[SMEM, SMEM, ANY, ANY],
        out_specs=[VMEM] * (2 + shifts),
        scratch_shapes=[
            pltpu.VMEM((tiles, micro, tokens, edge), activations.dtype),
            pltpu.SMEM((row_owners.shape[-1] * (width // edge),), jnp.int32),
            pltpu.SemaphoreType.DMA((tiles + shifts,)),
        ],
        compiler_params=SMALL,
        name="pick",
    )(in_hbm(picks), in_hbm(row_owners), in_hbm(activations), in_hbm(error_tiles))
    carried = [
        lax.ppermute(
            error, "tensor", [((group + shift + 1) % groups, group) for group in range(groups)]
        )
        for shift, error in enumerate(errors)
    ]

    zero_rows = min(strip_rows, 256)
    strip_shape = (1, 1, strip_rows, width)
    cleared = pl.pallas_call(
        clear,
        out_shape=pltpu.HBM(strip_shape, jnp.bfloat16),
        in_specs=[ANY],
        out_specs=pl.BlockSpec(memory_space=pltpu.HBM),
        scratch_shapes=[
            pltpu.VMEM((zero_rows, width), jnp.bfloat16),
            pltpu.SemaphoreType.DMA((strip_rows // zero_rows,)),
        ],
        compiler_params=SMALL,
        cost_estimate=pl.CostEstimate(
            flops=0, bytes_accessed=2 * strip_rows * width, transcendentals=0
        ),
        name="clear",
    )(picked)

    to_step, to_column, to_row, to_col, _ = plan_sizes(tiles, steps)
    tile_shape = (edge, edge)
    if apart:
        out_shape = [jax.ShapeDtypeStruct((tiles,) + tile_shape, jnp.float32)]
        out_shape += [jax.ShapeDtypeStruct(tile_shape, jnp.bfloat16)] * steps
    else:
        out_shape = [jax.ShapeDtypeStruct((replicas,) + tile_shape, jnp.float32)]
    outgoing = pl.pallas_call(
        functools.partial(multiply, groups, apart, to_step, to_column),
        out_shape=out_shape,
        in_specs=[VMEM] * (2 * groups + 2),
        out_specs=[VMEM] * len(out_shape),
        compiler_params=SMALL,
        name="multiply",
    )(plan, picked, error_tiles, *returned, *carried)

    def placed(alone, incoming):
        return pl.pallas_call(
            functools.partial(place, len(incoming), alone, to_row, to_col),
            out_shape=jax.ShapeDtypeStruct(strip_shape, jnp.bfloat16),
            in_specs=[VMEM] * (1 + len(incoming)) + [ANY],
            out_specs=ANY,
            scratch_shapes=[
                pltpu.VMEM((steps,) + tile_shape, jnp.bfloat16),
                pltpu.SemaphoreType.DMA((steps,)),
            ],
            input_output_aliases={1 + len(incoming): 0},
            compiler_params=SMALL,
            name="place",
        )(plan, *incoming, cleared)

    def exchanged(blocks):
        moved = [
            lax.ppermute(block, "dp", list(enumerate(targets)))
            for block, targets in zip(blocks[1:], rounds(replicas))
        ]
        return [blocks[0], *moved]

    def in_full():
        blocks = pl.pallas_call(
            functools.partial(spread, to_step),
            out_shape=[jax.ShapeDtypeStruct(tile_shape, jnp.float32)] * steps,
            in_specs=[VMEM, VMEM],
            out_specs=[VMEM] * steps,
            compiler_params=SMALL,
            name="spread",
        )(plan, outgoing[0])
        return placed(False, exchanged(blocks))

    if not apart:
        swapped = lax.all_to_all(outgoing[0], "dp", split_axis=0, concat_axis=0, tiled=True)
        return placed(False, [swapped])
    return lax.cond(plan[0, 0] > 0, in_full, lambda: placed(True, exchanged(outgoing[1:])))


def solution(mesh):
    in_specs = (
        P("pipe", None, "dp", "tensor"),
        P("pipe", None, "dp", "tensor"),
        P("pipe", "dp", "tensor", None, None, None, None),
        P("pipe", None, "tensor", None, None, None),
        P("pipe", "tensor", None),
    )
    out_specs = P("pipe", "tensor", "dp", None)
    return jax.shard_map(
        functools.partial(body, mesh),
        mesh=mesh,
        in_specs=in_specs,
        out_specs=out_specs,
        check_vma=False,
    )
```

```python
import functools

import jax
import jax.numpy as jnp
from jax import lax
from jax.experimental import pallas as pl
from jax.experimental.pallas import tpu as pltpu
from jax.sharding import PartitionSpec as P

VMEM = pl.BlockSpec(memory_space=pltpu.VMEM)
SMEM = pl.BlockSpec(memory_space=pltpu.SMEM)
ANY = pl.BlockSpec(memory_space=pl.ANY)
MOST_STEPS = 8
ROUNDS = {4: [(2, 3, 1, 0), (3, 2, 0, 1), (1, 0, 3, 2)]}
SMALL = pltpu.CompilerParams(vmem_limit_bytes=4 << 20)


def in_hbm(value):
    return pltpu.with_memory_space_constraint(value, pltpu.HBM)


def column(index, edge):
    return pl.ds(pl.multiple_of(index * edge, edge), edge)


def rounds(replicas):
    shifts = [
        tuple((one + step) % replicas for one in range(replicas)) for step in range(1, replicas)
    ]
    return ROUNDS.get(replicas, shifts)


def step_table(replicas):
    table = []
    for source in range(replicas):
        steps = [0] * replicas
        for step, targets in reversed(list(enumerate(rounds(replicas), 1))):
            steps[targets[source]] = step
        table.append(sum(step << 4 * target for target, step in enumerate(steps)))
    return table


def plan_sizes(tiles, steps):
    return 1, 1 + tiles, 1 + 2 * tiles, 1 + 2 * tiles + steps, 1 + 2 * tiles + 2 * steps


def pick(shifts, apart, columns, picks, owners, activations, errors, picked, plan, *refs):
    cuts, (read, seen, copied) = refs[:shifts], refs[shifts:]
    replica, group_at = lax.axis_index("dp"), lax.axis_index("tensor")
    groups, slots, replicas = picks.shape[2], picks.shape[3], picks.shape[-1]
    edge = picked.shape[1]
    tiles = [
        (lax.rem(group_at + shift, groups), slot) for shift in range(groups) for slot in range(slots)
    ]
    reads = []
    for at, (group, slot) in enumerate(tiles):
        block = picks[0, 0, group, slot, 0, replica]
        reads.append(
            pltpu.make_async_copy(
                activations.at[0, :, :, column(block, edge)], read.at[at], copied.at[at]
            )
        )
    for shift, cut in enumerate(cuts):
        other = lax.rem(group_at + groups - shift - 1, groups)
        reads.append(
            pltpu.make_async_copy(errors.at[0, 0, 0, other], cut, copied.at[len(tiles) + shift])
        )
    for copy in reads:
        copy.start()

    owned = owners.shape[-1] // replicas
    per_group = columns // groups
    steps = len(rounds(replicas)) + 1 if apart else replicas
    to_step, to_column, to_row, to_col, end = plan_sizes(len(tiles), steps)
    table = step_table(replicas) if apart else []
    mine = jnp.int32(0)
    for source, packed in enumerate(table):
        mine = jnp.where(replica == source, packed, mine)
    lane = lax.broadcasted_iota(jnp.int32, plan.shape, 1)
    planned = jnp.where((lane >= to_row) & (lane < end), -1, 0)

    for at, (group, slot) in enumerate(tiles):
        row = owners[0, 0, picks[0, 0, group, slot, 0, replica]]
        owner = jnp.int32(0)
        for one in range(1, replicas):
            owner += (row >= one * owned).astype(jnp.int32)
        step = (mine >> 4 * owner) & 15 if apart else owner
        planned = jnp.where(lane == to_step + at, step, planned)
        planned = jnp.where(lane == to_column + at, picks[0, 0, group, slot, 1, replica], planned)

    for origin in range(replicas):
        place_row, place_col = jnp.int32(-1), jnp.int32(0)
        for group, slot in tiles:
            row = owners[0, 0, picks[0, 0, group, slot, 0, origin]] - replica * owned
            here = (row >= 0) & (row < owned)
            place_row = jnp.where(here, row, place_row)
            place_col = jnp.where(
                here, picks[0, 0, group, slot, 1, origin] + group * per_group, place_col
            )
        step = (jnp.int32(table[origin]) >> 4 * replica) & 15 if apart else origin
        planned = jnp.where(lane == to_row + step, place_row, planned)
        planned = jnp.where(lane == to_col + step, place_col, planned)

    meets = jnp.int32(0)
    if apart:
        spots = [
            picks[0, 0, group, slot, 0, origin] * columns
            + picks[0, 0, group, slot, 1, origin]
            + group * per_group
            for group, slot in tiles
            for origin in range(replicas)
        ]
        for spot in spots:
            seen[spot] = 0
        for spot in spots:
            meets = meets | seen[spot]
            seen[spot] = 1
    plan[...] = jnp.where(lane == 0, meets, planned)

    for at, copy in enumerate(reads):
        copy.wait()
        if at < len(tiles):
            picked[at] = read[at].reshape(-1, edge).T


def clear(after, strip, zeros, cleared):
    zeros[...] = jnp.zeros_like(zeros)
    rows = zeros.shape[0]
    writes = [
        pltpu.make_async_copy(zeros, strip.at[0, 0, pl.ds(part * rows, rows)], cleared.at[part])
        for part in range(strip.shape[2] // rows)
    ]
    for write in writes:
        write.start()
    for write in writes:
        write.wait()


def multiply(groups, apart, to_step, to_column, plan, picked, error, *refs):
    returned, carried, outs = refs[:groups], refs[groups : 2 * groups - 1], refs[2 * groups - 1 :]
    mine = lax.axis_index("tensor")
    slots, (edge, tokens) = error.shape[4], picked.shape[1:]
    count = groups * slots
    meet = plan[0, 0] > 0
    columns = [plan[0, to_column + at] for at in range(count)]
    steps = [plan[0, to_step + at] for at in range(count)]
    tiles = []
    for shift in range(groups):
        for slot in range(slots):
            at = shift * slots + slot
            right = returned[shift][0, :, :, column(columns[at], edge)].reshape(tokens, edge)
            extra = error[0, 0, 0, mine, slot] if shift == 0 else carried[shift - 1][slot]
            tile = jnp.dot(picked[at], right, preferred_element_type=jnp.float32)
            tiles.append(tile + extra.astype(jnp.float32))
    if not apart:
        for step, tile in zip(steps, tiles):
            outs[0][step] = tile
        return

    def store(buffers):
        for step, tile in zip(steps, tiles):
            for at, buffer in enumerate(buffers):

                @pl.when(step == at)
                def _():
                    buffer[...] = tile.astype(buffer.dtype)

    @pl.when(meet)
    def _():
        store(outs[: len(outs) // 2])

    @pl.when(jnp.logical_not(meet))
    def _():
        store(outs[len(outs) // 2 :])


def place(count, alone, to_row, to_col, plan, *refs):
    blocks, strip, staged, sent = refs[:count], refs[-3], refs[-2], refs[-1]
    steps, edge = staged.shape[0], staged.shape[-1]

    rows = [plan[0, to_row + step] for step in range(steps)]
    cols = [plan[0, to_col + step] for step in range(steps)]

    def meets(one, other):
        return (rows[one] == rows[other]) & (cols[one] == cols[other])

    def block_of(step):
        return blocks[0][step] if count == 1 else blocks[step][...]

    def first_of(step):
        first = rows[step] >= 0
        for earlier in range(0 if alone else step):
            first = first & jnp.logical_not(meets(earlier, step))
        return first

    def write_of(step):
        return pltpu.make_async_copy(
            blocks[step] if alone else staged.at[step],
            strip.at[0, 0, column(rows[step], edge), column(cols[step], edge)],
            sent.at[step],
        )

    for step in range(steps):

        @pl.when(first_of(step))
        def _():
            if not alone:
                total = block_of(step)
                for later in range(step + 1, steps):
                    total = total + jnp.where(meets(step, later), block_of(later), 0.0)
                staged[step] = total.astype(staged.dtype)
            write_of(step).start()

    for step in range(steps):

        @pl.when(first_of(step))
        def _():
            write_of(step).wait()


def body(mesh, activations, cotangent, error_tiles, tile_picks, row_owners):
    sections, replicas, groups = mesh.shape["pipe"], mesh.shape["dp"], mesh.shape["tensor"]
    edge = error_tiles.shape[-1]
    slots = tile_picks.shape[4]
    micro, tokens = activations.shape[1:3]
    width = cotangent.shape[-1] * groups
    strip_rows = row_owners.shape[-1] // replicas * edge
    picks = jnp.transpose(tile_picks, (0, 2, 3, 4, 5, 1))

    returned = []
    for shift in range(groups):
        pairs = [
            (
                (section + 1) % sections * groups + (group + shift) % groups,
                section * groups + group,
            )
            for section in range(sections)
            for group in range(groups)
        ]
        returned.append(lax.ppermute(cotangent, ("pipe", "tensor"), pairs))
    apart = replicas <= MOST_STEPS
    tiles, shifts = groups * slots, groups - 1
    steps = len(rounds(replicas)) + 1 if apart else replicas
    picked, plan, *errors = pl.pallas_call(
        functools.partial(pick, shifts, apart, width // edge),
        out_shape=[
            pltpu.VMEM((tiles, edge, micro * tokens), activations.dtype),
            pltpu.VMEM((1, -(-plan_sizes(tiles, steps)[-1] // 128) * 128), jnp.int32),
        ]
        + [pltpu.VMEM((slots, edge, edge), error_tiles.dtype)] * shifts,
        in_specs=[SMEM, SMEM, ANY, ANY],
        out_specs=[VMEM] * (2 + shifts),
        scratch_shapes=[
            pltpu.VMEM((tiles, micro, tokens, edge), activations.dtype),
            pltpu.SMEM((row_owners.shape[-1] * (width // edge),), jnp.int32),
            pltpu.SemaphoreType.DMA((tiles + shifts,)),
        ],
        compiler_params=SMALL,
        name="pick",
    )(in_hbm(picks), in_hbm(row_owners), in_hbm(activations), in_hbm(error_tiles))
    carried = [
        lax.ppermute(
            error, "tensor", [((group + shift + 1) % groups, group) for group in range(groups)]
        )
        for shift, error in enumerate(errors)
    ]

    zero_rows = min(strip_rows, 256)
    strip_shape = (1, 1, strip_rows, width)
    cleared = pl.pallas_call(
        clear,
        out_shape=pltpu.HBM(strip_shape, jnp.bfloat16),
        in_specs=[ANY],
        out_specs=pl.BlockSpec(memory_space=pltpu.HBM),
        scratch_shapes=[
            pltpu.VMEM((zero_rows, width), jnp.bfloat16),
            pltpu.SemaphoreType.DMA((strip_rows // zero_rows,)),
        ],
        compiler_params=SMALL,
        cost_estimate=pl.CostEstimate(
            flops=0, bytes_accessed=2 * strip_rows * width, transcendentals=0
        ),
        name="clear",
    )(picked)

    to_step, to_column, to_row, to_col, _ = plan_sizes(tiles, steps)
    tile_shape = (edge, edge)
    if apart:
        out_shape = [
            jax.ShapeDtypeStruct(tile_shape, dtype)
            for dtype in (jnp.float32, jnp.bfloat16)
            for step in range(steps)
        ]
    else:
        out_shape = [jax.ShapeDtypeStruct((replicas,) + tile_shape, jnp.float32)]
    outgoing = pl.pallas_call(
        functools.partial(multiply, groups, apart, to_step, to_column),
        out_shape=out_shape,
        in_specs=[VMEM] * (2 * groups + 2),
        out_specs=[VMEM] * len(out_shape),
        compiler_params=SMALL,
        name="multiply",
    )(plan, picked, error_tiles, *returned, *carried)

    def placed(alone, incoming):
        return pl.pallas_call(
            functools.partial(place, len(incoming), alone, to_row, to_col),
            out_shape=jax.ShapeDtypeStruct(strip_shape, jnp.bfloat16),
            in_specs=[VMEM] * (1 + len(incoming)) + [ANY],
            out_specs=ANY,
            scratch_shapes=[
                pltpu.VMEM((steps,) + tile_shape, jnp.bfloat16),
                pltpu.SemaphoreType.DMA((steps,)),
            ],
            input_output_aliases={1 + len(incoming): 0},
            compiler_params=SMALL,
            name="place",
        )(plan, *incoming, cleared)

    def exchanged(blocks):
        moved = [
            lax.ppermute(block, "dp", list(enumerate(targets)))
            for block, targets in zip(blocks[1:], rounds(replicas))
        ]
        return [blocks[0], *moved]

    if not apart:
        swapped = lax.all_to_all(outgoing[0], "dp", split_axis=0, concat_axis=0, tiled=True)
        return placed(False, [swapped])
    return lax.cond(
        plan[0, 0] > 0,
        lambda: placed(False, exchanged(outgoing[:steps])),
        lambda: placed(True, exchanged(outgoing[steps:])),
    )


def solution(mesh):
    in_specs = (
        P("pipe", None, "dp", "tensor"),
        P("pipe", None, "dp", "tensor"),
        P("pipe", "dp", "tensor", None, None, None, None),
        P("pipe", None, "tensor", None, None, None),
        P("pipe", "tensor", None),
    )
    out_specs = P("pipe", "tensor", "dp", None)
    return jax.shard_map(
        functools.partial(body, mesh),
        mesh=mesh,
        in_specs=in_specs,
        out_specs=out_specs,
        check_vma=False,
    )
```

```python
import functools

import jax
import jax.numpy as jnp
from jax import lax
from jax.experimental import pallas as pl
from jax.experimental.pallas import tpu as pltpu
from jax.sharding import PartitionSpec as P

VMEM = pl.BlockSpec(memory_space=pltpu.VMEM)
SMEM = pl.BlockSpec(memory_space=pltpu.SMEM)
ANY = pl.BlockSpec(memory_space=pl.ANY)
MOST_STEPS = 8
ROUNDS = {4: [(2, 3, 1, 0), (3, 2, 0, 1), (1, 0, 3, 2)]}
SMALL = pltpu.CompilerParams(vmem_limit_bytes=4 << 20)


def in_hbm(value):
    return pltpu.with_memory_space_constraint(value, pltpu.HBM)


def column(index, edge):
    return pl.ds(pl.multiple_of(index * edge, edge), edge)


def rounds(replicas):
    shifts = [
        tuple((one + step) % replicas for one in range(replicas)) for step in range(1, replicas)
    ]
    return ROUNDS.get(replicas, shifts)


def step_table(replicas):
    table = []
    for source in range(replicas):
        steps = [0] * replicas
        for step, targets in reversed(list(enumerate(rounds(replicas), 1))):
            steps[targets[source]] = step
        table.append(sum(step << 4 * target for target, step in enumerate(steps)))
    return table


def wide_bit(step, count):
    return step - 1 if count <= 4 else 0


def plan_sizes(tiles, steps):
    return 1, 1 + tiles, 1 + 2 * tiles, 1 + 2 * tiles + steps, 1 + 2 * tiles + 2 * steps


def pick(shifts, apart, columns, picks, owners, activations, errors, picked, plan, *refs):
    cuts, (read, seen, copied) = refs[:shifts], refs[shifts:]
    replica, group_at = lax.axis_index("dp"), lax.axis_index("tensor")
    groups, slots, replicas = picks.shape[2], picks.shape[3], picks.shape[-1]
    edge = picked.shape[1]
    tiles = [
        (lax.rem(group_at + shift, groups), slot) for shift in range(groups) for slot in range(slots)
    ]
    reads = []
    for at, (group, slot) in enumerate(tiles):
        block = picks[0, 0, group, slot, 0, replica]
        reads.append(
            pltpu.make_async_copy(
                activations.at[0, :, :, column(block, edge)], read.at[at], copied.at[at]
            )
        )
    for shift, cut in enumerate(cuts):
        other = lax.rem(group_at + groups - shift - 1, groups)
        reads.append(
            pltpu.make_async_copy(errors.at[0, 0, 0, other], cut, copied.at[len(tiles) + shift])
        )
    for copy in reads:
        copy.start()

    owned = owners.shape[-1] // replicas
    per_group = columns // groups
    steps = len(rounds(replicas)) + 1 if apart else replicas
    to_step, to_column, to_row, to_col, end = plan_sizes(len(tiles), steps)

    def owner_of(row):
        owner = jnp.int32(0)
        for one in range(1, replicas):
            owner += (row >= one * owned).astype(jnp.int32)
        return owner

    table = step_table(replicas) if apart else []
    mine = jnp.int32(0)
    for source, packed in enumerate(table):
        mine = jnp.where(replica == source, packed, mine)
    lane = lax.broadcasted_iota(jnp.int32, plan.shape, 1)
    planned = jnp.where((lane >= to_row) & (lane < end), -1, 0)

    for at, (group, slot) in enumerate(tiles):
        owner = owner_of(owners[0, 0, picks[0, 0, group, slot, 0, replica]])
        step = (mine >> 4 * owner) & 15 if apart else owner
        planned = jnp.where(lane == to_step + at, step, planned)
        planned = jnp.where(lane == to_column + at, picks[0, 0, group, slot, 1, replica], planned)

    for origin in range(replicas):
        place_row, place_col = jnp.int32(-1), jnp.int32(0)
        for group, slot in tiles:
            row = owners[0, 0, picks[0, 0, group, slot, 0, origin]] - replica * owned
            here = (row >= 0) & (row < owned)
            place_row = jnp.where(here, row, place_row)
            place_col = jnp.where(
                here, picks[0, 0, group, slot, 1, origin] + group * per_group, place_col
            )
        step = (jnp.int32(table[origin]) >> 4 * replica) & 15 if apart else origin
        planned = jnp.where(lane == to_row + step, place_row, planned)
        planned = jnp.where(lane == to_col + step, place_col, planned)

    wide = jnp.int32(0)
    if apart:
        spots = [
            picks[0, 0, group, slot, 0, origin] * columns
            + picks[0, 0, group, slot, 1, origin]
            + group * per_group
            for origin in range(replicas)
            for group, slot in tiles
        ]
        for spot in spots:
            seen[spot] = 0
        for spot in spots:
            seen[spot] = seen[spot] + 1
        for at, spot in enumerate(spots):
            origin, (group, slot) = at // len(tiles), tiles[at % len(tiles)]
            owner = owner_of(owners[0, 0, picks[0, 0, group, slot, 0, origin]])
            step = (jnp.int32(table[origin]) >> 4 * owner) & 15
            bit = jnp.int32(1) << wide_bit(jnp.maximum(step, 1), steps)
            wide = jnp.where((seen[spot] > 1) & (step > 0), wide | bit, wide)
    plan[...] = jnp.where(lane == 0, wide, planned)

    for at, copy in enumerate(reads):
        copy.wait()
        if at < len(tiles):
            picked[at] = read[at].reshape(-1, edge).T


def clear(after, strip, zeros, cleared):
    zeros[...] = jnp.zeros_like(zeros)
    rows = zeros.shape[0]
    writes = [
        pltpu.make_async_copy(zeros, strip.at[0, 0, pl.ds(part * rows, rows)], cleared.at[part])
        for part in range(strip.shape[2] // rows)
    ]
    for write in writes:
        write.start()
    for write in writes:
        write.wait()


def multiply(groups, apart, to_step, to_column, plan, picked, error, *refs):
    returned, carried, outs = refs[:groups], refs[groups : 2 * groups - 1], refs[2 * groups - 1 :]
    mine = lax.axis_index("tensor")
    slots, (edge, tokens) = error.shape[4], picked.shape[1:]
    count = groups * slots
    wide = plan[0, 0]
    columns = [plan[0, to_column + at] for at in range(count)]
    steps = [plan[0, to_step + at] for at in range(count)]
    tiles = []
    for shift in range(groups):
        for slot in range(slots):
            at = shift * slots + slot
            right = returned[shift][0, :, :, column(columns[at], edge)].reshape(tokens, edge)
            extra = error[0, 0, 0, mine, slot] if shift == 0 else carried[shift - 1][slot]
            tile = jnp.dot(picked[at], right, preferred_element_type=jnp.float32)
            tiles.append(tile + extra.astype(jnp.float32))
    if not apart:
        for step, tile in zip(steps, tiles):
            outs[0][step] = tile
        return

    buffers = len(outs) // 2

    def store(step, tile, buffers):
        for at, buffer in enumerate(buffers):

            @pl.when(step == at)
            def _():
                buffer[...] = tile.astype(buffer.dtype)

    for step, tile in zip(steps, tiles):
        bit = (wide >> wide_bit(jnp.maximum(step, 1), buffers)) & 1
        full = jnp.where(step == 0, wide, bit) > 0

        @pl.when(full)
        def _():
            store(step, tile, outs[:buffers])

        @pl.when(jnp.logical_not(full))
        def _():
            store(step, tile, outs[buffers:])


def place(count, alone, to_row, to_col, plan, *refs):
    blocks, strip, staged, sent = refs[:count], refs[-3], refs[-2], refs[-1]
    steps, edge = staged.shape[0], staged.shape[-1]

    rows = [plan[0, to_row + step] for step in range(steps)]
    cols = [plan[0, to_col + step] for step in range(steps)]

    def meets(one, other):
        return (rows[one] == rows[other]) & (cols[one] == cols[other])

    def block_of(step):
        return blocks[0][step] if count == 1 else blocks[step][...]

    def first_of(step):
        first = rows[step] >= 0
        for earlier in range(0 if alone else step):
            first = first & jnp.logical_not(meets(earlier, step))
        return first

    def write_of(step):
        return pltpu.make_async_copy(
            blocks[step] if alone else staged.at[step],
            strip.at[0, 0, column(rows[step], edge), column(cols[step], edge)],
            sent.at[step],
        )

    for step in range(steps):

        @pl.when(first_of(step))
        def _():
            if not alone:
                total = block_of(step).astype(jnp.float32)
                for later in range(step + 1, steps):
                    block = block_of(later).astype(jnp.float32)
                    total = total + jnp.where(meets(step, later), block, 0.0)
                staged[step] = total.astype(staged.dtype)
            write_of(step).start()

    for step in range(steps):

        @pl.when(first_of(step))
        def _():
            write_of(step).wait()


def body(mesh, activations, cotangent, error_tiles, tile_picks, row_owners):
    sections, replicas, groups = mesh.shape["pipe"], mesh.shape["dp"], mesh.shape["tensor"]
    edge = error_tiles.shape[-1]
    slots = tile_picks.shape[4]
    micro, tokens = activations.shape[1:3]
    width = cotangent.shape[-1] * groups
    strip_rows = row_owners.shape[-1] // replicas * edge
    picks = jnp.transpose(tile_picks, (0, 2, 3, 4, 5, 1))

    returned = []
    for shift in range(groups):
        pairs = [
            (
                (section + 1) % sections * groups + (group + shift) % groups,
                section * groups + group,
            )
            for section in range(sections)
            for group in range(groups)
        ]
        returned.append(lax.ppermute(cotangent, ("pipe", "tensor"), pairs))
    apart = replicas <= MOST_STEPS
    tiles, shifts = groups * slots, groups - 1
    steps = len(rounds(replicas)) + 1 if apart else replicas
    picked, plan, *errors = pl.pallas_call(
        functools.partial(pick, shifts, apart, width // edge),
        out_shape=[
            pltpu.VMEM((tiles, edge, micro * tokens), activations.dtype),
            pltpu.VMEM((1, -(-plan_sizes(tiles, steps)[-1] // 128) * 128), jnp.int32),
        ]
        + [pltpu.VMEM((slots, edge, edge), error_tiles.dtype)] * shifts,
        in_specs=[SMEM, SMEM, ANY, ANY],
        out_specs=[VMEM] * (2 + shifts),
        scratch_shapes=[
            pltpu.VMEM((tiles, micro, tokens, edge), activations.dtype),
            pltpu.SMEM((row_owners.shape[-1] * (width // edge),), jnp.int32),
            pltpu.SemaphoreType.DMA((tiles + shifts,)),
        ],
        compiler_params=SMALL,
        name="pick",
    )(in_hbm(picks), in_hbm(row_owners), in_hbm(activations), in_hbm(error_tiles))
    carried = [
        lax.ppermute(
            error, "tensor", [((group + shift + 1) % groups, group) for group in range(groups)]
        )
        for shift, error in enumerate(errors)
    ]

    zero_rows = min(strip_rows, 256)
    strip_shape = (1, 1, strip_rows, width)
    cleared = pl.pallas_call(
        clear,
        out_shape=pltpu.HBM(strip_shape, jnp.bfloat16),
        in_specs=[ANY],
        out_specs=pl.BlockSpec(memory_space=pltpu.HBM),
        scratch_shapes=[
            pltpu.VMEM((zero_rows, width), jnp.bfloat16),
            pltpu.SemaphoreType.DMA((strip_rows // zero_rows,)),
        ],
        compiler_params=SMALL,
        cost_estimate=pl.CostEstimate(
            flops=0, bytes_accessed=2 * strip_rows * width, transcendentals=0
        ),
        name="clear",
    )(picked)

    to_step, to_column, to_row, to_col, _ = plan_sizes(tiles, steps)
    tile_shape = (edge, edge)
    if apart:
        out_shape = [
            jax.ShapeDtypeStruct(tile_shape, dtype)
            for dtype in (jnp.float32, jnp.bfloat16)
            for step in range(steps)
        ]
    else:
        out_shape = [jax.ShapeDtypeStruct((replicas,) + tile_shape, jnp.float32)]
    outgoing = pl.pallas_call(
        functools.partial(multiply, groups, apart, to_step, to_column),
        out_shape=out_shape,
        in_specs=[VMEM] * (2 * groups + 2),
        out_specs=[VMEM] * len(out_shape),
        compiler_params=SMALL,
        name="multiply",
    )(plan, picked, error_tiles, *returned, *carried)

    def placed(alone, incoming):
        return pl.pallas_call(
            functools.partial(place, len(incoming), alone, to_row, to_col),
            out_shape=jax.ShapeDtypeStruct(strip_shape, jnp.bfloat16),
            in_specs=[VMEM] * (1 + len(incoming)) + [ANY],
            out_specs=ANY,
            scratch_shapes=[
                pltpu.VMEM((steps,) + tile_shape, jnp.bfloat16),
                pltpu.SemaphoreType.DMA((steps,)),
            ],
            input_output_aliases={1 + len(incoming): 0},
            compiler_params=SMALL,
            name="place",
        )(plan, *incoming, cleared)

    def exchanged(blocks):
        moved = [
            lax.ppermute(block, "dp", list(enumerate(targets)))
            for block, targets in zip(blocks[1:], rounds(replicas))
        ]
        return [blocks[0], *moved]

    if not apart:
        swapped = lax.all_to_all(outgoing[0], "dp", split_axis=0, concat_axis=0, tiled=True)
        return placed(False, [swapped])
    def branch(wide):
        blocks = [
            outgoing[at if (wide >> wide_bit(at, steps) & 1 if at else wide) else steps + at]
            for at in range(steps)
        ]
        return lambda: placed(not wide, exchanged(blocks))

    sets = 1 << (wide_bit(steps - 1, steps) + 1)
    return lax.switch(plan[0, 0], [branch(wide) for wide in range(sets)])


def solution(mesh):
    in_specs = (
        P("pipe", None, "dp", "tensor"),
        P("pipe", None, "dp", "tensor"),
        P("pipe", "dp", "tensor", None, None, None, None),
        P("pipe", None, "tensor", None, None, None),
        P("pipe", "tensor", None),
    )
    out_specs = P("pipe", "tensor", "dp", None)
    return jax.shard_map(
        functools.partial(body, mesh),
        mesh=mesh,
        in_specs=in_specs,
        out_specs=out_specs,
        check_vma=False,
    )
```

```python
import functools

import jax
import jax.numpy as jnp
from jax import lax
from jax.experimental import pallas as pl
from jax.experimental.pallas import tpu as pltpu
from jax.sharding import PartitionSpec as P

VMEM = pl.BlockSpec(memory_space=pltpu.VMEM)
SMEM = pl.BlockSpec(memory_space=pltpu.SMEM)
ANY = pl.BlockSpec(memory_space=pl.ANY)
MOST_STEPS = 8
ROUNDS = {4: [(2, 3, 1, 0), (3, 2, 0, 1), (1, 0, 3, 2)]}
SMALL = pltpu.CompilerParams(vmem_limit_bytes=4 << 20)


def in_hbm(value):
    return pltpu.with_memory_space_constraint(value, pltpu.HBM)


def column(index, edge):
    return pl.ds(pl.multiple_of(index * edge, edge), edge)


def rounds(replicas):
    shifts = [
        tuple((one + step) % replicas for one in range(replicas)) for step in range(1, replicas)
    ]
    return ROUNDS.get(replicas, shifts)


def step_table(replicas):
    table = []
    for source in range(replicas):
        steps = [0] * replicas
        for step, targets in reversed(list(enumerate(rounds(replicas), 1))):
            steps[targets[source]] = step
        table.append(sum(step << 4 * target for target, step in enumerate(steps)))
    return table


def wide_bit(step, count):
    return step - 1 if count <= 4 else 0


def plan_sizes(tiles, steps):
    return 1, 1 + tiles, 1 + 2 * tiles, 1 + 2 * tiles + steps, 1 + 2 * tiles + 2 * steps


def pick(shifts, apart, columns, picks, owners, activations, errors, picked, plan, *refs):
    cuts, (read, seen, copied) = refs[:shifts], refs[shifts:]
    replica, group_at = lax.axis_index("dp"), lax.axis_index("tensor")
    groups, slots, replicas = picks.shape[2], picks.shape[3], picks.shape[-1]
    edge = picked.shape[1]
    tiles = [
        (lax.rem(group_at + shift, groups), slot) for shift in range(groups) for slot in range(slots)
    ]
    reads = []
    for at, (group, slot) in enumerate(tiles):
        block = picks[0, 0, group, slot, 0, replica]
        reads.append(
            pltpu.make_async_copy(
                activations.at[0, :, :, column(block, edge)], read.at[at], copied.at[at]
            )
        )
    for shift, cut in enumerate(cuts):
        other = lax.rem(group_at + groups - shift - 1, groups)
        reads.append(
            pltpu.make_async_copy(errors.at[0, 0, 0, other], cut, copied.at[len(tiles) + shift])
        )
    for copy in reads:
        copy.start()

    owned = owners.shape[-1] // replicas
    per_group = columns // groups
    steps = len(rounds(replicas)) + 1 if apart else replicas
    to_step, to_column, to_row, to_col, end = plan_sizes(len(tiles), steps)

    def owner_of(row):
        owner = jnp.int32(0)
        for one in range(1, replicas):
            owner += (row >= one * owned).astype(jnp.int32)
        return owner

    table = step_table(replicas) if apart else []
    mine = jnp.int32(0)
    for source, packed in enumerate(table):
        mine = jnp.where(replica == source, packed, mine)
    lane = lax.broadcasted_iota(jnp.int32, plan.shape, 1)
    planned = jnp.where((lane >= to_row) & (lane < end), -1, 0)

    for at, (group, slot) in enumerate(tiles):
        owner = owner_of(owners[0, 0, picks[0, 0, group, slot, 0, replica]])
        step = (mine >> 4 * owner) & 15 if apart else owner
        planned = jnp.where(lane == to_step + at, step, planned)
        planned = jnp.where(lane == to_column + at, picks[0, 0, group, slot, 1, replica], planned)

    for origin in range(replicas):
        place_row, place_col = jnp.int32(-1), jnp.int32(0)
        for group, slot in tiles:
            row = owners[0, 0, picks[0, 0, group, slot, 0, origin]] - replica * owned
            here = (row >= 0) & (row < owned)
            place_row = jnp.where(here, row, place_row)
            place_col = jnp.where(
                here, picks[0, 0, group, slot, 1, origin] + group * per_group, place_col
            )
        step = (jnp.int32(table[origin]) >> 4 * replica) & 15 if apart else origin
        planned = jnp.where(lane == to_row + step, place_row, planned)
        planned = jnp.where(lane == to_col + step, place_col, planned)

    wide = jnp.int32(0)
    if apart:
        spots = [
            picks[0, 0, group, slot, 0, origin] * columns
            + picks[0, 0, group, slot, 1, origin]
            + group * per_group
            for origin in range(replicas)
            for group, slot in tiles
        ]
        for spot in spots:
            seen[spot] = 0
        for spot in spots:
            seen[spot] = seen[spot] + 1
        for at, spot in enumerate(spots):
            origin, (group, slot) = at // len(tiles), tiles[at % len(tiles)]
            owner = owner_of(owners[0, 0, picks[0, 0, group, slot, 0, origin]])
            step = (jnp.int32(table[origin]) >> 4 * owner) & 15
            bit = jnp.int32(1) << wide_bit(jnp.maximum(step, 1), steps)
            wide = jnp.where((seen[spot] > 1) & (step > 0), wide | bit, wide)
    plan[...] = jnp.where(lane == 0, wide, planned)

    for at, copy in enumerate(reads):
        copy.wait()
        if at < len(tiles):
            picked[at] = read[at].reshape(-1, edge).T


def clear(after, strip, zeros, cleared):
    zeros[...] = jnp.zeros_like(zeros)
    rows = zeros.shape[0]
    writes = [
        pltpu.make_async_copy(zeros, strip.at[0, 0, pl.ds(part * rows, rows)], cleared.at[part])
        for part in range(strip.shape[2] // rows)
    ]
    for write in writes:
        write.start()
    for write in writes:
        write.wait()


def multiply(groups, apart, to_step, to_column, plan, picked, error, *refs):
    returned, carried, outs = refs[:groups], refs[groups : 2 * groups - 1], refs[2 * groups - 1 :]
    mine = lax.axis_index("tensor")
    slots, (edge, tokens) = error.shape[4], picked.shape[1:]
    count = groups * slots
    wide = plan[0, 0]
    columns = [plan[0, to_column + at] for at in range(count)]
    steps = [plan[0, to_step + at] for at in range(count)]
    tiles = []
    for shift in range(groups):
        for slot in range(slots):
            at = shift * slots + slot
            right = returned[shift][0, :, :, column(columns[at], edge)].reshape(tokens, edge)
            extra = error[0, 0, 0, mine, slot] if shift == 0 else carried[shift - 1][slot]
            tile = jnp.dot(picked[at], right, preferred_element_type=jnp.float32)
            tiles.append(tile + extra.astype(jnp.float32))
    if not apart:
        for step, tile in zip(steps, tiles):
            outs[0][step] = tile
        return

    buffers = len(outs) // 2

    def store(step, tile, buffers):
        for at, buffer in enumerate(buffers):

            @pl.when(step == at)
            def _():
                buffer[...] = tile.astype(buffer.dtype)

    for step, tile in zip(steps, tiles):
        bit = (wide >> wide_bit(jnp.maximum(step, 1), buffers)) & 1
        full = jnp.where(step == 0, wide, bit) > 0

        @pl.when(full)
        def _():
            store(step, tile, outs[:buffers])

        @pl.when(jnp.logical_not(full))
        def _():
            store(step, tile, outs[buffers:])


def place(count, alone, to_row, to_col, plan, *refs):
    blocks, strip, staged, sent = refs[:count], refs[-3], refs[-2], refs[-1]
    steps, edge = staged.shape[0], staged.shape[-1]

    rows = [plan[0, to_row + step] for step in range(steps)]
    cols = [plan[0, to_col + step] for step in range(steps)]

    def meets(one, other):
        return (rows[one] == rows[other]) & (cols[one] == cols[other])

    def block_of(step):
        return blocks[0][step] if count == 1 else blocks[step][...]

    def first_of(step):
        first = rows[step] >= 0
        for earlier in range(0 if alone else step):
            first = first & jnp.logical_not(meets(earlier, step))
        return first

    half = edge // 2

    def writes_of(step):
        source = blocks[step] if alone else staged.at[step]
        return [
            pltpu.make_async_copy(
                source.at[pl.ds(part * half, half)],
                strip.at[
                    0,
                    0,
                    pl.ds(pl.multiple_of(rows[step] * edge + part * half, half), half),
                    column(cols[step], edge),
                ],
                sent.at[step, part],
            )
            for part in range(2)
        ]

    for step in range(steps):

        @pl.when(first_of(step))
        def _():
            if not alone:
                total = block_of(step).astype(jnp.float32)
                for later in range(step + 1, steps):
                    block = block_of(later).astype(jnp.float32)
                    total = total + jnp.where(meets(step, later), block, 0.0)
                staged[step] = total.astype(staged.dtype)
            for write in writes_of(step):
                write.start()

    for step in range(steps):

        @pl.when(first_of(step))
        def _():
            for write in writes_of(step):
                write.wait()


def body(mesh, activations, cotangent, error_tiles, tile_picks, row_owners):
    sections, replicas, groups = mesh.shape["pipe"], mesh.shape["dp"], mesh.shape["tensor"]
    edge = error_tiles.shape[-1]
    slots = tile_picks.shape[4]
    micro, tokens = activations.shape[1:3]
    width = cotangent.shape[-1] * groups
    strip_rows = row_owners.shape[-1] // replicas * edge
    picks = jnp.transpose(tile_picks, (0, 2, 3, 4, 5, 1))

    returned = []
    for shift in range(groups):
        pairs = [
            (
                (section + 1) % sections * groups + (group + shift) % groups,
                section * groups + group,
            )
            for section in range(sections)
            for group in range(groups)
        ]
        returned.append(lax.ppermute(cotangent, ("pipe", "tensor"), pairs))
    apart = replicas <= MOST_STEPS
    tiles, shifts = groups * slots, groups - 1
    steps = len(rounds(replicas)) + 1 if apart else replicas
    picked, plan, *errors = pl.pallas_call(
        functools.partial(pick, shifts, apart, width // edge),
        out_shape=[
            pltpu.VMEM((tiles, edge, micro * tokens), activations.dtype),
            pltpu.VMEM((1, -(-plan_sizes(tiles, steps)[-1] // 128) * 128), jnp.int32),
        ]
        + [pltpu.VMEM((slots, edge, edge), error_tiles.dtype)] * shifts,
        in_specs=[SMEM, SMEM, ANY, ANY],
        out_specs=[VMEM] * (2 + shifts),
        scratch_shapes=[
            pltpu.VMEM((tiles, micro, tokens, edge), activations.dtype),
            pltpu.SMEM((row_owners.shape[-1] * (width // edge),), jnp.int32),
            pltpu.SemaphoreType.DMA((tiles + shifts,)),
        ],
        compiler_params=SMALL,
        name="pick",
    )(in_hbm(picks), in_hbm(row_owners), in_hbm(activations), in_hbm(error_tiles))
    carried = [
        lax.ppermute(
            error, "tensor", [((group + shift + 1) % groups, group) for group in range(groups)]
        )
        for shift, error in enumerate(errors)
    ]

    zero_rows = min(strip_rows, 256)
    strip_shape = (1, 1, strip_rows, width)
    cleared = pl.pallas_call(
        clear,
        out_shape=pltpu.HBM(strip_shape, jnp.bfloat16),
        in_specs=[ANY],
        out_specs=pl.BlockSpec(memory_space=pltpu.HBM),
        scratch_shapes=[
            pltpu.VMEM((zero_rows, width), jnp.bfloat16),
            pltpu.SemaphoreType.DMA((strip_rows // zero_rows,)),
        ],
        compiler_params=SMALL,
        cost_estimate=pl.CostEstimate(
            flops=0, bytes_accessed=2 * strip_rows * width, transcendentals=0
        ),
        name="clear",
    )(picked)

    to_step, to_column, to_row, to_col, _ = plan_sizes(tiles, steps)
    tile_shape = (edge, edge)
    if apart:
        out_shape = [
            jax.ShapeDtypeStruct(tile_shape, dtype)
            for dtype in (jnp.float32, jnp.bfloat16)
            for step in range(steps)
        ]
    else:
        out_shape = [jax.ShapeDtypeStruct((replicas,) + tile_shape, jnp.float32)]
    outgoing = pl.pallas_call(
        functools.partial(multiply, groups, apart, to_step, to_column),
        out_shape=out_shape,
        in_specs=[VMEM] * (2 * groups + 2),
        out_specs=[VMEM] * len(out_shape),
        compiler_params=SMALL,
        name="multiply",
    )(plan, picked, error_tiles, *returned, *carried)

    def placed(alone, incoming):
        return pl.pallas_call(
            functools.partial(place, len(incoming), alone, to_row, to_col),
            out_shape=jax.ShapeDtypeStruct(strip_shape, jnp.bfloat16),
            in_specs=[VMEM] * (1 + len(incoming)) + [ANY],
            out_specs=ANY,
            scratch_shapes=[
                pltpu.VMEM((steps,) + tile_shape, jnp.bfloat16),
                pltpu.SemaphoreType.DMA((steps, 2)),
            ],
            input_output_aliases={1 + len(incoming): 0},
            compiler_params=SMALL,
            name="place",
        )(plan, *incoming, cleared)

    def exchanged(blocks):
        moved = [
            lax.ppermute(block, "dp", list(enumerate(targets)))
            for block, targets in zip(blocks[1:], rounds(replicas))
        ]
        return [blocks[0], *moved]

    if not apart:
        swapped = lax.all_to_all(outgoing[0], "dp", split_axis=0, concat_axis=0, tiled=True)
        return placed(False, [swapped])
    def branch(wide):
        blocks = [
            outgoing[at if (wide >> wide_bit(at, steps) & 1 if at else wide) else steps + at]
            for at in range(steps)
        ]
        return lambda: placed(not wide, exchanged(blocks))

    sets = 1 << (wide_bit(steps - 1, steps) + 1)
    return lax.switch(plan[0, 0], [branch(wide) for wide in range(sets)])


def solution(mesh):
    in_specs = (
        P("pipe", None, "dp", "tensor"),
        P("pipe", None, "dp", "tensor"),
        P("pipe", "dp", "tensor", None, None, None, None),
        P("pipe", None, "tensor", None, None, None),
        P("pipe", "tensor", None),
    )
    out_specs = P("pipe", "tensor", "dp", None)
    return jax.shard_map(
        functools.partial(body, mesh),
        mesh=mesh,
        in_specs=in_specs,
        out_specs=out_specs,
        check_vma=False,
    )
```

```python
import functools

import jax
import jax.numpy as jnp
from jax import lax
from jax.experimental import pallas as pl
from jax.experimental.pallas import tpu as pltpu
from jax.sharding import PartitionSpec as P

VMEM = pl.BlockSpec(memory_space=pltpu.VMEM)
SMEM = pl.BlockSpec(memory_space=pltpu.SMEM)
ANY = pl.BlockSpec(memory_space=pl.ANY)
MOST_STEPS = 8
ROUNDS = {4: [(2, 3, 1, 0), (3, 2, 0, 1), (1, 0, 3, 2)]}
SMALL = pltpu.CompilerParams(vmem_limit_bytes=4 << 20)


def in_hbm(value):
    return pltpu.with_memory_space_constraint(value, pltpu.HBM)


def column(index, edge):
    return pl.ds(pl.multiple_of(index * edge, edge), edge)


def rounds(replicas):
    shifts = [
        tuple((one + step) % replicas for one in range(replicas)) for step in range(1, replicas)
    ]
    return ROUNDS.get(replicas, shifts)


def step_table(replicas):
    table = []
    for source in range(replicas):
        steps = [0] * replicas
        for step, targets in reversed(list(enumerate(rounds(replicas), 1))):
            steps[targets[source]] = step
        table.append(sum(step << 4 * target for target, step in enumerate(steps)))
    return table


def wide_bit(step, count):
    return step - 1 if count <= 4 else 0


def plan_sizes(tiles, steps):
    return 1, 1 + tiles, 1 + 2 * tiles, 1 + 2 * tiles + steps, 1 + 2 * tiles + 2 * steps


def pick(shifts, apart, columns, picks, owners, activations, errors, picked, plan, *refs):
    cuts, (read, seen, copied) = refs[:shifts], refs[shifts:]
    replica, group_at = lax.axis_index("dp"), lax.axis_index("tensor")
    groups, slots, replicas = picks.shape[2], picks.shape[3], picks.shape[-1]
    edge = picked.shape[1]
    tiles = [
        (lax.rem(group_at + shift, groups), slot) for shift in range(groups) for slot in range(slots)
    ]
    reads = []
    for at, (group, slot) in enumerate(tiles):
        block = picks[0, 0, group, slot, 0, replica]
        reads.append(
            pltpu.make_async_copy(
                activations.at[0, :, :, column(block, edge)], read.at[at], copied.at[at]
            )
        )
    for shift, cut in enumerate(cuts):
        other = lax.rem(group_at + groups - shift - 1, groups)
        reads.append(
            pltpu.make_async_copy(errors.at[0, 0, 0, other], cut, copied.at[len(tiles) + shift])
        )
    for copy in reads:
        copy.start()

    owned = owners.shape[-1] // replicas
    per_group = columns // groups
    steps = len(rounds(replicas)) + 1 if apart else replicas
    to_step, to_column, to_row, to_col, end = plan_sizes(len(tiles), steps)

    def owner_of(row):
        owner = jnp.int32(0)
        for one in range(1, replicas):
            owner += (row >= one * owned).astype(jnp.int32)
        return owner

    table = step_table(replicas) if apart else []
    mine = jnp.int32(0)
    for source, packed in enumerate(table):
        mine = jnp.where(replica == source, packed, mine)
    lane = lax.broadcasted_iota(jnp.int32, plan.shape, 1)
    planned = jnp.where((lane >= to_row) & (lane < end), -1, 0)

    for at, (group, slot) in enumerate(tiles):
        owner = owner_of(owners[0, 0, picks[0, 0, group, slot, 0, replica]])
        step = (mine >> 4 * owner) & 15 if apart else owner
        planned = jnp.where(lane == to_step + at, step, planned)
        planned = jnp.where(lane == to_column + at, picks[0, 0, group, slot, 1, replica], planned)

    for origin in range(replicas):
        place_row, place_col = jnp.int32(-1), jnp.int32(0)
        for group, slot in tiles:
            row = owners[0, 0, picks[0, 0, group, slot, 0, origin]] - replica * owned
            here = (row >= 0) & (row < owned)
            place_row = jnp.where(here, row, place_row)
            place_col = jnp.where(
                here, picks[0, 0, group, slot, 1, origin] + group * per_group, place_col
            )
        step = (jnp.int32(table[origin]) >> 4 * replica) & 15 if apart else origin
        planned = jnp.where(lane == to_row + step, place_row, planned)
        planned = jnp.where(lane == to_col + step, place_col, planned)

    wide = jnp.int32(0)
    if apart:
        spots = [
            picks[0, 0, group, slot, 0, origin] * columns
            + picks[0, 0, group, slot, 1, origin]
            + group * per_group
            for origin in range(replicas)
            for group, slot in tiles
        ]
        for spot in spots:
            seen[spot] = 0
        for spot in spots:
            seen[spot] = seen[spot] + 1
        for at, spot in enumerate(spots):
            origin, (group, slot) = at // len(tiles), tiles[at % len(tiles)]
            owner = owner_of(owners[0, 0, picks[0, 0, group, slot, 0, origin]])
            step = (jnp.int32(table[origin]) >> 4 * owner) & 15
            bit = jnp.int32(1) << wide_bit(jnp.maximum(step, 1), steps)
            wide = jnp.where((seen[spot] > 1) & (step > 0), wide | bit, wide)
    plan[...] = jnp.where(lane == 0, wide, planned)

    for at, copy in enumerate(reads):
        copy.wait()
        if at < len(tiles):
            picked[at] = read[at].reshape(-1, edge).T


def clear(after, strip, zeros, cleared):
    zeros[...] = jnp.zeros_like(zeros)
    rows = zeros.shape[0]
    writes = [
        pltpu.make_async_copy(zeros, strip.at[0, 0, pl.ds(part * rows, rows)], cleared.at[part])
        for part in range(strip.shape[2] // rows)
    ]
    for write in writes:
        write.start()
    for write in writes:
        write.wait()


def multiply(groups, apart, to_step, to_column, plan, picked, error, *refs):
    returned, carried, outs = refs[:groups], refs[groups : 2 * groups - 1], refs[2 * groups - 1 :]
    mine = lax.axis_index("tensor")
    slots, (edge, tokens) = error.shape[4], picked.shape[1:]
    count = groups * slots
    wide = plan[0, 0]
    columns = [plan[0, to_column + at] for at in range(count)]
    steps = [plan[0, to_step + at] for at in range(count)]
    tiles = []
    for shift in range(groups):
        for slot in range(slots):
            at = shift * slots + slot
            right = returned[shift][0, :, :, column(columns[at], edge)].reshape(tokens, edge)
            extra = error[0, 0, 0, mine, slot] if shift == 0 else carried[shift - 1][slot]
            tile = jnp.dot(picked[at], right, preferred_element_type=jnp.float32)
            tiles.append(tile + extra.astype(jnp.float32))
    if not apart:
        for step, tile in zip(steps, tiles):
            outs[0][step] = tile
        return

    buffers = len(outs) // 2

    def store(step, tile, buffers):
        for at, buffer in enumerate(buffers):

            @pl.when(step == at)
            def _():
                buffer[...] = tile.astype(buffer.dtype)

    for step, tile in zip(steps, tiles):
        bit = (wide >> wide_bit(jnp.maximum(step, 1), buffers)) & 1
        full = jnp.where(step == 0, wide, bit) > 0

        @pl.when(full)
        def _():
            store(step, tile, outs[:buffers])

        @pl.when(jnp.logical_not(full))
        def _():
            store(step, tile, outs[buffers:])


def place(count, alone, to_row, to_col, plan, *refs):
    blocks, strip, staged, sent = refs[:count], refs[-3], refs[-2], refs[-1]
    steps, edge = staged.shape[0], staged.shape[-1]

    rows = [plan[0, to_row + step] for step in range(steps)]
    cols = [plan[0, to_col + step] for step in range(steps)]

    def meets(one, other):
        return (rows[one] == rows[other]) & (cols[one] == cols[other])

    def block_of(step):
        return blocks[0][step] if count == 1 else blocks[step][...]

    def first_of(step):
        first = rows[step] >= 0
        for earlier in range(0 if alone else step):
            first = first & jnp.logical_not(meets(earlier, step))
        return first

    def write_of(step):
        return pltpu.make_async_copy(
            blocks[step] if alone else staged.at[step],
            strip.at[0, 0, column(rows[step], edge), column(cols[step], edge)],
            sent.at[step],
        )

    for step in range(steps):

        @pl.when(first_of(step))
        def _():
            if not alone:
                total = block_of(step).astype(jnp.float32)
                for later in range(step + 1, steps):
                    block = block_of(later).astype(jnp.float32)
                    total = total + jnp.where(meets(step, later), block, 0.0)
                staged[step] = total.astype(staged.dtype)
            write_of(step).start()

    for step in range(steps):

        @pl.when(first_of(step))
        def _():
            write_of(step).wait()


def body(mesh, activations, cotangent, error_tiles, tile_picks, row_owners):
    sections, replicas, groups = mesh.shape["pipe"], mesh.shape["dp"], mesh.shape["tensor"]
    edge = error_tiles.shape[-1]
    slots = tile_picks.shape[4]
    micro, tokens = activations.shape[1:3]
    width = cotangent.shape[-1] * groups
    strip_rows = row_owners.shape[-1] // replicas * edge
    picks = jnp.transpose(tile_picks, (0, 2, 3, 4, 5, 1))

    returned = []
    for shift in range(groups):
        pairs = [
            (
                (section + 1) % sections * groups + (group + shift) % groups,
                section * groups + group,
            )
            for section in range(sections)
            for group in range(groups)
        ]
        returned.append(lax.ppermute(cotangent, ("pipe", "tensor"), pairs))
    apart = replicas <= MOST_STEPS
    tiles, shifts = groups * slots, groups - 1
    steps = len(rounds(replicas)) + 1 if apart else replicas
    picked, plan, *errors = pl.pallas_call(
        functools.partial(pick, shifts, apart, width // edge),
        out_shape=[
            pltpu.VMEM((tiles, edge, micro * tokens), activations.dtype),
            pltpu.VMEM((1, -(-plan_sizes(tiles, steps)[-1] // 128) * 128), jnp.int32),
        ]
        + [pltpu.VMEM((slots, edge, edge), error_tiles.dtype)] * shifts,
        in_specs=[SMEM, SMEM, ANY, ANY],
        out_specs=[VMEM] * (2 + shifts),
        scratch_shapes=[
            pltpu.VMEM((tiles, micro, tokens, edge), activations.dtype),
            pltpu.SMEM((row_owners.shape[-1] * (width // edge),), jnp.int32),
            pltpu.SemaphoreType.DMA((tiles + shifts,)),
        ],
        compiler_params=SMALL,
        name="pick",
    )(in_hbm(picks), in_hbm(row_owners), in_hbm(activations), in_hbm(error_tiles))
    carried = [
        lax.ppermute(
            error, "tensor", [((group + shift + 1) % groups, group) for group in range(groups)]
        )
        for shift, error in enumerate(errors)
    ]

    zero_rows = min(strip_rows, 256)
    strip_shape = (1, 1, strip_rows, width)
    cleared = pl.pallas_call(
        clear,
        out_shape=pltpu.HBM(strip_shape, jnp.bfloat16),
        in_specs=[ANY],
        out_specs=pl.BlockSpec(memory_space=pltpu.HBM),
        scratch_shapes=[
            pltpu.VMEM((zero_rows, width), jnp.bfloat16),
            pltpu.SemaphoreType.DMA((strip_rows // zero_rows,)),
        ],
        compiler_params=SMALL,
        cost_estimate=pl.CostEstimate(
            flops=0, bytes_accessed=2 * strip_rows * width, transcendentals=0
        ),
        name="clear",
    )(picked)

    to_step, to_column, to_row, to_col, _ = plan_sizes(tiles, steps)
    tile_shape = (edge, edge)
    if apart:
        out_shape = [
            jax.ShapeDtypeStruct(tile_shape, dtype)
            for dtype in (jnp.float32, jnp.bfloat16)
            for step in range(steps)
        ]
    else:
        out_shape = [jax.ShapeDtypeStruct((replicas,) + tile_shape, jnp.float32)]
    outgoing = pl.pallas_call(
        functools.partial(multiply, groups, apart, to_step, to_column),
        out_shape=out_shape,
        in_specs=[VMEM] * (2 * groups + 2),
        out_specs=[VMEM] * len(out_shape),
        compiler_params=SMALL,
        name="multiply",
    )(plan, picked, error_tiles, *returned, *carried)

    def placed(alone, incoming, strip, first=0):
        count = len(incoming) if apart else replicas
        return pl.pallas_call(
            functools.partial(place, len(incoming), alone, to_row + first, to_col + first),
            out_shape=jax.ShapeDtypeStruct(strip_shape, jnp.bfloat16),
            in_specs=[VMEM] * (1 + len(incoming)) + [ANY],
            out_specs=ANY,
            scratch_shapes=[
                pltpu.VMEM((count,) + tile_shape, jnp.bfloat16),
                pltpu.SemaphoreType.DMA((count,)),
            ],
            input_output_aliases={1 + len(incoming): 0},
            compiler_params=SMALL,
            name="place",
        )(plan, *incoming, strip)

    def exchanged(blocks):
        moved = [
            lax.ppermute(block, "dp", list(enumerate(targets)))
            for block, targets in zip(blocks[1:], rounds(replicas))
        ]
        return [blocks[0], *moved]

    if not apart:
        swapped = lax.all_to_all(outgoing[0], "dp", split_axis=0, concat_axis=0, tiled=True)
        return placed(False, [swapped], cleared)
    def branch(wide):
        blocks = [
            outgoing[at if (wide >> wide_bit(at, steps) & 1 if at else wide) else steps + at]
            for at in range(steps)
        ]
        def run():
            arrived = exchanged(blocks)
            if wide:
                return placed(False, arrived, cleared)
            return placed(True, arrived[2:], placed(True, arrived[:2], cleared), 2)

        return run

    sets = 1 << (wide_bit(steps - 1, steps) + 1)
    return lax.switch(plan[0, 0], [branch(wide) for wide in range(sets)])


def solution(mesh):
    in_specs = (
        P("pipe", None, "dp", "tensor"),
        P("pipe", None, "dp", "tensor"),
        P("pipe", "dp", "tensor", None, None, None, None),
        P("pipe", None, "tensor", None, None, None),
        P("pipe", "tensor", None),
    )
    out_specs = P("pipe", "tensor", "dp", None)
    return jax.shard_map(
        functools.partial(body, mesh),
        mesh=mesh,
        in_specs=in_specs,
        out_specs=out_specs,
        check_vma=False,
    )
```

```python
import functools

import jax
import jax.numpy as jnp
from jax import lax
from jax.experimental import pallas as pl
from jax.experimental.pallas import tpu as pltpu
from jax.sharding import PartitionSpec as P

VMEM = pl.BlockSpec(memory_space=pltpu.VMEM)
SMEM = pl.BlockSpec(memory_space=pltpu.SMEM)
ANY = pl.BlockSpec(memory_space=pl.ANY)
MOST_STEPS = 8
ROUNDS = {4: [(2, 3, 1, 0), (3, 2, 0, 1), (1, 0, 3, 2)]}
SMALL = pltpu.CompilerParams(vmem_limit_bytes=4 << 20)


def in_hbm(value):
    return pltpu.with_memory_space_constraint(value, pltpu.HBM)


def column(index, edge):
    return pl.ds(pl.multiple_of(index * edge, edge), edge)


def rounds(replicas, odd=0):
    shifts = [
        tuple((one + step) % replicas for one in range(replicas)) for step in range(1, replicas)
    ]
    return shifts if odd else ROUNDS.get(replicas, shifts)


def step_table(replicas, odd):
    table = []
    for source in range(replicas):
        steps = [0] * replicas
        for step, targets in reversed(list(enumerate(rounds(replicas, odd), 1))):
            steps[targets[source]] = step
        table.append(sum(step << 4 * target for target, step in enumerate(steps)))
    return table


def wide_bit(step, count):
    return step - 1 if count <= 4 else 0


def plan_sizes(tiles, steps):
    return 1, 1 + tiles, 1 + 2 * tiles, 1 + 2 * tiles + steps, 1 + 2 * tiles + 2 * steps


def pick(shifts, apart, columns, picks, owners, activations, errors, picked, plan, *refs):
    cuts, (read, seen, copied) = refs[:shifts], refs[shifts:]
    replica, group_at = lax.axis_index("dp"), lax.axis_index("tensor")
    groups, slots, replicas = picks.shape[2], picks.shape[3], picks.shape[-1]
    edge = picked.shape[1]
    tiles = [
        (lax.rem(group_at + shift, groups), slot) for shift in range(groups) for slot in range(slots)
    ]
    reads = []
    for at, (group, slot) in enumerate(tiles):
        block = picks[0, 0, group, slot, 0, replica]
        reads.append(
            pltpu.make_async_copy(
                activations.at[0, :, :, column(block, edge)], read.at[at], copied.at[at]
            )
        )
    for shift, cut in enumerate(cuts):
        other = lax.rem(group_at + groups - shift - 1, groups)
        reads.append(
            pltpu.make_async_copy(errors.at[0, 0, 0, other], cut, copied.at[len(tiles) + shift])
        )
    for copy in reads:
        copy.start()

    owned = owners.shape[-1] // replicas
    per_group = columns // groups
    steps = len(rounds(replicas)) + 1 if apart else replicas
    to_step, to_column, to_row, to_col, end = plan_sizes(len(tiles), steps)

    def owner_of(row):
        owner = jnp.int32(0)
        for one in range(1, replicas):
            owner += (row >= one * owned).astype(jnp.int32)
        return owner

    odd = lax.rem(lax.axis_index("pipe"), 2) > 0
    table = [
        jnp.where(odd, other, packed)
        for packed, other in zip(step_table(replicas, 0), step_table(replicas, 1))
    ] if apart else []
    mine = jnp.int32(0)
    for source, packed in enumerate(table):
        mine = jnp.where(replica == source, packed, mine)
    lane = lax.broadcasted_iota(jnp.int32, plan.shape, 1)
    planned = jnp.where((lane >= to_row) & (lane < end), -1, 0)

    for at, (group, slot) in enumerate(tiles):
        owner = owner_of(owners[0, 0, picks[0, 0, group, slot, 0, replica]])
        step = (mine >> 4 * owner) & 15 if apart else owner
        planned = jnp.where(lane == to_step + at, step, planned)
        planned = jnp.where(lane == to_column + at, picks[0, 0, group, slot, 1, replica], planned)

    for origin in range(replicas):
        place_row, place_col = jnp.int32(-1), jnp.int32(0)
        for group, slot in tiles:
            row = owners[0, 0, picks[0, 0, group, slot, 0, origin]] - replica * owned
            here = (row >= 0) & (row < owned)
            place_row = jnp.where(here, row, place_row)
            place_col = jnp.where(
                here, picks[0, 0, group, slot, 1, origin] + group * per_group, place_col
            )
        step = (table[origin] >> 4 * replica) & 15 if apart else origin
        planned = jnp.where(lane == to_row + step, place_row, planned)
        planned = jnp.where(lane == to_col + step, place_col, planned)

    wide = jnp.int32(0)
    if apart:
        spots = [
            picks[0, 0, group, slot, 0, origin] * columns
            + picks[0, 0, group, slot, 1, origin]
            + group * per_group
            for origin in range(replicas)
            for group, slot in tiles
        ]
        for spot in spots:
            seen[spot] = 0
        for spot in spots:
            seen[spot] = seen[spot] + 1
        for at, spot in enumerate(spots):
            origin, (group, slot) = at // len(tiles), tiles[at % len(tiles)]
            owner = owner_of(owners[0, 0, picks[0, 0, group, slot, 0, origin]])
            step = (table[origin] >> 4 * owner) & 15
            bit = jnp.int32(1) << wide_bit(jnp.maximum(step, 1), steps)
            wide = jnp.where((seen[spot] > 1) & (step > 0), wide | bit, wide)
    plan[...] = jnp.where(lane == 0, wide, planned)

    for at, copy in enumerate(reads):
        copy.wait()
        if at < len(tiles):
            picked[at] = read[at].reshape(-1, edge).T


def clear(after, strip, zeros, cleared):
    zeros[...] = jnp.zeros_like(zeros)
    rows = zeros.shape[0]
    writes = [
        pltpu.make_async_copy(zeros, strip.at[0, 0, pl.ds(part * rows, rows)], cleared.at[part])
        for part in range(strip.shape[2] // rows)
    ]
    for write in writes:
        write.start()
    for write in writes:
        write.wait()


def multiply(groups, apart, to_step, to_column, plan, picked, error, *refs):
    returned, carried, outs = refs[:groups], refs[groups : 2 * groups - 1], refs[2 * groups - 1 :]
    mine = lax.axis_index("tensor")
    slots, (edge, tokens) = error.shape[4], picked.shape[1:]
    count = groups * slots
    wide = plan[0, 0]
    columns = [plan[0, to_column + at] for at in range(count)]
    steps = [plan[0, to_step + at] for at in range(count)]
    tiles = []
    for shift in range(groups):
        for slot in range(slots):
            at = shift * slots + slot
            right = returned[shift][0, :, :, column(columns[at], edge)].reshape(tokens, edge)
            extra = error[0, 0, 0, mine, slot] if shift == 0 else carried[shift - 1][slot]
            tile = jnp.dot(picked[at], right, preferred_element_type=jnp.float32)
            tiles.append(tile + extra.astype(jnp.float32))
    if not apart:
        for step, tile in zip(steps, tiles):
            outs[0][step] = tile
        return

    buffers = len(outs) // 2

    def store(step, tile, buffers):
        for at, buffer in enumerate(buffers):

            @pl.when(step == at)
            def _():
                buffer[...] = tile.astype(buffer.dtype)

    for step, tile in zip(steps, tiles):
        bit = (wide >> wide_bit(jnp.maximum(step, 1), buffers)) & 1
        full = jnp.where(step == 0, wide, bit) > 0

        @pl.when(full)
        def _():
            store(step, tile, outs[:buffers])

        @pl.when(jnp.logical_not(full))
        def _():
            store(step, tile, outs[buffers:])


def place(count, alone, to_row, to_col, plan, *refs):
    blocks, strip, staged, sent = refs[:count], refs[-3], refs[-2], refs[-1]
    steps, edge = staged.shape[0], staged.shape[-1]

    rows = [plan[0, to_row + step] for step in range(steps)]
    cols = [plan[0, to_col + step] for step in range(steps)]

    def meets(one, other):
        return (rows[one] == rows[other]) & (cols[one] == cols[other])

    def block_of(step):
        return blocks[0][step] if count == 1 else blocks[step][...]

    def first_of(step):
        first = rows[step] >= 0
        for earlier in range(0 if alone else step):
            first = first & jnp.logical_not(meets(earlier, step))
        return first

    def write_of(step):
        return pltpu.make_async_copy(
            blocks[step] if alone else staged.at[step],
            strip.at[0, 0, column(rows[step], edge), column(cols[step], edge)],
            sent.at[step],
        )

    for step in range(steps):

        @pl.when(first_of(step))
        def _():
            if not alone:
                total = block_of(step).astype(jnp.float32)
                for later in range(step + 1, steps):
                    block = block_of(later).astype(jnp.float32)
                    total = total + jnp.where(meets(step, later), block, 0.0)
                staged[step] = total.astype(staged.dtype)
            write_of(step).start()

    for step in range(steps):

        @pl.when(first_of(step))
        def _():
            write_of(step).wait()


def body(mesh, activations, cotangent, error_tiles, tile_picks, row_owners):
    sections, replicas, groups = mesh.shape["pipe"], mesh.shape["dp"], mesh.shape["tensor"]
    edge = error_tiles.shape[-1]
    slots = tile_picks.shape[4]
    micro, tokens = activations.shape[1:3]
    width = cotangent.shape[-1] * groups
    strip_rows = row_owners.shape[-1] // replicas * edge
    picks = jnp.transpose(tile_picks, (0, 2, 3, 4, 5, 1))

    returned = []
    for shift in range(groups):
        pairs = [
            (
                (section + 1) % sections * groups + (group + shift) % groups,
                section * groups + group,
            )
            for section in range(sections)
            for group in range(groups)
        ]
        returned.append(lax.ppermute(cotangent, ("pipe", "tensor"), pairs))
    apart = replicas <= MOST_STEPS
    tiles, shifts = groups * slots, groups - 1
    steps = len(rounds(replicas)) + 1 if apart else replicas
    picked, plan, *errors = pl.pallas_call(
        functools.partial(pick, shifts, apart, width // edge),
        out_shape=[
            pltpu.VMEM((tiles, edge, micro * tokens), activations.dtype),
            pltpu.VMEM((1, -(-plan_sizes(tiles, steps)[-1] // 128) * 128), jnp.int32),
        ]
        + [pltpu.VMEM((slots, edge, edge), error_tiles.dtype)] * shifts,
        in_specs=[SMEM, SMEM, ANY, ANY],
        out_specs=[VMEM] * (2 + shifts),
        scratch_shapes=[
            pltpu.VMEM((tiles, micro, tokens, edge), activations.dtype),
            pltpu.SMEM((row_owners.shape[-1] * (width // edge),), jnp.int32),
            pltpu.SemaphoreType.DMA((tiles + shifts,)),
        ],
        compiler_params=SMALL,
        name="pick",
    )(in_hbm(picks), in_hbm(row_owners), in_hbm(activations), in_hbm(error_tiles))
    carried = [
        lax.ppermute(
            error, "tensor", [((group + shift + 1) % groups, group) for group in range(groups)]
        )
        for shift, error in enumerate(errors)
    ]

    zero_rows = min(strip_rows, 256)
    strip_shape = (1, 1, strip_rows, width)
    cleared = pl.pallas_call(
        clear,
        out_shape=pltpu.HBM(strip_shape, jnp.bfloat16),
        in_specs=[ANY],
        out_specs=pl.BlockSpec(memory_space=pltpu.HBM),
        scratch_shapes=[
            pltpu.VMEM((zero_rows, width), jnp.bfloat16),
            pltpu.SemaphoreType.DMA((strip_rows // zero_rows,)),
        ],
        compiler_params=SMALL,
        cost_estimate=pl.CostEstimate(
            flops=0, bytes_accessed=2 * strip_rows * width, transcendentals=0
        ),
        name="clear",
    )(picked)

    to_step, to_column, to_row, to_col, _ = plan_sizes(tiles, steps)
    tile_shape = (edge, edge)
    if apart:
        out_shape = [
            jax.ShapeDtypeStruct(tile_shape, dtype)
            for dtype in (jnp.float32, jnp.bfloat16)
            for step in range(steps)
        ]
    else:
        out_shape = [jax.ShapeDtypeStruct((replicas,) + tile_shape, jnp.float32)]
    outgoing = pl.pallas_call(
        functools.partial(multiply, groups, apart, to_step, to_column),
        out_shape=out_shape,
        in_specs=[VMEM] * (2 * groups + 2),
        out_specs=[VMEM] * len(out_shape),
        compiler_params=SMALL,
        name="multiply",
    )(plan, picked, error_tiles, *returned, *carried)

    def placed(alone, incoming, strip, first=0):
        count = len(incoming) if apart else replicas
        return pl.pallas_call(
            functools.partial(place, len(incoming), alone, to_row + first, to_col + first),
            out_shape=jax.ShapeDtypeStruct(strip_shape, jnp.bfloat16),
            in_specs=[VMEM] * (1 + len(incoming)) + [ANY],
            out_specs=ANY,
            scratch_shapes=[
                pltpu.VMEM((count,) + tile_shape, jnp.bfloat16),
                pltpu.SemaphoreType.DMA((count,)),
            ],
            input_output_aliases={1 + len(incoming): 0},
            compiler_params=SMALL,
            name="place",
        )(plan, *incoming, strip)

    def exchanged(blocks):
        moved = []
        for at, block in enumerate(blocks[1:]):
            pairs = [
                (section * replicas + source, section * replicas + target)
                for section in range(sections)
                for source, target in enumerate(rounds(replicas, section % 2)[at])
            ]
            moved.append(lax.ppermute(block, ("pipe", "dp"), pairs))
        return [blocks[0], *moved]

    if not apart:
        swapped = lax.all_to_all(outgoing[0], "dp", split_axis=0, concat_axis=0, tiled=True)
        return placed(False, [swapped], cleared)
    def branch(wide):
        blocks = [
            outgoing[at if (wide >> wide_bit(at, steps) & 1 if at else wide) else steps + at]
            for at in range(steps)
        ]
        def run():
            arrived = exchanged(blocks)
            if wide:
                return placed(False, arrived, cleared)
            return placed(True, arrived[2:], placed(True, arrived[:2], cleared), 2)

        return run

    sets = 1 << (wide_bit(steps - 1, steps) + 1)
    return lax.switch(plan[0, 0], [branch(wide) for wide in range(sets)])


def solution(mesh):
    in_specs = (
        P("pipe", None, "dp", "tensor"),
        P("pipe", None, "dp", "tensor"),
        P("pipe", "dp", "tensor", None, None, None, None),
        P("pipe", None, "tensor", None, None, None),
        P("pipe", "tensor", None),
    )
    out_specs = P("pipe", "tensor", "dp", None)
    return jax.shard_map(
        functools.partial(body, mesh),
        mesh=mesh,
        in_specs=in_specs,
        out_specs=out_specs,
        check_vma=False,
    )
```

```python
import functools

import jax
import jax.numpy as jnp
from jax import lax
from jax.experimental import pallas as pl
from jax.experimental.pallas import tpu as pltpu
from jax.sharding import PartitionSpec as P

VMEM = pl.BlockSpec(memory_space=pltpu.VMEM)
SMEM = pl.BlockSpec(memory_space=pltpu.SMEM)
ANY = pl.BlockSpec(memory_space=pl.ANY)
MOST_STEPS = 8
ROUNDS = {4: [(1, 3, 0, 2), (3, 2, 1, 0), (2, 0, 3, 1)]}
SMALL = pltpu.CompilerParams(vmem_limit_bytes=4 << 20)


def in_hbm(value):
    return pltpu.with_memory_space_constraint(value, pltpu.HBM)


def column(index, edge):
    return pl.ds(pl.multiple_of(index * edge, edge), edge)


def rounds(replicas):
    shifts = [
        tuple((one + step) % replicas for one in range(replicas)) for step in range(1, replicas)
    ]
    return ROUNDS.get(replicas, shifts)


def step_table(replicas):
    table = []
    for source in range(replicas):
        steps = [0] * replicas
        for step, targets in reversed(list(enumerate(rounds(replicas), 1))):
            steps[targets[source]] = step
        table.append(sum(step << 4 * target for target, step in enumerate(steps)))
    return table


def wide_bit(step, count):
    return step - 1 if count <= 4 else 0


def plan_sizes(tiles, steps):
    return 1, 1 + tiles, 1 + 2 * tiles, 1 + 2 * tiles + steps, 1 + 2 * tiles + 2 * steps


def pick(shifts, apart, columns, picks, owners, activations, errors, picked, plan, *refs):
    cuts, (read, seen, copied) = refs[:shifts], refs[shifts:]
    replica, group_at = lax.axis_index("dp"), lax.axis_index("tensor")
    groups, slots, replicas = picks.shape[2], picks.shape[3], picks.shape[-1]
    edge = picked.shape[1]
    tiles = [
        (lax.rem(group_at + shift, groups), slot) for shift in range(groups) for slot in range(slots)
    ]
    reads = []
    for at, (group, slot) in enumerate(tiles):
        block = picks[0, 0, group, slot, 0, replica]
        reads.append(
            pltpu.make_async_copy(
                activations.at[0, :, :, column(block, edge)], read.at[at], copied.at[at]
            )
        )
    for shift, cut in enumerate(cuts):
        other = lax.rem(group_at + groups - shift - 1, groups)
        reads.append(
            pltpu.make_async_copy(errors.at[0, 0, 0, other], cut, copied.at[len(tiles) + shift])
        )
    for copy in reads:
        copy.start()

    owned = owners.shape[-1] // replicas
    per_group = columns // groups
    steps = len(rounds(replicas)) + 1 if apart else replicas
    to_step, to_column, to_row, to_col, end = plan_sizes(len(tiles), steps)

    def owner_of(row):
        owner = jnp.int32(0)
        for one in range(1, replicas):
            owner += (row >= one * owned).astype(jnp.int32)
        return owner

    table = step_table(replicas) if apart else []
    mine = jnp.int32(0)
    for source, packed in enumerate(table):
        mine = jnp.where(replica == source, packed, mine)
    lane = lax.broadcasted_iota(jnp.int32, plan.shape, 1)
    planned = jnp.where((lane >= to_row) & (lane < end), -1, 0)

    for at, (group, slot) in enumerate(tiles):
        owner = owner_of(owners[0, 0, picks[0, 0, group, slot, 0, replica]])
        step = (mine >> 4 * owner) & 15 if apart else owner
        planned = jnp.where(lane == to_step + at, step, planned)
        planned = jnp.where(lane == to_column + at, picks[0, 0, group, slot, 1, replica], planned)

    for origin in range(replicas):
        place_row, place_col = jnp.int32(-1), jnp.int32(0)
        for group, slot in tiles:
            row = owners[0, 0, picks[0, 0, group, slot, 0, origin]] - replica * owned
            here = (row >= 0) & (row < owned)
            place_row = jnp.where(here, row, place_row)
            place_col = jnp.where(
                here, picks[0, 0, group, slot, 1, origin] + group * per_group, place_col
            )
        step = (jnp.int32(table[origin]) >> 4 * replica) & 15 if apart else origin
        planned = jnp.where(lane == to_row + step, place_row, planned)
        planned = jnp.where(lane == to_col + step, place_col, planned)

    wide = jnp.int32(0)
    if apart:
        spots = [
            picks[0, 0, group, slot, 0, origin] * columns
            + picks[0, 0, group, slot, 1, origin]
            + group * per_group
            for origin in range(replicas)
            for group, slot in tiles
        ]
        for spot in spots:
            seen[spot] = 0
        for spot in spots:
            seen[spot] = seen[spot] + 1
        for at, spot in enumerate(spots):
            origin, (group, slot) = at // len(tiles), tiles[at % len(tiles)]
            owner = owner_of(owners[0, 0, picks[0, 0, group, slot, 0, origin]])
            step = (jnp.int32(table[origin]) >> 4 * owner) & 15
            bit = jnp.int32(1) << wide_bit(jnp.maximum(step, 1), steps)
            wide = jnp.where((seen[spot] > 1) & (step > 0), wide | bit, wide)
    plan[...] = jnp.where(lane == 0, wide, planned)

    for at, copy in enumerate(reads):
        copy.wait()
        if at < len(tiles):
            picked[at] = read[at].reshape(-1, edge).T


def clear(after, strip, zeros, cleared):
    zeros[...] = jnp.zeros_like(zeros)
    rows = zeros.shape[0]
    writes = [
        pltpu.make_async_copy(zeros, strip.at[0, 0, pl.ds(part * rows, rows)], cleared.at[part])
        for part in range(strip.shape[2] // rows)
    ]
    for write in writes:
        write.start()
    for write in writes:
        write.wait()


def multiply(groups, apart, to_step, to_column, plan, picked, error, *refs):
    returned, carried, outs = refs[:groups], refs[groups : 2 * groups - 1], refs[2 * groups - 1 :]
    mine = lax.axis_index("tensor")
    slots, (edge, tokens) = error.shape[4], picked.shape[1:]
    count = groups * slots
    wide = plan[0, 0]
    columns = [plan[0, to_column + at] for at in range(count)]
    steps = [plan[0, to_step + at] for at in range(count)]
    tiles = []
    for shift in range(groups):
        for slot in range(slots):
            at = shift * slots + slot
            right = returned[shift][0, :, :, column(columns[at], edge)].reshape(tokens, edge)
            extra = error[0, 0, 0, mine, slot] if shift == 0 else carried[shift - 1][slot]
            tile = jnp.dot(picked[at], right, preferred_element_type=jnp.float32)
            tiles.append(tile + extra.astype(jnp.float32))
    if not apart:
        for step, tile in zip(steps, tiles):
            outs[0][step] = tile
        return

    buffers = len(outs) // 2

    def store(step, tile, buffers):
        for at, buffer in enumerate(buffers):

            @pl.when(step == at)
            def _():
                buffer[...] = tile.astype(buffer.dtype)

    for step, tile in zip(steps, tiles):
        bit = (wide >> wide_bit(jnp.maximum(step, 1), buffers)) & 1
        full = jnp.where(step == 0, wide, bit) > 0

        @pl.when(full)
        def _():
            store(step, tile, outs[:buffers])

        @pl.when(jnp.logical_not(full))
        def _():
            store(step, tile, outs[buffers:])


def place(count, alone, to_row, to_col, plan, *refs):
    blocks, strip, staged, sent = refs[:count], refs[-3], refs[-2], refs[-1]
    steps, edge = staged.shape[0], staged.shape[-1]

    rows = [plan[0, to_row + step] for step in range(steps)]
    cols = [plan[0, to_col + step] for step in range(steps)]

    def meets(one, other):
        return (rows[one] == rows[other]) & (cols[one] == cols[other])

    def block_of(step):
        return blocks[0][step] if count == 1 else blocks[step][...]

    def first_of(step):
        first = rows[step] >= 0
        for earlier in range(0 if alone else step):
            first = first & jnp.logical_not(meets(earlier, step))
        return first

    def write_of(step):
        return pltpu.make_async_copy(
            blocks[step] if alone else staged.at[step],
            strip.at[0, 0, column(rows[step], edge), column(cols[step], edge)],
            sent.at[step],
        )

    for step in range(steps):

        @pl.when(first_of(step))
        def _():
            if not alone:
                total = block_of(step).astype(jnp.float32)
                for later in range(step + 1, steps):
                    block = block_of(later).astype(jnp.float32)
                    total = total + jnp.where(meets(step, later), block, 0.0)
                staged[step] = total.astype(staged.dtype)
            write_of(step).start()

    for step in range(steps):

        @pl.when(first_of(step))
        def _():
            write_of(step).wait()


def body(mesh, activations, cotangent, error_tiles, tile_picks, row_owners):
    sections, replicas, groups = mesh.shape["pipe"], mesh.shape["dp"], mesh.shape["tensor"]
    edge = error_tiles.shape[-1]
    slots = tile_picks.shape[4]
    micro, tokens = activations.shape[1:3]
    width = cotangent.shape[-1] * groups
    strip_rows = row_owners.shape[-1] // replicas * edge
    picks = jnp.transpose(tile_picks, (0, 2, 3, 4, 5, 1))

    returned = []
    for shift in range(groups):
        pairs = [
            (
                (section + 1) % sections * groups + (group + shift) % groups,
                section * groups + group,
            )
            for section in range(sections)
            for group in range(groups)
        ]
        returned.append(lax.ppermute(cotangent, ("pipe", "tensor"), pairs))
    apart = replicas <= MOST_STEPS
    tiles, shifts = groups * slots, groups - 1
    steps = len(rounds(replicas)) + 1 if apart else replicas
    picked, plan, *errors = pl.pallas_call(
        functools.partial(pick, shifts, apart, width // edge),
        out_shape=[
            pltpu.VMEM((tiles, edge, micro * tokens), activations.dtype),
            pltpu.VMEM((1, -(-plan_sizes(tiles, steps)[-1] // 128) * 128), jnp.int32),
        ]
        + [pltpu.VMEM((slots, edge, edge), error_tiles.dtype)] * shifts,
        in_specs=[SMEM, SMEM, ANY, ANY],
        out_specs=[VMEM] * (2 + shifts),
        scratch_shapes=[
            pltpu.VMEM((tiles, micro, tokens, edge), activations.dtype),
            pltpu.SMEM((row_owners.shape[-1] * (width // edge),), jnp.int32),
            pltpu.SemaphoreType.DMA((tiles + shifts,)),
        ],
        compiler_params=SMALL,
        name="pick",
    )(in_hbm(picks), in_hbm(row_owners), in_hbm(activations), in_hbm(error_tiles))
    carried = [
        lax.ppermute(
            error, "tensor", [((group + shift + 1) % groups, group) for group in range(groups)]
        )
        for shift, error in enumerate(errors)
    ]

    zero_rows = min(strip_rows, 256)
    strip_shape = (1, 1, strip_rows, width)
    cleared = pl.pallas_call(
        clear,
        out_shape=pltpu.HBM(strip_shape, jnp.bfloat16),
        in_specs=[ANY],
        out_specs=pl.BlockSpec(memory_space=pltpu.HBM),
        scratch_shapes=[
            pltpu.VMEM((zero_rows, width), jnp.bfloat16),
            pltpu.SemaphoreType.DMA((strip_rows // zero_rows,)),
        ],
        compiler_params=SMALL,
        cost_estimate=pl.CostEstimate(
            flops=0, bytes_accessed=2 * strip_rows * width, transcendentals=0
        ),
        name="clear",
    )(picked)

    to_step, to_column, to_row, to_col, _ = plan_sizes(tiles, steps)
    tile_shape = (edge, edge)
    if apart:
        out_shape = [
            jax.ShapeDtypeStruct(tile_shape, dtype)
            for dtype in (jnp.float32, jnp.bfloat16)
            for step in range(steps)
        ]
    else:
        out_shape = [jax.ShapeDtypeStruct((replicas,) + tile_shape, jnp.float32)]
    outgoing = pl.pallas_call(
        functools.partial(multiply, groups, apart, to_step, to_column),
        out_shape=out_shape,
        in_specs=[VMEM] * (2 * groups + 2),
        out_specs=[VMEM] * len(out_shape),
        compiler_params=SMALL,
        name="multiply",
    )(plan, picked, error_tiles, *returned, *carried)

    def placed(alone, incoming, strip, first=0):
        count = len(incoming) if apart else replicas
        return pl.pallas_call(
            functools.partial(place, len(incoming), alone, to_row + first, to_col + first),
            out_shape=jax.ShapeDtypeStruct(strip_shape, jnp.bfloat16),
            in_specs=[VMEM] * (1 + len(incoming)) + [ANY],
            out_specs=ANY,
            scratch_shapes=[
                pltpu.VMEM((count,) + tile_shape, jnp.bfloat16),
                pltpu.SemaphoreType.DMA((count,)),
            ],
            input_output_aliases={1 + len(incoming): 0},
            compiler_params=SMALL,
            name="place",
        )(plan, *incoming, strip)

    def exchanged(blocks):
        moved = [
            lax.ppermute(block, "dp", list(enumerate(targets)))
            for block, targets in zip(blocks[1:], rounds(replicas))
        ]
        return [blocks[0], *moved]

    if not apart:
        swapped = lax.all_to_all(outgoing[0], "dp", split_axis=0, concat_axis=0, tiled=True)
        return placed(False, [swapped], cleared)
    def branch(wide):
        blocks = [
            outgoing[at if (wide >> wide_bit(at, steps) & 1 if at else wide) else steps + at]
            for at in range(steps)
        ]
        def run():
            arrived = exchanged(blocks)
            if wide:
                return placed(False, arrived, cleared)
            return placed(True, arrived[2:], placed(True, arrived[:2], cleared), 2)

        return run

    sets = 1 << (wide_bit(steps - 1, steps) + 1)
    return lax.switch(plan[0, 0], [branch(wide) for wide in range(sets)])


def solution(mesh):
    in_specs = (
        P("pipe", None, "dp", "tensor"),
        P("pipe", None, "dp", "tensor"),
        P("pipe", "dp", "tensor", None, None, None, None),
        P("pipe", None, "tensor", None, None, None),
        P("pipe", "tensor", None),
    )
    out_specs = P("pipe", "tensor", "dp", None)
    return jax.shard_map(
        functools.partial(body, mesh),
        mesh=mesh,
        in_specs=in_specs,
        out_specs=out_specs,
        check_vma=False,
    )
```

```python
import functools

import jax
import jax.numpy as jnp
from jax import lax
from jax.experimental import pallas as pl
from jax.experimental.pallas import tpu as pltpu
from jax.sharding import PartitionSpec as P

VMEM = pl.BlockSpec(memory_space=pltpu.VMEM)
SMEM = pl.BlockSpec(memory_space=pltpu.SMEM)
ANY = pl.BlockSpec(memory_space=pl.ANY)
MOST_STEPS = 8
ROUNDS = {4: [(2, 3, 1, 0), (3, 2, 0, 1), (1, 0, 3, 2)]}
SMALL = pltpu.CompilerParams(vmem_limit_bytes=4 << 20)


def in_hbm(value):
    return pltpu.with_memory_space_constraint(value, pltpu.HBM)


def column(index, edge):
    return pl.ds(pl.multiple_of(index * edge, edge), edge)


def rounds(replicas):
    shifts = [
        tuple((one + step) % replicas for one in range(replicas)) for step in range(1, replicas)
    ]
    return ROUNDS.get(replicas, shifts)


def step_table(replicas):
    table = []
    for source in range(replicas):
        steps = [0] * replicas
        for step, targets in reversed(list(enumerate(rounds(replicas), 1))):
            steps[targets[source]] = step
        table.append(sum(step << 4 * target for target, step in enumerate(steps)))
    return table


def wide_bit(step, count):
    return step - 1 if count <= 4 else 0


def plan_sizes(tiles, steps):
    return 1, 1 + tiles, 1 + 2 * tiles, 1 + 2 * tiles + steps, 1 + 2 * tiles + 2 * steps


def pick(apart, columns, picks, owners, activations, picked, plan, read, seen, copied):
    replica, group_at = lax.axis_index("dp"), lax.axis_index("tensor")
    groups, slots, replicas = picks.shape[2], picks.shape[3], picks.shape[-1]
    edge = picked.shape[1]
    tiles = [
        (lax.rem(group_at + shift, groups), slot) for shift in range(groups) for slot in range(slots)
    ]
    reads = []
    for at, (group, slot) in enumerate(tiles):
        block = picks[0, 0, group, slot, 0, replica]
        reads.append(
            pltpu.make_async_copy(
                activations.at[0, :, :, column(block, edge)], read.at[at], copied.at[at]
            )
        )
    for copy in reads:
        copy.start()

    owned = owners.shape[-1] // replicas
    per_group = columns // groups
    steps = len(rounds(replicas)) + 1 if apart else replicas
    to_step, to_column, to_row, to_col, end = plan_sizes(len(tiles), steps)

    def owner_of(row):
        owner = jnp.int32(0)
        for one in range(1, replicas):
            owner += (row >= one * owned).astype(jnp.int32)
        return owner

    table = step_table(replicas) if apart else []
    mine = jnp.int32(0)
    for source, packed in enumerate(table):
        mine = jnp.where(replica == source, packed, mine)
    lane = lax.broadcasted_iota(jnp.int32, plan.shape, 1)
    planned = jnp.where((lane >= to_row) & (lane < end), -1, 0)

    for at, (group, slot) in enumerate(tiles):
        owner = owner_of(owners[0, 0, picks[0, 0, group, slot, 0, replica]])
        step = (mine >> 4 * owner) & 15 if apart else owner
        planned = jnp.where(lane == to_step + at, step, planned)
        planned = jnp.where(lane == to_column + at, picks[0, 0, group, slot, 1, replica], planned)

    for origin in range(replicas):
        place_row, place_col = jnp.int32(-1), jnp.int32(0)
        for group, slot in tiles:
            row = owners[0, 0, picks[0, 0, group, slot, 0, origin]] - replica * owned
            here = (row >= 0) & (row < owned)
            place_row = jnp.where(here, row, place_row)
            place_col = jnp.where(
                here, picks[0, 0, group, slot, 1, origin] + group * per_group, place_col
            )
        step = (jnp.int32(table[origin]) >> 4 * replica) & 15 if apart else origin
        planned = jnp.where(lane == to_row + step, place_row, planned)
        planned = jnp.where(lane == to_col + step, place_col, planned)

    wide = jnp.int32(0)
    if apart:
        spots = [
            picks[0, 0, group, slot, 0, origin] * columns
            + picks[0, 0, group, slot, 1, origin]
            + group * per_group
            for origin in range(replicas)
            for group, slot in tiles
        ]
        for spot in spots:
            seen[spot] = 0
        for spot in spots:
            seen[spot] = seen[spot] + 1
        for at, spot in enumerate(spots):
            origin, (group, slot) = at // len(tiles), tiles[at % len(tiles)]
            owner = owner_of(owners[0, 0, picks[0, 0, group, slot, 0, origin]])
            step = (jnp.int32(table[origin]) >> 4 * owner) & 15
            bit = jnp.int32(1) << wide_bit(jnp.maximum(step, 1), steps)
            wide = jnp.where((seen[spot] > 1) & (step > 0), wide | bit, wide)
    plan[...] = jnp.where(lane == 0, wide, planned)

    for at, copy in enumerate(reads):
        copy.wait()
        picked[at] = read[at].reshape(-1, edge).T


def clear(after, strip, zeros, cleared):
    zeros[...] = jnp.zeros_like(zeros)
    rows = zeros.shape[0]
    writes = [
        pltpu.make_async_copy(zeros, strip.at[0, 0, pl.ds(part * rows, rows)], cleared.at[part])
        for part in range(strip.shape[2] // rows)
    ]
    for write in writes:
        write.start()
    for write in writes:
        write.wait()


def multiply(groups, apart, to_step, to_column, plan, picked, error, *refs):
    returned, carried, outs = refs[:groups], refs[groups : 2 * groups - 1], refs[2 * groups - 1 :]
    mine = lax.axis_index("tensor")
    slots, (edge, tokens) = error.shape[4], picked.shape[1:]
    count = groups * slots
    wide = plan[0, 0]
    columns = [plan[0, to_column + at] for at in range(count)]
    steps = [plan[0, to_step + at] for at in range(count)]
    tiles = []
    for shift in range(groups):
        for slot in range(slots):
            at = shift * slots + slot
            right = returned[shift][0, :, :, column(columns[at], edge)].reshape(tokens, edge)
            extra = error[0, 0, 0, mine, slot] if shift == 0 else carried[shift - 1][0, 0, 0, 0, slot]
            tile = jnp.dot(picked[at], right, preferred_element_type=jnp.float32)
            tiles.append(tile + extra.astype(jnp.float32))
    if not apart:
        for step, tile in zip(steps, tiles):
            outs[0][step] = tile
        return

    buffers = len(outs) // 2

    def store(step, tile, buffers):
        for at, buffer in enumerate(buffers):

            @pl.when(step == at)
            def _():
                buffer[...] = tile.astype(buffer.dtype)

    for step, tile in zip(steps, tiles):
        bit = (wide >> wide_bit(jnp.maximum(step, 1), buffers)) & 1
        full = jnp.where(step == 0, wide, bit) > 0

        @pl.when(full)
        def _():
            store(step, tile, outs[:buffers])

        @pl.when(jnp.logical_not(full))
        def _():
            store(step, tile, outs[buffers:])


def place(count, alone, to_row, to_col, plan, *refs):
    blocks, strip, staged, sent = refs[:count], refs[-3], refs[-2], refs[-1]
    steps, edge = staged.shape[0], staged.shape[-1]

    rows = [plan[0, to_row + step] for step in range(steps)]
    cols = [plan[0, to_col + step] for step in range(steps)]

    def meets(one, other):
        return (rows[one] == rows[other]) & (cols[one] == cols[other])

    def block_of(step):
        return blocks[0][step] if count == 1 else blocks[step][...]

    def first_of(step):
        first = rows[step] >= 0
        for earlier in range(0 if alone else step):
            first = first & jnp.logical_not(meets(earlier, step))
        return first

    def write_of(step):
        return pltpu.make_async_copy(
            blocks[step] if alone else staged.at[step],
            strip.at[0, 0, column(rows[step], edge), column(cols[step], edge)],
            sent.at[step],
        )

    for step in range(steps):

        @pl.when(first_of(step))
        def _():
            if not alone:
                total = block_of(step).astype(jnp.float32)
                for later in range(step + 1, steps):
                    block = block_of(later).astype(jnp.float32)
                    total = total + jnp.where(meets(step, later), block, 0.0)
                staged[step] = total.astype(staged.dtype)
            write_of(step).start()

    for step in range(steps):

        @pl.when(first_of(step))
        def _():
            write_of(step).wait()


def body(mesh, activations, cotangent, error_tiles, tile_picks, row_owners):
    sections, replicas, groups = mesh.shape["pipe"], mesh.shape["dp"], mesh.shape["tensor"]
    edge = error_tiles.shape[-1]
    slots = tile_picks.shape[4]
    micro, tokens = activations.shape[1:3]
    width = cotangent.shape[-1] * groups
    strip_rows = row_owners.shape[-1] // replicas * edge
    picks = jnp.transpose(tile_picks, (0, 2, 3, 4, 5, 1))

    returned = []
    for shift in range(groups):
        pairs = [
            (
                (section + 1) % sections * groups + (group + shift) % groups,
                section * groups + group,
            )
            for section in range(sections)
            for group in range(groups)
        ]
        returned.append(lax.ppermute(cotangent, ("pipe", "tensor"), pairs))
    apart = replicas <= MOST_STEPS
    tiles = groups * slots
    steps = len(rounds(replicas)) + 1 if apart else replicas
    mine = lax.axis_index("tensor")
    carried = [
        lax.ppermute(
            lax.dynamic_index_in_dim(error_tiles, (mine - shift + groups) % groups, axis=3),
            "tensor",
            [((group + shift) % groups, group) for group in range(groups)],
        )
        for shift in range(1, groups)
    ]
    picked, plan = pl.pallas_call(
        functools.partial(pick, apart, width // edge),
        out_shape=[
            pltpu.VMEM((tiles, edge, micro * tokens), activations.dtype),
            pltpu.VMEM((1, -(-plan_sizes(tiles, steps)[-1] // 128) * 128), jnp.int32),
        ],
        in_specs=[SMEM, SMEM, ANY],
        out_specs=[VMEM] * 2,
        scratch_shapes=[
            pltpu.VMEM((tiles, micro, tokens, edge), activations.dtype),
            pltpu.SMEM((row_owners.shape[-1] * (width // edge),), jnp.int32),
            pltpu.SemaphoreType.DMA((tiles,)),
        ],
        compiler_params=SMALL,
        name="pick",
    )(in_hbm(picks), in_hbm(row_owners), in_hbm(activations))

    zero_rows = min(strip_rows, 256)
    strip_shape = (1, 1, strip_rows, width)
    cleared = pl.pallas_call(
        clear,
        out_shape=pltpu.HBM(strip_shape, jnp.bfloat16),
        in_specs=[ANY],
        out_specs=pl.BlockSpec(memory_space=pltpu.HBM),
        scratch_shapes=[
            pltpu.VMEM((zero_rows, width), jnp.bfloat16),
            pltpu.SemaphoreType.DMA((strip_rows // zero_rows,)),
        ],
        compiler_params=SMALL,
        cost_estimate=pl.CostEstimate(
            flops=0, bytes_accessed=2 * strip_rows * width, transcendentals=0
        ),
        name="clear",
    )(picked)

    to_step, to_column, to_row, to_col, _ = plan_sizes(tiles, steps)
    tile_shape = (edge, edge)
    if apart:
        out_shape = [
            jax.ShapeDtypeStruct(tile_shape, dtype)
            for dtype in (jnp.float32, jnp.bfloat16)
            for step in range(steps)
        ]
    else:
        out_shape = [jax.ShapeDtypeStruct((replicas,) + tile_shape, jnp.float32)]
    outgoing = pl.pallas_call(
        functools.partial(multiply, groups, apart, to_step, to_column),
        out_shape=out_shape,
        in_specs=[VMEM] * (2 * groups + 2),
        out_specs=[VMEM] * len(out_shape),
        compiler_params=SMALL,
        name="multiply",
    )(plan, picked, error_tiles, *returned, *carried)

    def placed(alone, incoming, strip, first=0):
        count = len(incoming) if apart else replicas
        return pl.pallas_call(
            functools.partial(place, len(incoming), alone, to_row + first, to_col + first),
            out_shape=jax.ShapeDtypeStruct(strip_shape, jnp.bfloat16),
            in_specs=[VMEM] * (1 + len(incoming)) + [ANY],
            out_specs=ANY,
            scratch_shapes=[
                pltpu.VMEM((count,) + tile_shape, jnp.bfloat16),
                pltpu.SemaphoreType.DMA((count,)),
            ],
            input_output_aliases={1 + len(incoming): 0},
            compiler_params=SMALL,
            name="place",
        )(plan, *incoming, strip)

    def exchanged(blocks):
        moved = [
            lax.ppermute(block, "dp", list(enumerate(targets)))
            for block, targets in zip(blocks[1:], rounds(replicas))
        ]
        return [blocks[0], *moved]

    if not apart:
        swapped = lax.all_to_all(outgoing[0], "dp", split_axis=0, concat_axis=0, tiled=True)
        return placed(False, [swapped], cleared)
    def branch(wide):
        blocks = [
            outgoing[at if (wide >> wide_bit(at, steps) & 1 if at else wide) else steps + at]
            for at in range(steps)
        ]
        def run():
            arrived = exchanged(blocks)
            if wide:
                return placed(False, arrived, cleared)
            return placed(True, arrived[2:], placed(True, arrived[:2], cleared), 2)

        return run

    sets = 1 << (wide_bit(steps - 1, steps) + 1)
    return lax.switch(plan[0, 0], [branch(wide) for wide in range(sets)])


def solution(mesh):
    in_specs = (
        P("pipe", None, "dp", "tensor"),
        P("pipe", None, "dp", "tensor"),
        P("pipe", "dp", "tensor", None, None, None, None),
        P("pipe", None, "tensor", None, None, None),
        P("pipe", "tensor", None),
    )
    out_specs = P("pipe", "tensor", "dp", None)
    return jax.shard_map(
        functools.partial(body, mesh),
        mesh=mesh,
        in_specs=in_specs,
        out_specs=out_specs,
        check_vma=False,
    )
```

```python
import functools

import jax
import jax.numpy as jnp
from jax import lax
from jax.experimental import pallas as pl
from jax.experimental.pallas import tpu as pltpu
from jax.sharding import PartitionSpec as P

VMEM = pl.BlockSpec(memory_space=pltpu.VMEM)
SMEM = pl.BlockSpec(memory_space=pltpu.SMEM)
ANY = pl.BlockSpec(memory_space=pl.ANY)
MOST_STEPS = 8
ROUNDS = {4: [(2, 3, 1, 0), (3, 2, 0, 1), (1, 0, 3, 2)]}
SMALL = pltpu.CompilerParams(vmem_limit_bytes=4 << 20)


def in_hbm(value):
    return pltpu.with_memory_space_constraint(value, pltpu.HBM)


def column(index, edge):
    return pl.ds(pl.multiple_of(index * edge, edge), edge)


def rounds(replicas):
    shifts = [
        tuple((one + step) % replicas for one in range(replicas)) for step in range(1, replicas)
    ]
    return ROUNDS.get(replicas, shifts)


def step_table(replicas):
    table = []
    for source in range(replicas):
        steps = [0] * replicas
        for step, targets in reversed(list(enumerate(rounds(replicas), 1))):
            steps[targets[source]] = step
        table.append(sum(step << 4 * target for target, step in enumerate(steps)))
    return table


def wide_bit(step, count):
    return step - 1 if count <= 4 else 0


def plan_sizes(tiles, steps):
    return 1, 1 + tiles, 1 + 2 * tiles, 1 + 2 * tiles + steps, 1 + 2 * tiles + 2 * steps


def pick(apart, columns, picks, owners, activations, picked, plan, read, seen, copied):
    replica, group_at = lax.axis_index("dp"), lax.axis_index("tensor")
    groups, slots, replicas = picks.shape[2], picks.shape[3], picks.shape[-1]
    edge = picked.shape[1]
    tiles = [
        (lax.rem(group_at + shift, groups), slot) for shift in range(groups) for slot in range(slots)
    ]
    reads = []
    for at, (group, slot) in enumerate(tiles):
        block = picks[0, 0, group, slot, 0, replica]
        reads.append(
            pltpu.make_async_copy(
                activations.at[0, :, :, column(block, edge)], read.at[at], copied.at[at]
            )
        )
    for copy in reads:
        copy.start()

    owned = owners.shape[-1] // replicas
    per_group = columns // groups
    steps = len(rounds(replicas)) + 1 if apart else replicas
    to_step, to_column, to_row, to_col, end = plan_sizes(len(tiles), steps)

    def owner_of(row):
        owner = jnp.int32(0)
        for one in range(1, replicas):
            owner += (row >= one * owned).astype(jnp.int32)
        return owner

    table = step_table(replicas) if apart else []
    mine = jnp.int32(0)
    for source, packed in enumerate(table):
        mine = jnp.where(replica == source, packed, mine)
    lane = lax.broadcasted_iota(jnp.int32, plan.shape, 1)
    planned = jnp.where((lane >= to_row) & (lane < end), -1, 0)

    for at, (group, slot) in enumerate(tiles):
        owner = owner_of(owners[0, 0, picks[0, 0, group, slot, 0, replica]])
        step = (mine >> 4 * owner) & 15 if apart else owner
        planned = jnp.where(lane == to_step + at, step, planned)
        planned = jnp.where(lane == to_column + at, picks[0, 0, group, slot, 1, replica], planned)

    for origin in range(replicas):
        place_row, place_col = jnp.int32(-1), jnp.int32(0)
        for group, slot in tiles:
            row = owners[0, 0, picks[0, 0, group, slot, 0, origin]] - replica * owned
            here = (row >= 0) & (row < owned)
            place_row = jnp.where(here, row, place_row)
            place_col = jnp.where(
                here, picks[0, 0, group, slot, 1, origin] + group * per_group, place_col
            )
        step = (jnp.int32(table[origin]) >> 4 * replica) & 15 if apart else origin
        planned = jnp.where(lane == to_row + step, place_row, planned)
        planned = jnp.where(lane == to_col + step, place_col, planned)

    wide = jnp.int32(0)
    if apart:
        spots = [
            picks[0, 0, group, slot, 0, origin] * columns
            + picks[0, 0, group, slot, 1, origin]
            + group * per_group
            for origin in range(replicas)
            for group, slot in tiles
        ]
        for spot in spots:
            seen[spot] = 0
        for spot in spots:
            seen[spot] = seen[spot] + 1
        for at, spot in enumerate(spots):
            origin, (group, slot) = at // len(tiles), tiles[at % len(tiles)]
            owner = owner_of(owners[0, 0, picks[0, 0, group, slot, 0, origin]])
            step = (jnp.int32(table[origin]) >> 4 * owner) & 15
            bit = jnp.int32(1) << wide_bit(jnp.maximum(step, 1), steps)
            wide = jnp.where((seen[spot] > 1) & (step > 0), wide | bit, wide)
    plan[...] = jnp.where(lane == 0, wide, planned)

    for at, copy in enumerate(reads):
        copy.wait()
        picked[at] = read[at].reshape(-1, edge).T


def clear(after, strip, zeros, cleared):
    zeros[...] = jnp.zeros_like(zeros)
    rows = zeros.shape[0]
    writes = [
        pltpu.make_async_copy(zeros, strip.at[0, 0, pl.ds(part * rows, rows)], cleared.at[part])
        for part in range(strip.shape[2] // rows)
    ]
    for write in writes:
        write.start()
    for write in writes:
        write.wait()


def multiply(groups, apart, to_step, to_column, plan, picked, error, *refs):
    returned, carried, outs = refs[:groups], refs[groups : 2 * groups - 1], refs[2 * groups - 1 :]
    mine = lax.axis_index("tensor")
    slots, (edge, tokens) = error.shape[4], picked.shape[1:]
    count = groups * slots
    wide = plan[0, 0]
    columns = [plan[0, to_column + at] for at in range(count)]
    steps = [plan[0, to_step + at] for at in range(count)]
    tiles = []
    for shift in range(groups):
        for slot in range(slots):
            at = shift * slots + slot
            right = returned[shift][0, :, :, column(columns[at], edge)].reshape(tokens, edge)
            extra = error[0, 0, 0, mine, slot] if shift == 0 else carried[shift - 1][0, 0, 0, 0, slot]
            tile = jnp.dot(picked[at], right, preferred_element_type=jnp.float32)
            tiles.append(tile + extra.astype(jnp.float32))
    if not apart:
        for step, tile in zip(steps, tiles):
            outs[0][step] = tile
        return

    buffers = len(outs) // 2

    def store(step, tile, buffers):
        for at, buffer in enumerate(buffers):

            @pl.when(step == at)
            def _():
                buffer[...] = tile.astype(buffer.dtype)

    for step, tile in zip(steps, tiles):
        bit = (wide >> wide_bit(jnp.maximum(step, 1), buffers)) & 1
        full = jnp.where(step == 0, wide, bit) > 0

        @pl.when(full)
        def _():
            store(step, tile, outs[:buffers])

        @pl.when(jnp.logical_not(full))
        def _():
            store(step, tile, outs[buffers:])


def place(count, alone, to_row, to_col, plan, *refs):
    blocks, strip, staged, sent = refs[:count], refs[-3], refs[-2], refs[-1]
    steps, edge = staged.shape[0], staged.shape[-1]

    rows = [plan[0, to_row + step] for step in range(steps)]
    cols = [plan[0, to_col + step] for step in range(steps)]

    def meets(one, other):
        return (rows[one] == rows[other]) & (cols[one] == cols[other])

    def block_of(step):
        return blocks[0][step] if count == 1 else blocks[step][...]

    def first_of(step):
        first = rows[step] >= 0
        for earlier in range(0 if alone else step):
            first = first & jnp.logical_not(meets(earlier, step))
        return first

    def write_of(step):
        return pltpu.make_async_copy(
            blocks[step] if alone else staged.at[step],
            strip.at[0, 0, column(rows[step], edge), column(cols[step], edge)],
            sent.at[step],
        )

    for step in range(steps):

        @pl.when(first_of(step))
        def _():
            if not alone:
                total = block_of(step).astype(jnp.float32)
                for later in range(step + 1, steps):
                    block = block_of(later).astype(jnp.float32)
                    total = total + jnp.where(meets(step, later), block, 0.0)
                staged[step] = total.astype(staged.dtype)
            write_of(step).start(priority=1)

    for step in range(steps):

        @pl.when(first_of(step))
        def _():
            write_of(step).wait()


def body(mesh, activations, cotangent, error_tiles, tile_picks, row_owners):
    sections, replicas, groups = mesh.shape["pipe"], mesh.shape["dp"], mesh.shape["tensor"]
    edge = error_tiles.shape[-1]
    slots = tile_picks.shape[4]
    micro, tokens = activations.shape[1:3]
    width = cotangent.shape[-1] * groups
    strip_rows = row_owners.shape[-1] // replicas * edge
    picks = jnp.transpose(tile_picks, (0, 2, 3, 4, 5, 1))

    returned = []
    for shift in range(groups):
        pairs = [
            (
                (section + 1) % sections * groups + (group + shift) % groups,
                section * groups + group,
            )
            for section in range(sections)
            for group in range(groups)
        ]
        returned.append(lax.ppermute(cotangent, ("pipe", "tensor"), pairs))
    apart = replicas <= MOST_STEPS
    tiles = groups * slots
    steps = len(rounds(replicas)) + 1 if apart else replicas
    mine = lax.axis_index("tensor")
    carried = [
        lax.ppermute(
            lax.dynamic_index_in_dim(error_tiles, (mine - shift + groups) % groups, axis=3),
            "tensor",
            [((group + shift) % groups, group) for group in range(groups)],
        )
        for shift in range(1, groups)
    ]
    picked, plan = pl.pallas_call(
        functools.partial(pick, apart, width // edge),
        out_shape=[
            pltpu.VMEM((tiles, edge, micro * tokens), activations.dtype),
            pltpu.VMEM((1, -(-plan_sizes(tiles, steps)[-1] // 128) * 128), jnp.int32),
        ],
        in_specs=[SMEM, SMEM, ANY],
        out_specs=[VMEM] * 2,
        scratch_shapes=[
            pltpu.VMEM((tiles, micro, tokens, edge), activations.dtype),
            pltpu.SMEM((row_owners.shape[-1] * (width // edge),), jnp.int32),
            pltpu.SemaphoreType.DMA((tiles,)),
        ],
        compiler_params=SMALL,
        name="pick",
    )(in_hbm(picks), in_hbm(row_owners), in_hbm(activations))

    zero_rows = min(strip_rows, 256)
    strip_shape = (1, 1, strip_rows, width)
    cleared = pl.pallas_call(
        clear,
        out_shape=pltpu.HBM(strip_shape, jnp.bfloat16),
        in_specs=[ANY],
        out_specs=pl.BlockSpec(memory_space=pltpu.HBM),
        scratch_shapes=[
            pltpu.VMEM((zero_rows, width), jnp.bfloat16),
            pltpu.SemaphoreType.DMA((strip_rows // zero_rows,)),
        ],
        compiler_params=SMALL,
        cost_estimate=pl.CostEstimate(
            flops=0, bytes_accessed=2 * strip_rows * width, transcendentals=0
        ),
        name="clear",
    )(picked)

    to_step, to_column, to_row, to_col, _ = plan_sizes(tiles, steps)
    tile_shape = (edge, edge)
    if apart:
        out_shape = [
            jax.ShapeDtypeStruct(tile_shape, dtype)
            for dtype in (jnp.float32, jnp.bfloat16)
            for step in range(steps)
        ]
    else:
        out_shape = [jax.ShapeDtypeStruct((replicas,) + tile_shape, jnp.float32)]
    outgoing = pl.pallas_call(
        functools.partial(multiply, groups, apart, to_step, to_column),
        out_shape=out_shape,
        in_specs=[VMEM] * (2 * groups + 2),
        out_specs=[VMEM] * len(out_shape),
        compiler_params=SMALL,
        name="multiply",
    )(plan, picked, error_tiles, *returned, *carried)

    def placed(alone, incoming, strip, first=0):
        count = len(incoming) if apart else replicas
        return pl.pallas_call(
            functools.partial(place, len(incoming), alone, to_row + first, to_col + first),
            out_shape=jax.ShapeDtypeStruct(strip_shape, jnp.bfloat16),
            in_specs=[VMEM] * (1 + len(incoming)) + [ANY],
            out_specs=ANY,
            scratch_shapes=[
                pltpu.VMEM((count,) + tile_shape, jnp.bfloat16),
                pltpu.SemaphoreType.DMA((count,)),
            ],
            input_output_aliases={1 + len(incoming): 0},
            compiler_params=SMALL,
            name="place",
        )(plan, *incoming, strip)

    def exchanged(blocks):
        moved = [
            lax.ppermute(block, "dp", list(enumerate(targets)))
            for block, targets in zip(blocks[1:], rounds(replicas))
        ]
        return [blocks[0], *moved]

    if not apart:
        swapped = lax.all_to_all(outgoing[0], "dp", split_axis=0, concat_axis=0, tiled=True)
        return placed(False, [swapped], cleared)
    def branch(wide):
        blocks = [
            outgoing[at if (wide >> wide_bit(at, steps) & 1 if at else wide) else steps + at]
            for at in range(steps)
        ]
        def run():
            arrived = exchanged(blocks)
            if wide:
                return placed(False, arrived, cleared)
            return placed(True, arrived[2:], placed(True, arrived[:2], cleared), 2)

        return run

    sets = 1 << (wide_bit(steps - 1, steps) + 1)
    return lax.switch(plan[0, 0], [branch(wide) for wide in range(sets)])


def solution(mesh):
    in_specs = (
        P("pipe", None, "dp", "tensor"),
        P("pipe", None, "dp", "tensor"),
        P("pipe", "dp", "tensor", None, None, None, None),
        P("pipe", None, "tensor", None, None, None),
        P("pipe", "tensor", None),
    )
    out_specs = P("pipe", "tensor", "dp", None)
    return jax.shard_map(
        functools.partial(body, mesh),
        mesh=mesh,
        in_specs=in_specs,
        out_specs=out_specs,
        check_vma=False,
    )
```

```python
import functools

import jax
import jax.numpy as jnp
from jax import lax
from jax.experimental import pallas as pl
from jax.experimental.pallas import tpu as pltpu
from jax.sharding import PartitionSpec as P

VMEM = pl.BlockSpec(memory_space=pltpu.VMEM)
SMEM = pl.BlockSpec(memory_space=pltpu.SMEM)
ANY = pl.BlockSpec(memory_space=pl.ANY)
MOST_STEPS = 8
ROUNDS = {4: [(2, 3, 1, 0), (3, 2, 0, 1), (1, 0, 3, 2)]}
SMALL = pltpu.CompilerParams(vmem_limit_bytes=4 << 20)


def in_hbm(value):
    return pltpu.with_memory_space_constraint(value, pltpu.HBM)


def column(index, edge):
    return pl.ds(pl.multiple_of(index * edge, edge), edge)


def rounds(replicas):
    shifts = [
        tuple((one + step) % replicas for one in range(replicas)) for step in range(1, replicas)
    ]
    return ROUNDS.get(replicas, shifts)


def step_table(replicas):
    table = []
    for source in range(replicas):
        steps = [0] * replicas
        for step, targets in reversed(list(enumerate(rounds(replicas), 1))):
            steps[targets[source]] = step
        table.append(sum(step << 4 * target for target, step in enumerate(steps)))
    return table


def wide_bit(step, count):
    return step - 1 if count <= 4 else 0


def plan_sizes(tiles, steps):
    return 1, 1 + tiles, 1 + 2 * tiles, 1 + 2 * tiles + steps, 1 + 2 * tiles + 2 * steps


def pick(apart, columns, picks, owners, activations, picked, plan, read, seen, copied):
    replica, group_at = lax.axis_index("dp"), lax.axis_index("tensor")
    groups, slots, replicas = picks.shape[2], picks.shape[3], picks.shape[-1]
    edge = picked.shape[1]
    tiles = [
        (lax.rem(group_at + shift, groups), slot) for shift in range(groups) for slot in range(slots)
    ]
    reads = []
    for at, (group, slot) in enumerate(tiles):
        block = picks[0, 0, group, slot, 0, replica]
        reads.append(
            pltpu.make_async_copy(
                activations.at[0, :, :, column(block, edge)], read.at[at], copied.at[at]
            )
        )
    for copy in reads:
        copy.start()

    owned = owners.shape[-1] // replicas
    per_group = columns // groups
    steps = len(rounds(replicas)) + 1 if apart else replicas
    to_step, to_column, to_row, to_col, end = plan_sizes(len(tiles), steps)

    def owner_of(row):
        owner = jnp.int32(0)
        for one in range(1, replicas):
            owner += (row >= one * owned).astype(jnp.int32)
        return owner

    table = step_table(replicas) if apart else []
    mine = jnp.int32(0)
    for source, packed in enumerate(table):
        mine = jnp.where(replica == source, packed, mine)
    lane = lax.broadcasted_iota(jnp.int32, plan.shape, 1)
    planned = jnp.where((lane >= to_row) & (lane < end), -1, 0)

    for at, (group, slot) in enumerate(tiles):
        owner = owner_of(owners[0, 0, picks[0, 0, group, slot, 0, replica]])
        step = (mine >> 4 * owner) & 15 if apart else owner
        planned = jnp.where(lane == to_step + at, step, planned)
        planned = jnp.where(lane == to_column + at, picks[0, 0, group, slot, 1, replica], planned)

    for origin in range(replicas):
        place_row, place_col = jnp.int32(-1), jnp.int32(0)
        for group, slot in tiles:
            row = owners[0, 0, picks[0, 0, group, slot, 0, origin]] - replica * owned
            here = (row >= 0) & (row < owned)
            place_row = jnp.where(here, row, place_row)
            place_col = jnp.where(
                here, picks[0, 0, group, slot, 1, origin] + group * per_group, place_col
            )
        step = (jnp.int32(table[origin]) >> 4 * replica) & 15 if apart else origin
        planned = jnp.where(lane == to_row + step, place_row, planned)
        planned = jnp.where(lane == to_col + step, place_col, planned)

    wide = jnp.int32(0)
    if apart:
        spots = [
            picks[0, 0, group, slot, 0, origin] * columns
            + picks[0, 0, group, slot, 1, origin]
            + group * per_group
            for origin in range(replicas)
            for group, slot in tiles
        ]
        for spot in spots:
            seen[spot] = 0
        for spot in spots:
            seen[spot] = seen[spot] + 1
        for at, spot in enumerate(spots):
            origin, (group, slot) = at // len(tiles), tiles[at % len(tiles)]
            owner = owner_of(owners[0, 0, picks[0, 0, group, slot, 0, origin]])
            step = (jnp.int32(table[origin]) >> 4 * owner) & 15
            bit = jnp.int32(1) << wide_bit(jnp.maximum(step, 1), steps)
            wide = jnp.where((seen[spot] > 1) & (step > 0), wide | bit, wide)
    plan[...] = jnp.where(lane == 0, wide, planned)

    for at, copy in enumerate(reads):
        copy.wait()
        picked[at] = read[at].reshape(-1, edge).T


def wipe(strip, zeros, cleared):
    zeros[...] = jnp.zeros_like(zeros)
    rows = zeros.shape[0]
    writes = [
        pltpu.make_async_copy(zeros, strip.at[0, 0, pl.ds(part * rows, rows)], cleared.at[part])
        for part in range(strip.shape[2] // rows)
    ]
    for write in writes:
        write.start()
    for write in writes:
        write.wait()


def is_odd():
    return lax.rem(lax.axis_index("pipe"), 2) > 0


def cut_errors(shifts, errors, strip, *refs):
    cuts, (zeros, cleared, copied) = refs[:shifts], refs[shifts:]
    mine, groups = lax.axis_index("tensor"), shifts + 1
    pl.when(is_odd())(lambda: wipe(strip, zeros, cleared))
    copies = [
        pltpu.make_async_copy(
            errors.at[0, 0, 0, lax.rem(mine + groups - shift - 1, groups)], cut, copied.at[shift]
        )
        for shift, cut in enumerate(cuts)
    ]
    for copy in copies:
        copy.start()
    for copy in copies:
        copy.wait()


def clear(after, before, strip, zeros, cleared):
    pl.when(jnp.logical_not(is_odd()))(lambda: wipe(strip, zeros, cleared))


def multiply(groups, apart, to_step, to_column, plan, picked, error, *refs):
    returned, carried, outs = refs[:groups], refs[groups : 2 * groups - 1], refs[2 * groups - 1 :]
    mine = lax.axis_index("tensor")
    slots, (edge, tokens) = error.shape[4], picked.shape[1:]
    count = groups * slots
    wide = plan[0, 0]
    columns = [plan[0, to_column + at] for at in range(count)]
    steps = [plan[0, to_step + at] for at in range(count)]
    tiles = []
    for shift in range(groups):
        for slot in range(slots):
            at = shift * slots + slot
            right = returned[shift][0, :, :, column(columns[at], edge)].reshape(tokens, edge)
            extra = error[0, 0, 0, mine, slot] if shift == 0 else carried[shift - 1][slot]
            tile = jnp.dot(picked[at], right, preferred_element_type=jnp.float32)
            tiles.append(tile + extra.astype(jnp.float32))
    if not apart:
        for step, tile in zip(steps, tiles):
            outs[0][step] = tile
        return

    buffers = len(outs) // 2

    def store(step, tile, buffers):
        for at, buffer in enumerate(buffers):

            @pl.when(step == at)
            def _():
                buffer[...] = tile.astype(buffer.dtype)

    for step, tile in zip(steps, tiles):
        bit = (wide >> wide_bit(jnp.maximum(step, 1), buffers)) & 1
        full = jnp.where(step == 0, wide, bit) > 0

        @pl.when(full)
        def _():
            store(step, tile, outs[:buffers])

        @pl.when(jnp.logical_not(full))
        def _():
            store(step, tile, outs[buffers:])


def place(count, alone, to_row, to_col, plan, *refs):
    blocks, strip, staged, sent = refs[:count], refs[-3], refs[-2], refs[-1]
    steps, edge = staged.shape[0], staged.shape[-1]

    rows = [plan[0, to_row + step] for step in range(steps)]
    cols = [plan[0, to_col + step] for step in range(steps)]

    def meets(one, other):
        return (rows[one] == rows[other]) & (cols[one] == cols[other])

    def block_of(step):
        return blocks[0][step] if count == 1 else blocks[step][...]

    def first_of(step):
        first = rows[step] >= 0
        for earlier in range(0 if alone else step):
            first = first & jnp.logical_not(meets(earlier, step))
        return first

    def write_of(step):
        return pltpu.make_async_copy(
            blocks[step] if alone else staged.at[step],
            strip.at[0, 0, column(rows[step], edge), column(cols[step], edge)],
            sent.at[step],
        )

    for step in range(steps):

        @pl.when(first_of(step))
        def _():
            if not alone:
                total = block_of(step).astype(jnp.float32)
                for later in range(step + 1, steps):
                    block = block_of(later).astype(jnp.float32)
                    total = total + jnp.where(meets(step, later), block, 0.0)
                staged[step] = total.astype(staged.dtype)
            write_of(step).start()

    for step in range(steps):

        @pl.when(first_of(step))
        def _():
            write_of(step).wait()


def body(mesh, activations, cotangent, error_tiles, tile_picks, row_owners):
    sections, replicas, groups = mesh.shape["pipe"], mesh.shape["dp"], mesh.shape["tensor"]
    edge = error_tiles.shape[-1]
    slots = tile_picks.shape[4]
    micro, tokens = activations.shape[1:3]
    width = cotangent.shape[-1] * groups
    strip_rows = row_owners.shape[-1] // replicas * edge
    picks = jnp.transpose(tile_picks, (0, 2, 3, 4, 5, 1))

    returned = []
    for shift in range(groups):
        pairs = [
            (
                (section + 1) % sections * groups + (group + shift) % groups,
                section * groups + group,
            )
            for section in range(sections)
            for group in range(groups)
        ]
        returned.append(lax.ppermute(cotangent, ("pipe", "tensor"), pairs))
    apart = replicas <= MOST_STEPS
    tiles = groups * slots
    steps = len(rounds(replicas)) + 1 if apart else replicas
    shifts = groups - 1
    zero_rows = min(strip_rows, 256)
    strip_shape = (1, 1, strip_rows, width)
    wiping = [
        pltpu.VMEM((zero_rows, width), jnp.bfloat16),
        pltpu.SemaphoreType.DMA((strip_rows // zero_rows,)),
    ]
    started, *cuts = pl.pallas_call(
        functools.partial(cut_errors, shifts),
        out_shape=[pltpu.HBM(strip_shape, jnp.bfloat16)]
        + [pltpu.VMEM((slots, edge, edge), error_tiles.dtype)] * shifts,
        in_specs=[ANY],
        out_specs=[pl.BlockSpec(memory_space=pltpu.HBM)] + [VMEM] * shifts,
        scratch_shapes=wiping + [pltpu.SemaphoreType.DMA((shifts,))],
        compiler_params=SMALL,
        name="cut_errors",
    )(in_hbm(error_tiles))
    carried = [
        lax.ppermute(
            cut, "tensor", [((group + shift + 1) % groups, group) for group in range(groups)]
        )
        for shift, cut in enumerate(cuts)
    ]
    picked, plan = pl.pallas_call(
        functools.partial(pick, apart, width // edge),
        out_shape=[
            pltpu.VMEM((tiles, edge, micro * tokens), activations.dtype),
            pltpu.VMEM((1, -(-plan_sizes(tiles, steps)[-1] // 128) * 128), jnp.int32),
        ],
        in_specs=[SMEM, SMEM, ANY],
        out_specs=[VMEM] * 2,
        scratch_shapes=[
            pltpu.VMEM((tiles, micro, tokens, edge), activations.dtype),
            pltpu.SMEM((row_owners.shape[-1] * (width // edge),), jnp.int32),
            pltpu.SemaphoreType.DMA((tiles,)),
        ],
        compiler_params=SMALL,
        name="pick",
    )(in_hbm(picks), in_hbm(row_owners), in_hbm(activations))

    cleared = pl.pallas_call(
        clear,
        out_shape=jax.ShapeDtypeStruct(strip_shape, jnp.bfloat16),
        in_specs=[ANY, ANY],
        out_specs=ANY,
        scratch_shapes=wiping,
        input_output_aliases={1: 0},
        compiler_params=SMALL,
        name="clear",
    )(picked, started)

    to_step, to_column, to_row, to_col, _ = plan_sizes(tiles, steps)
    tile_shape = (edge, edge)
    if apart:
        out_shape = [
            jax.ShapeDtypeStruct(tile_shape, dtype)
            for dtype in (jnp.float32, jnp.bfloat16)
            for step in range(steps)
        ]
    else:
        out_shape = [jax.ShapeDtypeStruct((replicas,) + tile_shape, jnp.float32)]
    outgoing = pl.pallas_call(
        functools.partial(multiply, groups, apart, to_step, to_column),
        out_shape=out_shape,
        in_specs=[VMEM] * (2 * groups + 2),
        out_specs=[VMEM] * len(out_shape),
        compiler_params=SMALL,
        name="multiply",
    )(plan, picked, error_tiles, *returned, *carried)

    def placed(alone, incoming, strip, first=0):
        count = len(incoming) if apart else replicas
        return pl.pallas_call(
            functools.partial(place, len(incoming), alone, to_row + first, to_col + first),
            out_shape=jax.ShapeDtypeStruct(strip_shape, jnp.bfloat16),
            in_specs=[VMEM] * (1 + len(incoming)) + [ANY],
            out_specs=ANY,
            scratch_shapes=[
                pltpu.VMEM((count,) + tile_shape, jnp.bfloat16),
                pltpu.SemaphoreType.DMA((count,)),
            ],
            input_output_aliases={1 + len(incoming): 0},
            compiler_params=SMALL,
            name="place",
        )(plan, *incoming, strip)

    def exchanged(blocks):
        moved = [
            lax.ppermute(block, "dp", list(enumerate(targets)))
            for block, targets in zip(blocks[1:], rounds(replicas))
        ]
        return [blocks[0], *moved]

    if not apart:
        swapped = lax.all_to_all(outgoing[0], "dp", split_axis=0, concat_axis=0, tiled=True)
        return placed(False, [swapped], cleared)
    def branch(wide):
        blocks = [
            outgoing[at if (wide >> wide_bit(at, steps) & 1 if at else wide) else steps + at]
            for at in range(steps)
        ]
        def run():
            arrived = exchanged(blocks)
            if wide:
                return placed(False, arrived, cleared)
            return placed(True, arrived[2:], placed(True, arrived[:2], cleared), 2)

        return run

    sets = 1 << (wide_bit(steps - 1, steps) + 1)
    return lax.switch(plan[0, 0], [branch(wide) for wide in range(sets)])


def solution(mesh):
    in_specs = (
        P("pipe", None, "dp", "tensor"),
        P("pipe", None, "dp", "tensor"),
        P("pipe", "dp", "tensor", None, None, None, None),
        P("pipe", None, "tensor", None, None, None),
        P("pipe", "tensor", None),
    )
    out_specs = P("pipe", "tensor", "dp", None)
    return jax.shard_map(
        functools.partial(body, mesh),
        mesh=mesh,
        in_specs=in_specs,
        out_specs=out_specs,
        check_vma=False,
    )
```

```python
import functools

import jax
import jax.numpy as jnp
from jax import lax
from jax.experimental import pallas as pl
from jax.experimental.pallas import tpu as pltpu
from jax.sharding import PartitionSpec as P

VMEM = pl.BlockSpec(memory_space=pltpu.VMEM)
SMEM = pl.BlockSpec(memory_space=pltpu.SMEM)
ANY = pl.BlockSpec(memory_space=pl.ANY)
MOST_STEPS = 8
ROUNDS = {4: [(2, 3, 1, 0), (3, 2, 0, 1), (1, 0, 3, 2)]}
SMALL = pltpu.CompilerParams(vmem_limit_bytes=4 << 20)


def in_hbm(value):
    return pltpu.with_memory_space_constraint(value, pltpu.HBM)


def column(index, edge):
    return pl.ds(pl.multiple_of(index * edge, edge), edge)


def rounds(replicas, odd=0):
    shifts = [
        tuple((one + step) % replicas for one in range(replicas)) for step in range(1, replicas)
    ]
    return shifts if odd else ROUNDS.get(replicas, shifts)


def step_table(replicas, odd):
    table = []
    for source in range(replicas):
        steps = [0] * replicas
        for step, targets in reversed(list(enumerate(rounds(replicas, odd), 1))):
            steps[targets[source]] = step
        table.append(sum(step << 4 * target for target, step in enumerate(steps)))
    return table


def wide_bit(step, count):
    return step - 1 if count <= 4 else 0


def plan_sizes(tiles, steps):
    return 1, 1 + tiles, 1 + 2 * tiles, 1 + 2 * tiles + steps, 1 + 2 * tiles + 2 * steps


def pick(apart, columns, picks, owners, activations, picked, plan, read, seen, copied):
    replica, group_at = lax.axis_index("dp"), lax.axis_index("tensor")
    groups, slots, replicas = picks.shape[2], picks.shape[3], picks.shape[-1]
    edge = picked.shape[1]
    tiles = [
        (lax.rem(group_at + shift, groups), slot) for shift in range(groups) for slot in range(slots)
    ]
    reads = []
    for at, (group, slot) in enumerate(tiles):
        block = picks[0, 0, group, slot, 0, replica]
        reads.append(
            pltpu.make_async_copy(
                activations.at[0, :, :, column(block, edge)], read.at[at], copied.at[at]
            )
        )
    for copy in reads:
        copy.start()

    owned = owners.shape[-1] // replicas
    per_group = columns // groups
    steps = len(rounds(replicas)) + 1 if apart else replicas
    to_step, to_column, to_row, to_col, end = plan_sizes(len(tiles), steps)

    def owner_of(row):
        owner = jnp.int32(0)
        for one in range(1, replicas):
            owner += (row >= one * owned).astype(jnp.int32)
        return owner

    odd = lax.rem(lax.axis_index("pipe"), 2) > 0
    table = [
        jnp.where(odd, other, packed)
        for packed, other in zip(step_table(replicas, 0), step_table(replicas, 1))
    ] if apart else []
    mine = jnp.int32(0)
    for source, packed in enumerate(table):
        mine = jnp.where(replica == source, packed, mine)
    lane = lax.broadcasted_iota(jnp.int32, plan.shape, 1)
    planned = jnp.where((lane >= to_row) & (lane < end), -1, 0)

    for at, (group, slot) in enumerate(tiles):
        owner = owner_of(owners[0, 0, picks[0, 0, group, slot, 0, replica]])
        step = (mine >> 4 * owner) & 15 if apart else owner
        planned = jnp.where(lane == to_step + at, step, planned)
        planned = jnp.where(lane == to_column + at, picks[0, 0, group, slot, 1, replica], planned)

    for origin in range(replicas):
        place_row, place_col = jnp.int32(-1), jnp.int32(0)
        for group, slot in tiles:
            row = owners[0, 0, picks[0, 0, group, slot, 0, origin]] - replica * owned
            here = (row >= 0) & (row < owned)
            place_row = jnp.where(here, row, place_row)
            place_col = jnp.where(
                here, picks[0, 0, group, slot, 1, origin] + group * per_group, place_col
            )
        step = (table[origin] >> 4 * replica) & 15 if apart else origin
        planned = jnp.where(lane == to_row + step, place_row, planned)
        planned = jnp.where(lane == to_col + step, place_col, planned)

    wide = jnp.int32(0)
    if apart:
        spots = [
            picks[0, 0, group, slot, 0, origin] * columns
            + picks[0, 0, group, slot, 1, origin]
            + group * per_group
            for origin in range(replicas)
            for group, slot in tiles
        ]
        for spot in spots:
            seen[spot] = 0
        for spot in spots:
            seen[spot] = seen[spot] + 1
        for at, spot in enumerate(spots):
            origin, (group, slot) = at // len(tiles), tiles[at % len(tiles)]
            owner = owner_of(owners[0, 0, picks[0, 0, group, slot, 0, origin]])
            step = (table[origin] >> 4 * owner) & 15
            bit = jnp.int32(1) << wide_bit(jnp.maximum(step, 1), steps)
            wide = jnp.where((seen[spot] > 1) & (step > 0), wide | bit, wide)
    plan[...] = jnp.where(lane == 0, wide, planned)

    for at, copy in enumerate(reads):
        copy.wait()
        picked[at] = read[at].reshape(-1, edge).T


def clear(after, strip, zeros, cleared):
    zeros[...] = jnp.zeros_like(zeros)
    rows = zeros.shape[0]
    writes = [
        pltpu.make_async_copy(zeros, strip.at[0, 0, pl.ds(part * rows, rows)], cleared.at[part])
        for part in range(strip.shape[2] // rows)
    ]
    for write in writes:
        write.start()
    for write in writes:
        write.wait()


def multiply(groups, apart, to_step, to_column, plan, picked, error, *refs):
    returned, carried, outs = refs[:groups], refs[groups : 2 * groups - 1], refs[2 * groups - 1 :]
    mine = lax.axis_index("tensor")
    slots, (edge, tokens) = error.shape[4], picked.shape[1:]
    count = groups * slots
    wide = plan[0, 0]
    columns = [plan[0, to_column + at] for at in range(count)]
    steps = [plan[0, to_step + at] for at in range(count)]
    tiles = []
    for shift in range(groups):
        for slot in range(slots):
            at = shift * slots + slot
            right = returned[shift][0, :, :, column(columns[at], edge)].reshape(tokens, edge)
            extra = error[0, 0, 0, mine, slot] if shift == 0 else carried[shift - 1][0, 0, 0, 0, slot]
            tile = jnp.dot(picked[at], right, preferred_element_type=jnp.float32)
            tiles.append(tile + extra.astype(jnp.float32))
    if not apart:
        for step, tile in zip(steps, tiles):
            outs[0][step] = tile
        return

    buffers = len(outs) // 2

    def store(step, tile, buffers):
        for at, buffer in enumerate(buffers):

            @pl.when(step == at)
            def _():
                buffer[...] = tile.astype(buffer.dtype)

    for step, tile in zip(steps, tiles):
        bit = (wide >> wide_bit(jnp.maximum(step, 1), buffers)) & 1
        full = jnp.where(step == 0, wide, bit) > 0

        @pl.when(full)
        def _():
            store(step, tile, outs[:buffers])

        @pl.when(jnp.logical_not(full))
        def _():
            store(step, tile, outs[buffers:])


def place(count, alone, to_row, to_col, plan, *refs):
    blocks, strip, staged, sent = refs[:count], refs[-3], refs[-2], refs[-1]
    steps, edge = staged.shape[0], staged.shape[-1]

    rows = [plan[0, to_row + step] for step in range(steps)]
    cols = [plan[0, to_col + step] for step in range(steps)]

    def meets(one, other):
        return (rows[one] == rows[other]) & (cols[one] == cols[other])

    def block_of(step):
        return blocks[0][step] if count == 1 else blocks[step][...]

    def first_of(step):
        first = rows[step] >= 0
        for earlier in range(0 if alone else step):
            first = first & jnp.logical_not(meets(earlier, step))
        return first

    def write_of(step):
        return pltpu.make_async_copy(
            blocks[step] if alone else staged.at[step],
            strip.at[0, 0, column(rows[step], edge), column(cols[step], edge)],
            sent.at[step],
        )

    for step in range(steps):

        @pl.when(first_of(step))
        def _():
            if not alone:
                total = block_of(step).astype(jnp.float32)
                for later in range(step + 1, steps):
                    block = block_of(later).astype(jnp.float32)
                    total = total + jnp.where(meets(step, later), block, 0.0)
                staged[step] = total.astype(staged.dtype)
            write_of(step).start()

    for step in range(steps):

        @pl.when(first_of(step))
        def _():
            write_of(step).wait()


def body(mesh, activations, cotangent, error_tiles, tile_picks, row_owners):
    sections, replicas, groups = mesh.shape["pipe"], mesh.shape["dp"], mesh.shape["tensor"]
    edge = error_tiles.shape[-1]
    slots = tile_picks.shape[4]
    micro, tokens = activations.shape[1:3]
    width = cotangent.shape[-1] * groups
    strip_rows = row_owners.shape[-1] // replicas * edge
    picks = jnp.transpose(tile_picks, (0, 2, 3, 4, 5, 1))

    returned = []
    for shift in range(groups):
        pairs = [
            (
                (section + 1) % sections * groups + (group + shift) % groups,
                section * groups + group,
            )
            for section in range(sections)
            for group in range(groups)
        ]
        returned.append(lax.ppermute(cotangent, ("pipe", "tensor"), pairs))
    apart = replicas <= MOST_STEPS
    tiles = groups * slots
    steps = len(rounds(replicas)) + 1 if apart else replicas
    mine = lax.axis_index("tensor")
    carried = [
        lax.ppermute(
            lax.dynamic_index_in_dim(error_tiles, (mine - shift + groups) % groups, axis=3),
            "tensor",
            [((group + shift) % groups, group) for group in range(groups)],
        )
        for shift in range(1, groups)
    ]
    picked, plan = pl.pallas_call(
        functools.partial(pick, apart, width // edge),
        out_shape=[
            pltpu.VMEM((tiles, edge, micro * tokens), activations.dtype),
            pltpu.VMEM((1, -(-plan_sizes(tiles, steps)[-1] // 128) * 128), jnp.int32),
        ],
        in_specs=[SMEM, SMEM, ANY],
        out_specs=[VMEM] * 2,
        scratch_shapes=[
            pltpu.VMEM((tiles, micro, tokens, edge), activations.dtype),
            pltpu.SMEM((row_owners.shape[-1] * (width // edge),), jnp.int32),
            pltpu.SemaphoreType.DMA((tiles,)),
        ],
        compiler_params=SMALL,
        name="pick",
    )(in_hbm(picks), in_hbm(row_owners), in_hbm(activations))

    zero_rows = min(strip_rows, 256)
    strip_shape = (1, 1, strip_rows, width)
    cleared = pl.pallas_call(
        clear,
        out_shape=pltpu.HBM(strip_shape, jnp.bfloat16),
        in_specs=[ANY],
        out_specs=pl.BlockSpec(memory_space=pltpu.HBM),
        scratch_shapes=[
            pltpu.VMEM((zero_rows, width), jnp.bfloat16),
            pltpu.SemaphoreType.DMA((strip_rows // zero_rows,)),
        ],
        compiler_params=SMALL,
        cost_estimate=pl.CostEstimate(
            flops=0, bytes_accessed=2 * strip_rows * width, transcendentals=0
        ),
        name="clear",
    )(picked)

    to_step, to_column, to_row, to_col, _ = plan_sizes(tiles, steps)
    tile_shape = (edge, edge)
    if apart:
        out_shape = [
            jax.ShapeDtypeStruct(tile_shape, dtype)
            for dtype in (jnp.float32, jnp.bfloat16)
            for step in range(steps)
        ]
    else:
        out_shape = [jax.ShapeDtypeStruct((replicas,) + tile_shape, jnp.float32)]
    outgoing = pl.pallas_call(
        functools.partial(multiply, groups, apart, to_step, to_column),
        out_shape=out_shape,
        in_specs=[VMEM] * (2 * groups + 2),
        out_specs=[VMEM] * len(out_shape),
        compiler_params=SMALL,
        name="multiply",
    )(plan, picked, error_tiles, *returned, *carried)

    def placed(alone, incoming, strip, first=0):
        count = len(incoming) if apart else replicas
        return pl.pallas_call(
            functools.partial(place, len(incoming), alone, to_row + first, to_col + first),
            out_shape=jax.ShapeDtypeStruct(strip_shape, jnp.bfloat16),
            in_specs=[VMEM] * (1 + len(incoming)) + [ANY],
            out_specs=ANY,
            scratch_shapes=[
                pltpu.VMEM((count,) + tile_shape, jnp.bfloat16),
                pltpu.SemaphoreType.DMA((count,)),
            ],
            input_output_aliases={1 + len(incoming): 0},
            compiler_params=SMALL,
            name="place",
        )(plan, *incoming, strip)

    def exchanged(blocks):
        moved = []
        for at, block in enumerate(blocks[1:]):
            pairs = [
                (section * replicas + source, section * replicas + target)
                for section in range(sections)
                for source, target in enumerate(rounds(replicas, section % 2)[at])
            ]
            moved.append(lax.ppermute(block, ("pipe", "dp"), pairs))
        return [blocks[0], *moved]

    if not apart:
        swapped = lax.all_to_all(outgoing[0], "dp", split_axis=0, concat_axis=0, tiled=True)
        return placed(False, [swapped], cleared)
    def branch(wide):
        blocks = [
            outgoing[at if (wide >> wide_bit(at, steps) & 1 if at else wide) else steps + at]
            for at in range(steps)
        ]
        def run():
            arrived = exchanged(blocks)
            if wide:
                return placed(False, arrived, cleared)
            return placed(True, arrived[2:], placed(True, arrived[:2], cleared), 2)

        return run

    sets = 1 << (wide_bit(steps - 1, steps) + 1)
    return lax.switch(plan[0, 0], [branch(wide) for wide in range(sets)])


def solution(mesh):
    in_specs = (
        P("pipe", None, "dp", "tensor"),
        P("pipe", None, "dp", "tensor"),
        P("pipe", "dp", "tensor", None, None, None, None),
        P("pipe", None, "tensor", None, None, None),
        P("pipe", "tensor", None),
    )
    out_specs = P("pipe", "tensor", "dp", None)
    return jax.shard_map(
        functools.partial(body, mesh),
        mesh=mesh,
        in_specs=in_specs,
        out_specs=out_specs,
        check_vma=False,
    )
```
